128 devices in a mesh: dp: 8 (over z, core), row: 4 (over y), col: 4 (over x).
Axes of the slice: x: 4, y: 4, z: 4, core: 2. Of those that a mesh axis runs over, the one named last changes fastest.
Arguments:
- inputs: float32 [8192, 1024], P(('dp', 'row'), 'col'), may hold values from -6 to 6
- w_qkv: bfloat16 [2, 1024, 3, 1024], P(None, 'row', None, 'col'), may hold values from -0.1875 to 0.1875
- w_out: bfloat16 [2, 1024, 1024], P(None, 'row', 'col'), may hold values from -0.75 to 0.75
- w_up: bfloat16 [2, 1024, 4096], P(None, 'row', 'col'), may hold values from -0.1875 to 0.1875
- w_down: bfloat16 [2, 4096, 1024], P(None, 'row', 'col'), may hold values from -0.09375 to 0.09375
- small_params: float32 [2, 9, 1024], P(None, None, 'col'), may hold values from -0.75 to 1.875, as said below
- query_bias: float32 [2, 1024], P(None, 'col'), may hold values from -1.8 to 1.8
- up_bias: float32 [2, 4096], P(None, 'col'), may hold values from -1.8 to 1.8
- cotangent: float32 [8192, 1024], P(('dp', 'row'), 'col'), may hold values from -6 to 6
Outputs:
- output: float32 [8192, 1024], P(('dp', 'row'), 'col')
- input_grad: float32 [8192, 1024], P(('dp', 'row'), 'col')
- qkv_grad: float32 [2, 1024, 3, 1024], P(None, 'row', None, 'col')
- out_grad: float32 [2, 1024, 1024], P(None, 'row', 'col')
- up_grad: float32 [2, 1024, 4096], P(None, 'row', 'col')
- down_grad: float32 [2, 4096, 1024], P(None, 'row', 'col')
- small_grad: float32 [2, 9, 1024], P(None, None, 'col')
- query_bias_grad: float32 [2, 1024], P(None, 'col')
- up_bias_grad: float32 [2, 4096], P(None, 'col')
The draws below stay inside these ranges and needn't reach their ends.
Inputs may be any that keep to these rules, and one draw needn't show every extreme that they name: `small_params`: norm gains and layer scales are positive.
All inputs are finite; a program needn't handle non-finite values.
Results may differ from the reference program's by a relative error of at most 0.02.
Values may be sent and summed in bfloat16 or wider, within the bound.
A program may use at most 128 MiB of HBM per device.

```python
import jax
import jax.numpy as jnp
from jax import lax

D = 1024
HEADS = 16
HD = 64
FF = 4096
LAYERS = 2
SEQ = 1024
TOKENS = 8192
N_DP = 8


def draw_small_params(key, part):
    key = jax.random.fold_in(key, 11)
    spread = jnp.clip(jax.random.normal(key, (LAYERS, 9, D), jnp.float32), -2.5, 2.5)
    offsets = jnp.array([1.0, 0.0, 0.0, 0.0, 1.0, 1.0, 0.0, 0.0, 1.0], jnp.float32).reshape(1, 9, 1)
    widths = jnp.array([0.25, 0.3, 0.3, 0.3, 0.35, 0.25, 0.3, 0.3, 0.35], jnp.float32).reshape(1, 9, 1)
    return offsets + widths * spread


def level_of(stream_key, shape, split, low, high):
    gain, own = 1.0, jax.random.fold_in(stream_key, 6)
    for dim, blocks in split:
        steps = jnp.exp(jax.random.uniform(jax.random.fold_in(own, dim), (blocks,), jnp.float32, low / len(split), high / len(split)))
        gain = gain * jnp.repeat(steps, shape[dim] // blocks).reshape([-1 if axis == dim else 1 for axis in range(len(shape))])
    return gain


def normal_values(own_key, extent, width, bound, pieces=(), dtype=jnp.bfloat16):
    factor_of = level_of(own_key, extent, pieces, -0.22, 0.18) if pieces else 1.0
    drawn = jax.random.normal(own_key, extent, jnp.float32) * width * factor_of
    return jnp.minimum(jnp.maximum(drawn, -bound), bound).astype(dtype)


def setup_inputs(seed: int = 0) -> dict:
    streams_of = jax.random.split(jax.random.key(seed), 10)
    return {
        "inputs": normal_values(streams_of[0], (TOKENS, D), 1.0, 6.0, ((0, 32), (1, 4)), jnp.float32),
        "w_qkv": normal_values(streams_of[1], (LAYERS, D, 3, D), D ** -0.5, 0.1875, ((1, 4), (3, 4))),
        "w_out": normal_values(streams_of[2], (LAYERS, D, D), (D // 16) ** -0.5, 0.75, ((1, 4), (2, 4))),
        "w_up": normal_values(streams_of[3], (LAYERS, D, FF), D ** -0.5, 0.1875, ((1, 4), (2, 4))),
        "w_down": normal_values(streams_of[4], (LAYERS, FF, D), FF ** -0.5, 0.09375, ((1, 4), (2, 4))),
        "small_params": draw_small_params(jax.random.fold_in(streams_of[9], 71), 0),
        "query_bias": normal_values(streams_of[6], (LAYERS, D), 0.3, 1.8, ((1, 4),), jnp.float32),
        "up_bias": normal_values(streams_of[7], (LAYERS, FF), 0.3, 1.8, ((1, 4),), jnp.float32),
        "cotangent": normal_values(streams_of[8], (TOKENS, D), 1.0, 6.0, ((0, 32), (1, 4)), jnp.float32),
    }


EPS = 1e-06
HIGH = lax.Precision.HIGHEST

@jax.custom_vjp
def low(v):
    return lax.optimization_barrier(v.astype(jnp.bfloat16)).astype(jnp.float32)

@jax.custom_vjp
def low_back(v):
    return v

def low_keep(v):
    return (low(v), None)

def low_pass(kept, grad):
    return (grad,)

def back_keep(v):
    return (v, None)

def back_low(kept, grad):
    return (low(grad),)
low.defvjp(low_keep, low_pass)
low_back.defvjp(back_keep, back_low)

def matmul_high(left_side, right_side):
    return jnp.dot(left_side, right_side, precision=HIGH)

def layer_norm(stream, gain_row, shift_row):
    row_mean = lax.optimization_barrier(jnp.mean(stream, -1, keepdims=True))
    centered = stream - row_mean
    variance = lax.optimization_barrier(jnp.mean(centered * centered, -1, keepdims=True))
    return centered * lax.rsqrt(variance + EPS) * gain_row + shift_row

def residual_block(stream, qkv_weight, out_weight, up_weight, down_weight, layer_small, bias_query, bias_up):
    length = stream.shape[0]
    normed = low(layer_norm(stream, layer_small[0], layer_small[1]))
    projected = matmul_high(normed, qkv_weight.reshape(D, 3 * D)).reshape(length, 3, D)
    queries = low(low_back(projected[:, 0] + bias_query)).reshape(length, HEADS, HD)
    key_rows = low(low_back(projected[:, 1])).reshape(length, HEADS, HD)
    value_rows = low(low_back(projected[:, 2] + layer_small[2])).reshape(length, HEADS, HD)
    scores = low_back(jnp.einsum('qhd,khd->hqk', queries, key_rows, precision=HIGH) * HD ** (-0.5))
    attn_weights = low(jax.nn.softmax(scores, -1))
    attended = jnp.einsum('hqk,khd->qhd', attn_weights, value_rows, precision=HIGH).reshape(length, D)
    attended = low(low_back(attended))
    branch_one = low_back(matmul_high(attended, out_weight)) + layer_small[3]
    middle = stream + layer_small[4] * branch_one
    normed_mid = low(layer_norm(middle, layer_small[5], layer_small[6]))
    hidden_pre = low_back(matmul_high(normed_mid, up_weight) + bias_up)
    activated = low(jax.nn.gelu(hidden_pre, approximate=False))
    branch_two = low_back(matmul_high(activated, down_weight)) + layer_small[7]
    return middle + layer_small[8] * branch_two

def forward(stream, qkv_all, out_all, up_all, down_all, small_all, query_all, bias_all):
    for level in range(LAYERS):
        stream = residual_block(stream, qkv_all[level], out_all[level], up_all[level], down_all[level], small_all[level], query_all[level], bias_all[level])
    return stream

def reference(inputs, w_qkv, w_out, w_up, w_down, small_params, query_bias, up_bias, cotangent):
    params = (w_qkv.astype(jnp.float32), w_out.astype(jnp.float32), w_up.astype(jnp.float32), w_down.astype(jnp.float32), small_params, query_bias, up_bias)

    def per_image(running, scan_item):
        image_rows, image_grad = scan_item
        result, pullback = jax.vjp(forward, image_rows, *params)
        gradients = pullback(image_grad)
        running = tuple((total_grad + new_grad for total_grad, new_grad in zip(running, gradients[1:])))
        return (running, (result, gradients[0]))
    initial = tuple((jnp.zeros(param.shape, jnp.float32) for param in params))
    running, (results, input_grads) = lax.scan(per_image, initial, (inputs.reshape(N_DP, SEQ, D), cotangent.reshape(N_DP, SEQ, D)))
    return (results.reshape(TOKENS, D), input_grads.reshape(TOKENS, D), running[0], running[1], running[2], running[3], running[4], running[5], running[6])
```

```python
from functools import partial

import jax
import jax.numpy as jnp
from jax import lax
from jax.experimental import pallas as pl
from jax.experimental.pallas import tpu as pltpu
from jax.sharding import PartitionSpec as P

HD = 64
EPS = 1e-06
LANES = 128
BF = jnp.bfloat16
F32 = jnp.float32
MESH = pl.DeviceIdType.MESH


def mm(left, right):
    return jnp.dot(left, right, preferred_element_type=F32)


def mm_nt(left, right):
    return lax.dot_general(left, right, (((1,), (1,)), ((), ())), preferred_element_type=F32)


def mm_tn(left, right):
    return lax.dot_general(left, right, (((0,), (0,)), ((), ())), preferred_element_type=F32)


class Links:
    def __init__(self, sizes, send, recv, local):
        self.sizes = sizes
        self.send, self.recv, self.local = send, recv, local
        self.used = 0
        self.used_local = 0
        self.col = lax.axis_index("col")
        self.row = lax.axis_index("row")
        place = lax.axis_index("dp")
        self.z = place // 2
        self.core = place % 2
        self.sibling = {"dp": self.z * 2 + (1 - self.core)}

    def peer(self, axis, step):
        if axis == "z":
            index = lax.rem(self.z + step, self.sizes["z"])
            return index, {"dp": index * 2 + self.core}
        index = lax.rem(getattr(self, axis) + step, self.sizes[axis])
        return index, {axis: index}

    def start(self, source, target, device, begin=True):
        copy = pltpu.make_async_remote_copy(
            src_ref=source,
            dst_ref=target,
            send_sem=self.send.at[self.used],
            recv_sem=self.recv.at[self.used],
            device_id=device,
            device_id_type=MESH,
        )
        self.used += 1
        if begin:
            copy.start()
        return copy

    def bring(self, source, target):
        copy = pltpu.make_async_copy(source, target, self.local.at[self.used_local])
        self.used_local += 1
        copy.start()
        return copy

    def spread(self, axis, source, target):
        return [
            self.start(source, target, self.peer(axis, step)[1])
            for step in range(1, self.sizes[axis])
        ]

    def deal(self, axis, source_of, target):
        copies = []
        for step in range(1, self.sizes[axis]):
            index, device = self.peer(axis, step)
            copies.append(self.start(source_of(index), target, device))
        return copies


def finish(copies):
    for copy in copies:
        copy.wait()


def as_rows(first, second):
    tokens = first.shape[0]
    lane = lax.broadcasted_iota(jnp.int32, (tokens, LANES), 1)
    both = jnp.where(lane == 0, first, jnp.where(lane == 1, second, 0.0))
    return both.T[:8]


def as_columns(rows):
    count, tokens = rows.shape
    return jnp.concatenate([rows, jnp.zeros((LANES - count, tokens), F32)], 0).T


def body(sizes, layers, *refs):
    (
        x_in, cot, small, qbias, ubias, wq_in, wo_in, wu_in, wd_in,
        x_out, g_out, gw, sums_out,
        wq, wo, wu, wd, smg, xg, st1, h, q, kvg, probs, og, abr, xg2, st2, h2, gp, zz, mbr,
        inv1, inv2, msend, mrecv, dmg, dur, hsend, hrecv2, bst2, osend, orecv, dob, kvsend, kvrecv,
        jg, hrecv1, bst1, grad, crecv, ra, rb, ta, tb, ua, ub, fin, fdown, sums, sumc, sumy, sumz,
        send, recv, local,
    ) = refs
    net = Links(sizes, send, recv, local)
    c, r, z, core = net.col, net.row, net.z, net.core
    ncol, nrow, nz = sizes["col"], sizes["row"], sizes["z"]
    tokens, width = x_in.shape
    hidden = ubias.shape[1]
    full = width * ncol
    length = tokens * nrow
    blocks = hidden // width
    pairs = width // LANES
    scale = HD ** (-0.5)

    barrier = pltpu.get_barrier_semaphore()
    greeted = [net.peer(a, s)[1] for a in ("col", "row", "z") for s in range(1, sizes[a])]
    greeted.append(net.sibling)
    for device in greeted:
        pl.semaphore_signal(barrier, inc=1, device_id=device, device_id_type=MESH)
    mirror = {"row": c, "col": r}

    @pl.when(r != c)
    def _():
        pl.semaphore_signal(barrier, inc=1, device_id=mirror, device_id_type=MESH)

    pl.semaphore_wait(barrier, len(greeted) + jnp.where(r != c, 1, 0))

    def flip_start(source, target):
        copy = net.start(source, target, mirror, begin=False)
        here = pltpu.make_async_copy(source, target, local.at[net.used_local])
        net.used_local += 1

        @pl.when(r != c)
        def _():
            copy.start()

        @pl.when(r == c)
        def _():
            here.start()

        return copy, here

    def flip_wait(pair):
        copy, here = pair

        @pl.when(r != c)
        def _():
            copy.wait()

        @pl.when(r == c)
        def _():
            here.wait()

    class Weight:
        def __init__(self, level, source, store, flipped=False):
            self.level, self.source, self.store, self.flipped = level, source, store, flipped

        def flip(self):
            self.turn = flip_start(self.source.at[self.level, core], self.store.at[self.level, c, core])

        def begin(self):
            place = self.store.at[self.level, r, core]
            if self.flipped:
                flip_wait(self.turn)
                self.copies = net.spread("row", place, place)
            else:
                source = self.source.at[self.level, core]
                self.copies = [net.bring(source, place)] + net.spread("row", source, place)

        def share(self):
            finish(self.copies)
            place = self.store.at[self.level, :, core]
            self.shared = net.start(place, place, net.sibling)

        def ready(self):
            self.shared.wait()

    wqs = [Weight(l, wq_in, wq) for l in range(layers)]
    wos = [Weight(l, wo_in, wo) for l in range(layers)]
    wus = [Weight(l, wu_in, wu) for l in range(layers)]
    wds = [Weight(l, wd_in, wd, True) for l in range(layers)]

    def param(level, index):
        return small[level * 9 + index : level * 9 + index + 1, :]

    def any_param(level, index, block):
        return smg[block, level * 9 + index : level * 9 + index + 1, :]

    def norm_send(value, store, stats):
        mean = jnp.sum(value, 1, keepdims=True) * (1.0 / width)
        centered = value - mean
        store[c] = centered.astype(BF)
        stats[c] = as_rows(mean, jnp.sum(centered * centered, 1, keepdims=True))
        return net.spread("col", store.at[c], store.at[c]) + net.spread("col", stats.at[c], stats.at[c])

    def norm_apply(level, first, store, stats, inverse, result):
        columns = as_columns(stats[...].reshape(ncol * 8, tokens))
        means = [columns[:, 8 * i : 8 * i + 1] for i in range(ncol)]
        mean = sum(means) * (1.0 / ncol)
        spread = sum(columns[:, 8 * i + 1 : 8 * i + 2] for i in range(ncol))
        spread = spread + width * sum((m - mean) * (m - mean) for m in means)
        scaled = lax.rsqrt(spread * (1.0 / full) + EPS)
        inverse[...] = jnp.broadcast_to(scaled, inverse.shape)
        for i in range(ncol):
            normed = (store[i].astype(F32) + (means[i] - mean)) * scaled
            store[i] = normed.astype(BF)
            result[:, i * width : (i + 1) * width] = (
                normed * any_param(level, first, i) + any_param(level, first + 1, i)
            ).astype(BF)

    def slots(store):
        return sum(store[i].astype(F32) for i in range(store.shape[0]))

    lane = lax.broadcasted_iota(jnp.int32, (tokens, LANES), 1)
    half = [(lane < HD).astype(F32), (lane >= HD).astype(F32)]

    def pick(values):
        side = lax.broadcasted_iota(jnp.int32, values[0].shape, 1)
        return jnp.where(side < HD, values[0], values[1])

    def pair_lanes(p):
        return pl.ds(pl.multiple_of(p * LANES, LANES), LANES)

    def attend(level):
        def step(p, carry):
            lanes = pair_lanes(p)
            queries = q[level, :, lanes].astype(F32)
            keys = kvg[level, :, 0, :, lanes].reshape(length, LANES)
            values = kvg[level, :, 1, :, lanes].reshape(length, LANES)
            found = []
            for side in range(2):
                scores = mm_nt((queries * half[side]).astype(BF), keys) * scale
                raised = jnp.exp(scores - jnp.max(scores, 1, keepdims=True))
                share = (raised * (1.0 / jnp.sum(raised, 1, keepdims=True))).astype(BF)
                probs[level, 2 * p + side] = share
                found.append(mm(share, values))
            og[level, c, :, lanes] = pick(found).astype(BF)
            return carry

        lax.fori_loop(0, pairs, step, 0)

    def attend_back(level):
        def step(p, carry):
            lanes = pair_lanes(p)
            queries = q[level, :, lanes]
            upstream = dob[:, lanes]
            keys = kvg[level, :, 0, :, lanes].reshape(length, LANES)
            values = kvg[level, :, 1, :, lanes].reshape(length, LANES)
            dq, dk, dv = [], [], []
            for side in range(2):
                share = probs[level, 2 * p + side]
                wide = share.astype(F32)
                pulled = mm_nt((upstream.astype(F32) * half[side]).astype(BF), values)
                inner = jnp.sum(wide * pulled, 1, keepdims=True)
                slope = (wide * (pulled - inner)).astype(BF)
                dq.append(mm(slope, keys))
                dk.append(mm_tn(slope, queries))
                dv.append(mm_tn(share, upstream))
            jg[:, lanes] = (pick(dq) * scale).astype(BF)
            kvsend[:, 0, :, lanes] = (pick(dk) * scale).astype(BF).reshape(nrow, tokens, LANES)
            kvsend[:, 1, :, lanes] = pick(dv).astype(BF).reshape(nrow, tokens, LANES)
            return carry

        lax.fori_loop(0, pairs, step, 0)

    x_out[...] = x_in[...]
    smg[c] = small[...]
    wqs[0].begin()
    first_copies = net.spread("col", smg.at[c], smg.at[c])
    for level in range(layers):
        copies = norm_send(x_out[...], xg.at[level], st1.at[level])
        if level == 0:
            finish(first_copies)
            wds[0].flip()
            wos[0].begin()
            wus[0].begin()
        finish(copies)
        norm_apply(level, 0, xg.at[level], st1.at[level], inv1.at[level], h.at[level])
        if level == 0:
            wqs[0].share()
        wqs[level].ready()

        def project(j):
            weight = wq[level, :, :, :, j * width : (j + 1) * width].reshape(full, width)
            return mm(h[level], weight)

        kvg[level, r, 0] = project(1).astype(BF)
        kvg[level, r, 1] = (project(2) + param(level, 2)).astype(BF)
        copies = net.spread("row", kvg.at[level, r], kvg.at[level, r])
        q[level] = (project(0) + qbias[level : level + 1, :]).astype(BF)
        if level == 0:
            wos[0].share()
        finish(copies)
        attend(level)
        copies = net.spread("col", og.at[level, c], og.at[level, c])
        if level == 0:
            wds[0].begin()
            wus[0].share()
        finish(copies)
        wos[level].ready()
        branch = param(level, 3)
        for i in range(ncol):
            branch = branch + mm(og[level, i], wo[level, i].reshape(width, width))
        abr[level] = branch
        middle = x_out[...] + param(level, 4) * branch
        x_out[...] = middle
        copies = norm_send(middle, xg2.at[level], st2.at[level])
        if level + 1 < layers:
            wds[level + 1].flip()
        finish(copies)
        norm_apply(level, 5, xg2.at[level], st2.at[level], inv2.at[level], h2.at[level])
        wus[level].ready()
        if level == 0:
            wds[0].share()
        if level + 1 < layers:
            wqs[level + 1].begin()

        def widen_step(j, carry):
            lanes = pl.ds(pl.multiple_of(j * width, width), width)
            pre = mm(h2[level], wu[level, :, :, :, lanes].reshape(full, width)) + ubias[level : level + 1, lanes]
            below = 0.5 * (1.0 + lax.erf(pre * (0.5**0.5)))
            zz[level, :, lanes] = (pre * below).astype(BF)
            bell = jnp.exp(-0.5 * pre * pre) * (0.5 / jnp.pi) ** 0.5
            gp[level, :, lanes] = (below + pre * bell).astype(BF)
            return carry

        lax.fori_loop(0, blocks, widen_step, 0)
        wds[level].ready()
        copies = []
        for step in range(1, ncol + 1):
            i, device = net.peer("col", step)
            part = mm(zz[level], wd[level, i].reshape(hidden, width)).astype(BF)
            if step < ncol:
                msend[i] = part
                copies.append(net.start(msend.at[i], mrecv.at[level, c], device))
            else:
                mrecv[level, c] = part
        if level + 1 < layers:
            wqs[level + 1].share()
            wos[level + 1].begin()
            wus[level + 1].begin()
            wds[level + 1].begin()
        finish(copies)
        branch = slots(mrecv.at[level]) + param(level, 7)
        mbr[level] = branch
        x_out[...] = x_out[...] + param(level, 8) * branch
        if level + 1 < layers:
            wos[level + 1].share()
            wus[level + 1].share()
            wds[level + 1].share()

    sums[...] = jnp.zeros_like(sums)
    per = 9 + 1 + blocks

    def keep(level, index, value):
        sums[level * per + index : level * per + index + 1, :] = jnp.sum(value, 0, keepdims=True)

    def norm_back_send(level, part_of, gain, normed, store, stats):
        copies, first, second = [], 0.0, 0.0
        for step in range(1, ncol + 1):
            i, device = net.peer("col", step)
            part = part_of(i)
            scaled = part * any_param(level, gain, i)
            first = first + jnp.sum(scaled, 1, keepdims=True)
            second = second + jnp.sum(scaled * normed[i].astype(F32), 1, keepdims=True)
            if step < ncol:
                hsend[i] = part.astype(BF)
                copies.append(net.start(hsend.at[i], store.at[c], device))
            else:
                store[c] = part.astype(BF)
        stats[c] = as_rows(first, second)
        return copies + net.spread("col", stats.at[c], stats.at[c])

    def norm_back(level, gain, normed_own, inverse, store, stats):
        upstream = slots(store)
        normed = normed_own.astype(F32)
        keep(level, gain, upstream * normed)
        keep(level, gain + 1, upstream)
        columns = as_columns(slots(stats))
        scaled = upstream * param(level, gain)
        shift = columns[:, 0:1] * (1.0 / full) + normed * (columns[:, 1:2] * (1.0 / full))
        return inverse[:, 0:1] * (scaled - shift)

    def put_grad(i, piece, value):
        grad[piece % 2, i, piece // 2, 0:width, :] = value.astype(BF)

    def grads_down_up(level):
        def step(i, carry):
            down = mm_tn(zz[level], dmg[level, i]).astype(BF)
            rows = hidden // (2 * nz)
            for piece in range(2 * nz):
                grad[piece % 2, i, piece // 2, width:, :] = down[piece * rows : (piece + 1) * rows]
            lanes = pl.ds(pl.multiple_of(i * width, width), width)
            up = mm_tn(h2[level, :, lanes], dur[...])
            for j in range(blocks):
                put_grad(i, 4 + j, up[:, j * width : (j + 1) * width])
            return carry

        lax.fori_loop(0, nrow, step, 0)

    def grads_out(level, low):
        def step(i, carry):
            put_grad(i, 3, mm_tn(og[level, i], low[...]))
            return carry

        lax.fori_loop(0, nrow, step, 0)

    def grads_qkv(level):
        def step(i, carry):
            lanes = pl.ds(pl.multiple_of(i * width, width), width)
            value = mm_tn(h[level, :, lanes], jg[...])
            for j in range(3):
                put_grad(i, j, value[:, j * width : (j + 1) * width])
            return carry

        lax.fori_loop(0, nrow, step, 0)

    def reduce_steps(level):
        upper = ta.shape[1]
        top, low = pl.ds(0, upper), pl.ds(upper, upper)
        copy = net.start(grad.at[1 - core], crecv, net.sibling)
        yield
        copy.wait()

        def add(i, carry):
            for j in range(nz):
                total = grad[core, i, j].astype(F32) + crecv[i, j].astype(F32)
                grad[core, i, j] = total.astype(BF)
            return carry

        lax.fori_loop(0, nrow, add, 0)
        copies = net.deal("row", lambda i: grad.at[core, i, :, top], ra.at[r])
        copies += net.deal("z", lambda i: grad.at[core, :, i, low], rb.at[z])
        yield
        finish(copies)

        def add_top(j, carry):
            total = grad[core, r, j, 0:upper].astype(F32)
            for step in range(1, nrow):
                total = total + ra[net.peer("row", step)[0], j].astype(F32)
            ta[j] = total.astype(BF)
            return carry

        def add_low(j, carry):
            total = grad[core, j, z, upper:].astype(F32)
            for step in range(1, nz):
                total = total + rb[net.peer("z", step)[0], j].astype(F32)
            tb[j] = total.astype(BF)
            return carry

        lax.fori_loop(0, nz, add_top, 0)
        lax.fori_loop(0, nrow, add_low, 0)
        copies = net.deal("z", lambda i: ta.at[i], ua.at[level, z])
        copies += net.deal("row", lambda i: tb.at[i], ub.at[level, r])
        yield
        finish(copies)
        total = ta[z].astype(F32)
        for step in range(1, nz):
            total = total + ua[level, net.peer("z", step)[0]].astype(F32)
        fin[0:upper] = total.astype(BF)
        total = tb[r].astype(F32)
        for step in range(1, nrow):
            total = total + ub[level, net.peer("row", step)[0]].astype(F32)
        fin[upper:] = total.astype(BF)
        turn = flip_start(fin.at[pl.ds(width, fin.shape[0] - width)], fdown.at[level])
        yield
        flip_wait(turn)
        gw[level, core, z, 0:width] = fin[0:width]
        gw[level, core, z, width:] = fdown[level]
        copies = net.spread("z", gw.at[level, core, z], gw.at[level, core, z])
        yield
        finish(copies)
        copy = net.start(gw.at[level, core], gw.at[level, core], net.sibling)
        yield
        copy.wait()
        yield

    g_out[...] = cot[...]
    running = None

    def advance(count=1):
        for _ in range(count):
            if running is not None:
                next(running)

    for level in reversed(range(layers)):
        last = level == 0
        upstream = g_out[...]
        keep(level, 8, upstream * mbr[level])
        scaled = upstream * param(level, 8)
        keep(level, 7, scaled)
        dmg[level, c] = scaled.astype(BF)
        copies = net.spread("col", dmg.at[level, c], dmg.at[level, c])
        advance()
        finish(copies)

        def dz_step(j, carry):
            lanes = pl.ds(pl.multiple_of(j * width, width), width)
            rows = pl.ds(pl.multiple_of((j % (blocks // 2)) * width, width), width)
            value = 0.0
            for i in range(ncol):
                weight = wd[level, i, j // (blocks // 2), rows, :]
                value = value + mm_nt(dmg[level, i], weight)
            value = value * gp[level, :, lanes].astype(F32)
            rounded = value.astype(BF)
            dur[:, lanes] = rounded
            return carry

        lax.fori_loop(0, blocks, dz_step, 0)
        for j in range(blocks):
            keep(level, 10 + j, dur[:, j * width : (j + 1) * width].astype(F32))
        copies = norm_back_send(
            level,
            lambda i: mm_nt(dur[...], wu[level, i].reshape(width, hidden)),
            5, xg2.at[level], hrecv2.at[level], bst2.at[level],
        )
        if not last:
            grads_down_up(level)
        finish(copies)
        middle = g_out[...] + norm_back(
            level, 5, xg2[level, c], inv2.at[level], hrecv2.at[level], bst2.at[level]
        )
        g_out[...] = middle
        keep(level, 4, middle * abr[level])
        scaled = middle * param(level, 4)
        keep(level, 3, scaled)
        dob[...] = scaled.astype(BF)
        copies = []
        for step in range(1, ncol + 1):
            i, device = net.peer("col", step)
            part = mm_nt(dob[...], wo[level, i].reshape(width, width)).astype(BF)
            if step < ncol:
                osend[i] = part
                copies.append(net.start(osend.at[i], orecv.at[level, c], device))
            else:
                orecv[level, c] = part
        if last:
            advance()
        grads_out(level, dob)
        finish(copies)
        dob[...] = slots(orecv.at[level]).astype(BF)
        attend_back(level)
        copies = net.deal("row", lambda i: kvsend.at[i], kvrecv.at[level, r])
        kvrecv[level, r] = kvsend[r]
        if last:
            grads_down_up(level)
        finish(copies)
        for j in range(2):
            total = sum(kvrecv[level, i, j].astype(F32) for i in range(nrow))
            jg[:, (j + 1) * width : (j + 2) * width] = total.astype(BF)
        keep(level, 9, jg[:, 0:width].astype(F32))
        keep(level, 2, jg[:, 2 * width :].astype(F32))
        copies = norm_back_send(
            level,
            lambda i: mm_nt(jg[...], wq[level, i].reshape(width, 3 * width)),
            0, xg.at[level], hrecv1.at[level], bst1.at[level],
        )
        grads_qkv(level)
        if last:
            advance(4)
        running = reduce_steps(level)
        advance()
        finish(copies)
        g_out[...] = g_out[...] + norm_back(
            level, 0, xg[level, c], inv1.at[level], hrecv1.at[level], bst1.at[level]
        )

    sharing = net.start(sums, sumc, net.sibling)
    advance()
    sharing.wait()
    sumy[r] = sums[...] + sumc[...]
    copies = net.spread("row", sumy.at[r], sumy.at[r])
    advance()
    finish(copies)
    sumz[z] = sumy[0] + sumy[1] + sumy[2] + sumy[3]
    copies = net.spread("z", sumz.at[z], sumz.at[z])
    advance()
    finish(copies)
    sums_out[...] = sumz[0] + sumz[1] + sumz[2] + sumz[3]
    advance(3)


def shards(sizes, inputs, w_qkv, w_out, w_up, w_down, small_params, query_bias, up_bias, cotangent):
    tokens, width = inputs.shape
    layers, _, hidden = w_up.shape
    ncol, nrow, nz = sizes["col"], sizes["row"], sizes["z"]
    full, half = width * ncol, width // 2
    blocks = hidden // width
    small = jnp.pad(small_params.reshape(layers * 9, width), ((0, -(layers * 9) % 8), (0, 0)))
    rows = -(-layers * (10 + blocks) // 8) * 8
    piece = width + hidden // (2 * nz)
    vmem = lambda shape, dtype=BF: pltpu.VMEM(shape, dtype)
    scratch = [
        vmem((layers, nrow, 2, half, 3 * width)),
        vmem((layers, nrow, 2, half, width)),
        vmem((layers, nrow, 2, half, hidden)),
        vmem((layers, nrow, 2, hidden // 2, width)),
        vmem((ncol,) + small.shape, F32),
        vmem((layers, ncol, tokens, width)),
        vmem((layers, ncol, 8, tokens), F32),
        vmem((layers, tokens, full)),
        vmem((layers, tokens, width)),
        vmem((layers, nrow, 2, tokens, width)),
        vmem((layers, width // HD, tokens, tokens * nrow)),
        vmem((layers, ncol, tokens, width)),
        vmem((layers, tokens, width), F32),
        vmem((layers, ncol, tokens, width)),
        vmem((layers, ncol, 8, tokens), F32),
        vmem((layers, tokens, full)),
        vmem((layers, tokens, hidden)),
        vmem((layers, tokens, hidden)),
        vmem((layers, tokens, width), F32),
        vmem((layers, tokens, LANES), F32),
        vmem((layers, tokens, LANES), F32),
        vmem((ncol, tokens, width)),
        vmem((layers, ncol, tokens, width)),
        vmem((layers, ncol, tokens, width)),
        vmem((tokens, hidden)),
        vmem((ncol, tokens, width)),
        vmem((layers, ncol, tokens, width)),
        vmem((layers, ncol, 8, tokens), F32),
        vmem((ncol, tokens, width)),
        vmem((layers, ncol, tokens, width)),
        vmem((tokens, width)),
        vmem((nrow, 2, tokens, width)),
        vmem((layers, nrow, 2, tokens, width)),
        vmem((tokens, 3 * width)),
        vmem((layers, ncol, tokens, width)),
        vmem((layers, ncol, 8, tokens), F32),
        vmem((2, nrow, nz, piece, width)),
        vmem((nrow, nz, piece, width)),
        vmem((nrow, nz, piece // 2, width)),
        vmem((nz, nrow, piece // 2, width)),
        vmem((nz, piece // 2, width)),
        vmem((nrow, piece // 2, width)),
        vmem((layers, nz, piece // 2, width)),
        vmem((layers, nrow, piece // 2, width)),
        vmem((piece, width)),
        vmem((layers, piece - width, width)),
        vmem((rows, width), F32),
        vmem((rows, width), F32),
        vmem((nrow, rows, width), F32),
        vmem((nz, rows, width), F32),
        pltpu.SemaphoreType.DMA((192,)),
        pltpu.SemaphoreType.DMA((192,)),
        pltpu.SemaphoreType.DMA((16,)),
    ]
    here = pl.BlockSpec(memory_space=pltpu.VMEM)
    far = pl.BlockSpec(memory_space=pl.ANY)
    output, input_grad, grads, sums = pl.pallas_call(
        partial(body, sizes, layers),
        out_shape=(
            jax.ShapeDtypeStruct((tokens, width), F32),
            jax.ShapeDtypeStruct((tokens, width), F32),
            jax.ShapeDtypeStruct((layers, 2, nz, piece, width), BF),
            jax.ShapeDtypeStruct((rows, width), F32),
        ),
        in_specs=[here] * 5 + [far] * 4,
        out_specs=(here,) * 4,
        scratch_shapes=scratch,
        compiler_params=pltpu.CompilerParams(
            collective_id=0, has_side_effects=True, vmem_limit_bytes=63 << 20
        ),
        name="encoder",
    )(
        inputs,
        cotangent,
        small,
        query_bias,
        up_bias,
        w_qkv.reshape(layers, 2, half, 3 * width),
        w_out.reshape(layers, 2, half, width),
        w_up.reshape(layers, 2, half, hidden),
        w_down.reshape(layers, 2, hidden // 2, width),
    )
    grads = jnp.swapaxes(grads, 1, 2).reshape(layers, 2 * nz, piece, width).astype(F32)
    sums = sums[: layers * (10 + blocks)].reshape(layers, 10 + blocks, width)
    return (
        output,
        input_grad,
        jnp.swapaxes(grads[:, 0:3, :width], 1, 2),
        grads[:, 3, :width],
        jnp.swapaxes(grads[:, 4 : 4 + blocks, :width], 1, 2).reshape(layers, width, hidden),
        grads[:, :, width:].reshape(layers, hidden, width),
        sums[:, :9],
        sums[:, 9],
        sums[:, 10:].reshape(layers, hidden),
    )


def solution(mesh):
    sizes = {"col": mesh.shape["col"], "row": mesh.shape["row"], "z": mesh.shape["dp"] // 2}
    placed = (
        P(("dp", "row"), "col"),
        P(None, "row", None, "col"),
        P(None, "row", "col"),
        P(None, "row", "col"),
        P(None, "row", "col"),
        P(None, None, "col"),
        P(None, "col"),
        P(None, "col"),
        P(("dp", "row"), "col"),
    )
    return jax.shard_map(
        partial(shards, sizes),
        mesh=mesh,
        in_specs=placed,
        out_specs=(
            P(("dp", "row"), "col"),
            P(("dp", "row"), "col"),
            P(None, "row", None, "col"),
            P(None, "row", "col"),
            P(None, "row", "col"),
            P(None, "row", "col"),
            P(None, None, "col"),
            P(None, "col"),
            P(None, "col"),
        ),
        check_vma=False,
    )
```

```python
from functools import partial

import jax
import jax.numpy as jnp
from jax import lax
from jax.experimental import pallas as pl
from jax.experimental.pallas import tpu as pltpu
from jax.sharding import PartitionSpec as P

HD = 64
EPS = 1e-06
LANES = 128
BF = jnp.bfloat16
F32 = jnp.float32
MESH = pl.DeviceIdType.MESH


def mm(left, right):
    return jnp.dot(left, right, preferred_element_type=F32)


def mm_nt(left, right):
    return lax.dot_general(left, right, (((1,), (1,)), ((), ())), preferred_element_type=F32)


def mm_tn(left, right):
    return lax.dot_general(left, right, (((0,), (0,)), ((), ())), preferred_element_type=F32)


class Links:
    def __init__(self, sizes, send, recv, local):
        self.sizes = sizes
        self.send, self.recv, self.local = send, recv, local
        self.used = 0
        self.used_local = 0
        self.col = lax.axis_index("col")
        self.row = lax.axis_index("row")
        place = lax.axis_index("dp")
        self.z = place // 2
        self.core = place % 2
        self.sibling = {"dp": self.z * 2 + (1 - self.core)}

    def peer(self, axis, step):
        if axis == "z":
            index = lax.rem(self.z + step, self.sizes["z"])
            return index, {"dp": index * 2 + self.core}
        index = lax.rem(getattr(self, axis) + step, self.sizes[axis])
        return index, {axis: index}

    def start(self, source, target, device, begin=True):
        copy = pltpu.make_async_remote_copy(
            src_ref=source,
            dst_ref=target,
            send_sem=self.send.at[self.used],
            recv_sem=self.recv.at[self.used],
            device_id=device,
            device_id_type=MESH,
        )
        self.used += 1
        if begin:
            copy.start()
        return copy

    def bring(self, source, target):
        copy = pltpu.make_async_copy(source, target, self.local.at[self.used_local])
        self.used_local += 1
        copy.start()
        return copy

    def spread(self, axis, source, target):
        return [
            self.start(source, target, self.peer(axis, step)[1])
            for step in range(1, self.sizes[axis])
        ]

    def deal(self, axis, source_of, target):
        copies = []
        for step in range(1, self.sizes[axis]):
            index, device = self.peer(axis, step)
            copies.append(self.start(source_of(index), target, device))
        return copies


def finish(copies):
    for copy in copies:
        copy.wait()


def as_rows(first, second):
    tokens = first.shape[0]
    lane = lax.broadcasted_iota(jnp.int32, (tokens, LANES), 1)
    both = jnp.where(lane == 0, first, jnp.where(lane == 1, second, 0.0))
    return both.T[:8]


def as_columns(rows):
    count, tokens = rows.shape
    return jnp.concatenate([rows, jnp.zeros((LANES - count, tokens), F32)], 0).T


def body(sizes, layers, *refs):
    (
        x_in, cot, small, qbias, ubias, wq_in, wo_in, wu_in, wd_in,
        x_out, g_out, gq, gout, gup, gdown, sums_out,
        wq, wo, wu, wd, smg, xg, st1, h, q, kvg, probs, og, abr, xg2, st2, h2, gp, zz, mbr,
        inv1, inv2, msend, mrecv, dmg, dur, hsend, hrecv2, bst2, osend, orecv, dob, kvsend, kvrecv,
        jg, hrecv1, bst1, sums, sumc, sumy, sumz, *chunk_refs, send, recv, local,
    ) = refs
    bulk, tail = chunk_refs[: len(chunk_refs) // 2], chunk_refs[len(chunk_refs) // 2 :]
    net = Links(sizes, send, recv, local)
    c, r, z, core = net.col, net.row, net.z, net.core
    ncol, nrow, nz = sizes["col"], sizes["row"], sizes["z"]
    tokens, width = x_in.shape
    hidden = ubias.shape[1]
    full = width * ncol
    length = tokens * nrow
    blocks = hidden // width
    pairs = width // LANES
    scale = HD ** (-0.5)

    barrier = pltpu.get_barrier_semaphore()
    greeted = [net.peer(a, s)[1] for a in ("col", "row", "z") for s in range(1, sizes[a])]
    greeted.append(net.sibling)
    for device in greeted:
        pl.semaphore_signal(barrier, inc=1, device_id=device, device_id_type=MESH)
    mirror = {"row": c, "col": r}

    @pl.when(r != c)
    def _():
        pl.semaphore_signal(barrier, inc=1, device_id=mirror, device_id_type=MESH)

    pl.semaphore_wait(barrier, len(greeted) + jnp.where(r != c, 1, 0))

    def flip_start(source, target):
        copy = net.start(source, target, mirror, begin=False)
        here = pltpu.make_async_copy(source, target, local.at[net.used_local])
        net.used_local += 1

        @pl.when(r != c)
        def _():
            copy.start()

        @pl.when(r == c)
        def _():
            here.start()

        return copy, here

    def flip_wait(pair):
        copy, here = pair

        @pl.when(r != c)
        def _():
            copy.wait()

        @pl.when(r == c)
        def _():
            here.wait()

    class Weight:
        def __init__(self, level, source, store):
            self.level, self.source, self.store = level, source, store

        def begin(self):
            place = self.store.at[self.level, r, core]
            source = self.source.at[self.level, core]
            self.copies = [net.bring(source, place)] + net.spread("row", source, place)

        def share(self):
            finish(self.copies)
            place = self.store.at[self.level, :, core]
            self.shared = net.start(place, place, net.sibling)

        def ready(self):
            self.shared.wait()

    class Relayed(Weight):
        def begin(self):
            place = self.store.at[self.level, r, core, z]
            self.own = net.bring(self.source.at[self.level, core], self.store.at[self.level, r, core])
            self.copies = net.spread("row", self.source.at[self.level, core, z], place)

        def relay(self):
            finish(self.copies)
            self.copies = [self.own]
            for step in range(1, nrow):
                i, _ = net.peer("row", step)
                place = self.store.at[self.level, i, core, z]
                self.copies += net.spread("z", place, place)

    class Flipped(Weight):
        def flip(self):
            self.turn = flip_start(
                self.source.at[self.level, core, z], self.store.at[self.level, c, core, z]
            )

        def begin(self):
            place = self.store.at[self.level, r, core, z]
            flip_wait(self.turn)
            self.copies = net.spread("row", place, place)

        def relay(self):
            finish(self.copies)
            place = self.store.at[self.level, :, core, z]
            self.copies = net.spread("z", place, place)

    wqs = [Weight(l, wq_in, wq) for l in range(layers)]
    wos = [Weight(l, wo_in, wo) for l in range(layers)]
    wus = [Relayed(l, wu_in, wu) for l in range(layers)]
    wds = [Flipped(l, wd_in, wd) for l in range(layers)]

    def param(level, index):
        return small[level, index : index + 1, :]

    def any_param(level, index, block):
        return smg[block, level, index : index + 1, :]

    def norm_send(value, store, stats):
        mean = jnp.sum(value, 1, keepdims=True) * (1.0 / width)
        centered = value - mean
        store[c] = centered.astype(BF)
        stats[c] = as_rows(mean, jnp.sum(centered * centered, 1, keepdims=True))
        return net.spread("col", store.at[c], store.at[c]) + net.spread("col", stats.at[c], stats.at[c])

    def norm_apply(level, first, store, stats, inverse, result):
        columns = as_columns(stats[...].reshape(ncol * 8, tokens))
        means = [columns[:, 8 * i : 8 * i + 1] for i in range(ncol)]
        mean = sum(means) * (1.0 / ncol)
        spread = sum(columns[:, 8 * i + 1 : 8 * i + 2] for i in range(ncol))
        spread = spread + width * sum((m - mean) * (m - mean) for m in means)
        scaled = lax.rsqrt(spread * (1.0 / full) + EPS)
        inverse[...] = jnp.broadcast_to(scaled, inverse.shape)
        for i in range(ncol):
            normed = (store[i].astype(F32) + (means[i] - mean)) * scaled
            store[i] = normed.astype(BF)
            result[:, i * width : (i + 1) * width] = (
                normed * any_param(level, first, i) + any_param(level, first + 1, i)
            ).astype(BF)

    def slots(store):
        return sum(store[i].astype(F32) for i in range(store.shape[0]))

    lane = lax.broadcasted_iota(jnp.int32, (tokens, LANES), 1)
    half = [(lane < HD).astype(F32), (lane >= HD).astype(F32)]

    def pick(values):
        side = lax.broadcasted_iota(jnp.int32, values[0].shape, 1)
        return jnp.where(side < HD, values[0], values[1])

    def pair_lanes(p):
        return pl.ds(pl.multiple_of(p * LANES, LANES), LANES)

    def attend(level):
        copies = []
        for p in range(pairs):
            lanes = slice(p * LANES, (p + 1) * LANES)
            queries = q[level, :, lanes].astype(F32)
            keys = kvg[level, :, 0, :, lanes].reshape(length, LANES)
            values = kvg[level, :, 1, :, lanes].reshape(length, LANES)
            found = []
            for side in range(2):
                scores = mm_nt((queries * half[side]).astype(BF), keys) * scale
                raised = jnp.exp(scores - jnp.max(scores, 1, keepdims=True))
                share = (raised * (1.0 / jnp.sum(raised, 1, keepdims=True))).astype(BF)
                probs[level, 2 * p + side] = share
                found.append(mm(share, values))
            og[level, c, p] = pick(found).astype(BF)
            place = og.at[level, c, p]
            copies += net.spread("col", place, place)
        return copies

    def attended(level, i):
        return jnp.concatenate([og[level, i, p] for p in range(pairs)], 1)

    def attend_back(level):
        def step(p, carry):
            lanes = pair_lanes(p)
            queries = q[level, :, lanes]
            upstream = dob[:, lanes]
            keys = kvg[level, :, 0, :, lanes].reshape(length, LANES)
            values = kvg[level, :, 1, :, lanes].reshape(length, LANES)
            dq, dk, dv = [], [], []
            for side in range(2):
                share = probs[level, 2 * p + side]
                wide = share.astype(F32)
                pulled = mm_nt((upstream.astype(F32) * half[side]).astype(BF), values)
                inner = jnp.sum(wide * pulled, 1, keepdims=True)
                slope = (wide * (pulled - inner)).astype(BF)
                dq.append(mm(slope, keys))
                dk.append(mm_tn(slope, queries))
                dv.append(mm_tn(share, upstream))
            jg[:, lanes] = (pick(dq) * scale).astype(BF)
            kvsend[:, 0, :, lanes] = (pick(dk) * scale).astype(BF).reshape(nrow, tokens, LANES)
            kvsend[:, 1, :, lanes] = pick(dv).astype(BF).reshape(nrow, tokens, LANES)
            return carry

        lax.fori_loop(0, pairs, step, 0)

    x_out[...] = x_in[...]
    smg[c, :, 0 : small.shape[1]] = small[...]
    wqs[0].begin()
    first_copies = net.spread("col", smg.at[c], smg.at[c])
    for level in range(layers):
        copies = norm_send(x_out[...], xg.at[level], st1.at[level])
        if level == 0:
            wos[0].begin()
            wus[0].begin()
            wds[0].flip()
            finish(first_copies)
        finish(copies)
        norm_apply(level, 0, xg.at[level], st1.at[level], inv1.at[level], h.at[level])
        if level == 0:
            wqs[0].share()
            wds[0].begin()
        wqs[level].ready()

        def project(j):
            weight = wq[level, :, :, :, j * width : (j + 1) * width].reshape(full, width)
            return mm(h[level], weight)

        kvg[level, r, 0] = project(1).astype(BF)
        kvg[level, r, 1] = (project(2) + param(level, 2)).astype(BF)
        copies = net.spread("row", kvg.at[level, r], kvg.at[level, r])
        q[level] = (project(0) + qbias[level : level + 1, :]).astype(BF)
        wus[level].relay()
        wds[level].relay()
        if level == 0:
            wos[0].share()
        finish(copies)
        copies = attend(level)
        wus[level].share()
        if level + 1 < layers:
            wqs[level + 1].begin()
            wos[level + 1].begin()
            wus[level + 1].begin()
            wds[level + 1].flip()
        finish(copies)
        wos[level].ready()
        branch = param(level, 3)
        for i in range(ncol):
            branch = branch + mm(attended(level, i), wo[level, i].reshape(width, width))
        abr[level] = branch
        middle = x_out[...] + param(level, 4) * branch
        x_out[...] = middle
        copies = norm_send(middle, xg2.at[level], st2.at[level])
        wds[level].share()
        if level + 1 < layers:
            wds[level + 1].begin()
        finish(copies)
        norm_apply(level, 5, xg2.at[level], st2.at[level], inv2.at[level], h2.at[level])
        wus[level].ready()

        def widen_step(j, carry):
            lanes = pl.ds(pl.multiple_of(j * width, width), width)
            pre = mm(h2[level], wu[level, :, :, :, :, lanes].reshape(full, width)) + ubias[level : level + 1, lanes]
            below = 0.5 * (1.0 + lax.erf(pre * (0.5**0.5)))
            zz[level, :, lanes] = (pre * below).astype(BF)
            bell = jnp.exp(-0.5 * pre * pre) * (0.5 / jnp.pi) ** 0.5
            gp[level, :, lanes] = (below + pre * bell).astype(BF)
            return carry

        lax.fori_loop(0, blocks, widen_step, 0)
        wds[level].ready()
        copies = []
        for step in range(1, ncol + 1):
            i, device = net.peer("col", step)
            part = mm(zz[level], wd[level, i].reshape(hidden, width)).astype(BF)
            if step < ncol:
                msend[i] = part
                copies.append(net.start(msend.at[i], mrecv.at[level, c], device))
            else:
                mrecv[level, c] = part
        if level + 1 < layers:
            wqs[level + 1].share()
            wos[level + 1].share()
        finish(copies)
        branch = slots(mrecv.at[level]) + param(level, 7)
        mbr[level] = branch
        x_out[...] = x_out[...] + param(level, 8) * branch

    sums[...] = jnp.zeros_like(sums)
    per = 9 + 1 + blocks

    def keep(level, index, value):
        sums[level * per + index : level * per + index + 1, :] = jnp.sum(value, 0, keepdims=True)

    def norm_back_send(level, part_of, gain, normed, store, stats):
        copies, first, second = [], 0.0, 0.0
        for step in range(1, ncol + 1):
            i, device = net.peer("col", step)
            part = part_of(i)
            scaled = part * any_param(level, gain, i)
            first = first + jnp.sum(scaled, 1, keepdims=True)
            second = second + jnp.sum(scaled * normed[i].astype(F32), 1, keepdims=True)
            if step < ncol:
                hsend[i] = part.astype(BF)
                copies.append(net.start(hsend.at[i], store.at[c], device))
            else:
                store[c] = part.astype(BF)
        stats[c] = as_rows(first, second)
        return copies + net.spread("col", stats.at[c], stats.at[c])

    def norm_back(level, gain, normed_own, inverse, store, stats):
        upstream = slots(store)
        normed = normed_own.astype(F32)
        keep(level, gain, upstream * normed)
        keep(level, gain + 1, upstream)
        columns = as_columns(slots(stats))
        scaled = upstream * param(level, gain)
        shift = columns[:, 0:1] * (1.0 / full) + normed * (columns[:, 1:2] * (1.0 / full))
        return inverse[:, 0:1] * (scaled - shift)

    pieces = 2 * nz
    part_out, part_up = width // pieces, hidden // pieces

    def put_rows(store, i, start, value):
        rows = value.shape[0] // pieces
        for piece in range(pieces):
            store[piece % 2, i, piece // 2, start : start + rows, :] = value[piece * rows : (piece + 1) * rows]

    def grads_down_up(level):
        def step(i, carry):
            put_rows(bulk[0], i, part_out + part_up, mm_tn(zz[level], dmg[level, i]).astype(BF))
            lanes = pl.ds(pl.multiple_of(i * width, width), width)
            up = mm_tn(h2[level, :, lanes], dur[...]).astype(BF)
            up = [up[:, j * width : (j + 1) * width] for j in range(blocks)]
            put_rows(bulk[0], i, part_out, jnp.concatenate(up, 0))
            return carry

        lax.fori_loop(0, nrow, step, 0)

    def grads_out(level, low):
        def step(i, carry):
            put_rows(bulk[0], i, 0, mm_tn(attended(level, i), low[...]).astype(BF))
            return carry

        lax.fori_loop(0, nrow, step, 0)

    def grads_qkv(level):
        def step(i, carry):
            lanes = pl.ds(pl.multiple_of(i * width, width), width)
            value = mm_tn(h[level, :, lanes], jg[...]).astype(BF)
            for j in range(3):
                put_rows(tail[0], i, j * part_out, value[:, j * width : (j + 1) * width])
            return carry

        lax.fori_loop(0, nrow, step, 0)

    def reduce_steps(level, store, flipping):
        grad, crecv, ra, rb, ta, tb, ua, ub, fin, flipped, land = store
        rows = grad.shape[3]
        upper = rows // 2
        top, low = pl.ds(0, upper), pl.ds(upper, upper)
        copy = net.start(grad.at[1 - core], crecv, net.sibling)
        yield
        copy.wait()

        def add(i, carry):
            for j in range(nz):
                total = grad[core, i, j].astype(F32) + crecv[i, j].astype(F32)
                grad[core, i, j] = total.astype(BF)
            return carry

        lax.fori_loop(0, nrow, add, 0)
        copies = net.deal("row", lambda i: grad.at[core, i, :, top], ra.at[r])
        copies += net.deal("z", lambda i: grad.at[core, :, i, low], rb.at[z])
        yield
        finish(copies)

        def add_top(j, carry):
            total = grad[core, r, j, 0:upper].astype(F32)
            for step in range(1, nrow):
                total = total + ra[net.peer("row", step)[0], j].astype(F32)
            ta[j] = total.astype(BF)
            return carry

        def add_low(j, carry):
            total = grad[core, j, z, upper:].astype(F32)
            for step in range(1, nz):
                total = total + rb[net.peer("z", step)[0], j].astype(F32)
            tb[j] = total.astype(BF)
            return carry

        lax.fori_loop(0, nz, add_top, 0)
        lax.fori_loop(0, nrow, add_low, 0)
        copies = net.deal("z", lambda i: ta.at[i], ua.at[level, z])
        copies += net.deal("row", lambda i: tb.at[i], ub.at[level, r])
        yield
        finish(copies)
        total = ta[z].astype(F32)
        for step in range(1, nz):
            total = total + ua[level, net.peer("z", step)[0]].astype(F32)
        fin[level, 0:upper] = total.astype(BF)
        total = tb[r].astype(F32)
        for step in range(1, nrow):
            total = total + ub[level, net.peer("row", step)[0]].astype(F32)
        fin[level, upper:] = total.astype(BF)
        straight = rows - (part_up if flipping else 0)
        if flipping:
            turn = flip_start(fin.at[level, pl.ds(straight, part_up)], flipped.at[level])
            yield
            flip_wait(turn)
            land[core, z, straight:] = flipped[level]
        land[core, z, 0:straight] = fin[level, 0:straight]
        copies = net.spread("z", land.at[core, z], land.at[core, z])
        yield
        finish(copies)
        copy = net.start(land.at[core], land.at[core], net.sibling)
        yield
        copy.wait()
        for piece in range(pieces):
            found = land[piece % 2, piece // 2]
            some = slice(piece * part_out, (piece + 1) * part_out)
            if flipping:
                gout[level, some] = found[0:part_out]
                block, inner = divmod(piece * part_up, width)
                gup[level, inner : inner + part_up, block * width : (block + 1) * width] = found[
                    part_out : part_out + part_up
                ]
                gdown[level, piece * part_up : (piece + 1) * part_up] = found[part_out + part_up :]
            else:
                for j in range(3):
                    gq[level, j, some] = found[j * part_out : (j + 1) * part_out]
        yield

    g_out[...] = cot[...]
    heavy, light = [], []

    def advance(queue):
        for steps in queue:
            next(steps, None)

    for level in reversed(range(layers)):
        last = level == 0
        upstream = g_out[...]
        keep(level, 8, upstream * mbr[level])
        scaled = upstream * param(level, 8)
        keep(level, 7, scaled)
        dmg[level, c] = scaled.astype(BF)
        copies = net.spread("col", dmg.at[level, c], dmg.at[level, c])
        advance(heavy)
        advance(light)
        finish(copies)

        def dz_step(j, carry):
            lanes = pl.ds(pl.multiple_of(j * width, width), width)
            per_half = blocks // 2
            group = width // part_up
            value = 0.0
            for i in range(ncol):
                weight = wd[level, i, j // per_half, pl.ds((j % per_half) * group, group)]
                value = value + mm_nt(dmg[level, i], weight.reshape(width, width))
            value = value * gp[level, :, lanes].astype(F32)
            dur[:, lanes] = value.astype(BF)
            return carry

        lax.fori_loop(0, blocks, dz_step, 0)
        for j in range(blocks):
            keep(level, 10 + j, dur[:, j * width : (j + 1) * width].astype(F32))
        copies = norm_back_send(
            level,
            lambda i: mm_nt(dur[...], wu[level, i].reshape(width, hidden)),
            5, xg2.at[level], hrecv2.at[level], bst2.at[level],
        )
        advance(heavy)
        advance(light)
        grads_down_up(level)
        finish(copies)
        middle = g_out[...] + norm_back(
            level, 5, xg2[level, c], inv2.at[level], hrecv2.at[level], bst2.at[level]
        )
        g_out[...] = middle
        keep(level, 4, middle * abr[level])
        scaled = middle * param(level, 4)
        keep(level, 3, scaled)
        dob[...] = scaled.astype(BF)
        copies = []
        for step in range(1, ncol + 1):
            i, device = net.peer("col", step)
            part = mm_nt(dob[...], wo[level, i].reshape(width, width)).astype(BF)
            if step < ncol:
                osend[i] = part
                copies.append(net.start(osend.at[i], orecv.at[level, c], device))
            else:
                orecv[level, c] = part
        advance(heavy)
        advance(light)
        grads_out(level, dob)
        heavy.append(reduce_steps(level, bulk, True))
        advance(heavy[-1:])
        finish(copies)
        dob[...] = slots(orecv.at[level]).astype(BF)
        attend_back(level)
        copies = net.deal("row", lambda i: kvsend.at[i], kvrecv.at[level, r])
        kvrecv[level, r] = kvsend[r]
        advance(heavy)
        advance(light)
        finish(copies)
        for j in range(2):
            total = sum(kvrecv[level, i, j].astype(F32) for i in range(nrow))
            jg[:, (j + 1) * width : (j + 2) * width] = total.astype(BF)
        keep(level, 9, jg[:, 0:width].astype(F32))
        keep(level, 2, jg[:, 2 * width :].astype(F32))
        copies = norm_back_send(
            level,
            lambda i: mm_nt(jg[...], wq[level, i].reshape(width, 3 * width)),
            0, xg.at[level], hrecv1.at[level], bst1.at[level],
        )
        advance(light)
        grads_qkv(level)
        light.append(reduce_steps(level, tail, False))
        advance(light[-1:])
        advance(heavy)
        finish(copies)
        g_out[...] = g_out[...] + norm_back(
            level, 0, xg[level, c], inv1.at[level], hrecv1.at[level], bst1.at[level]
        )

    sharing = net.start(sums, sumc, net.sibling)
    advance(light)
    advance(heavy)
    sharing.wait()
    sumy[r] = sums[...] + sumc[...]
    copies = net.spread("row", sumy.at[r], sumy.at[r])
    advance(light)
    advance(heavy)
    finish(copies)
    sumz[z] = sumy[0] + sumy[1] + sumy[2] + sumy[3]
    copies = net.spread("z", sumz.at[z], sumz.at[z])
    advance(light)
    advance(heavy)
    finish(copies)
    sums_out[...] = sumz[0] + sumz[1] + sumz[2] + sumz[3]
    for steps in light + heavy:
        for _ in steps:
            pass


def shards(sizes, inputs, w_qkv, w_out, w_up, w_down, small_params, query_bias, up_bias, cotangent):
    tokens, width = inputs.shape
    layers, _, hidden = w_up.shape
    ncol, nrow, nz = sizes["col"], sizes["row"], sizes["z"]
    full, half = width * ncol, width // 2
    blocks = hidden // width
    rows = -(-layers * (10 + blocks) // 8) * 8
    bulk, tail = (width + 2 * hidden) // (2 * nz), 3 * width // (2 * nz)
    vmem = lambda shape, dtype=BF: pltpu.VMEM(shape, dtype)
    scratch = [
        vmem((layers, nrow, 2, half, 3 * width)),
        vmem((layers, nrow, 2, half, width)),
        vmem((layers, nrow, 2, nz, half // nz, hidden)),
        vmem((layers, nrow, 2, nz, hidden // (2 * nz), width)),
        vmem((ncol, layers, 16, width), F32),
        vmem((layers, ncol, tokens, width)),
        vmem((layers, ncol, 8, tokens), F32),
        vmem((layers, tokens, full)),
        vmem((layers, tokens, width)),
        vmem((layers, nrow, 2, tokens, width)),
        vmem((layers, width // HD, tokens, tokens * nrow)),
        vmem((layers, ncol, width // LANES, tokens, LANES)),
        vmem((layers, tokens, width), F32),
        vmem((layers, ncol, tokens, width)),
        vmem((layers, ncol, 8, tokens), F32),
        vmem((layers, tokens, full)),
        vmem((layers, tokens, hidden)),
        vmem((layers, tokens, hidden)),
        vmem((layers, tokens, width), F32),
        vmem((layers, tokens, LANES), F32),
        vmem((layers, tokens, LANES), F32),
        vmem((ncol, tokens, width)),
        vmem((layers, ncol, tokens, width)),
        vmem((layers, ncol, tokens, width)),
        vmem((tokens, hidden)),
        vmem((ncol, tokens, width)),
        vmem((layers, ncol, tokens, width)),
        vmem((layers, ncol, 8, tokens), F32),
        vmem((ncol, tokens, width)),
        vmem((layers, ncol, tokens, width)),
        vmem((tokens, width)),
        vmem((nrow, 2, tokens, width)),
        vmem((layers, nrow, 2, tokens, width)),
        vmem((tokens, 3 * width)),
        vmem((layers, ncol, tokens, width)),
        vmem((layers, ncol, 8, tokens), F32),
        vmem((rows, width), F32),
        vmem((rows, width), F32),
        vmem((nrow, rows, width), F32),
        vmem((nz, rows, width), F32),
    ]
    for piece in (bulk, tail):
        scratch += [
            vmem((2, nrow, nz, piece, width)),
            vmem((nrow, nz, piece, width)),
            vmem((nrow, nz, piece // 2, width)),
            vmem((nz, nrow, piece // 2, width)),
            vmem((nz, piece // 2, width)),
            vmem((nrow, piece // 2, width)),
            vmem((layers, nz, piece // 2, width)),
            vmem((layers, nrow, piece // 2, width)),
            vmem((layers, piece, width)),
            vmem((layers, hidden // (2 * nz), width)),
            vmem((2, nz, piece, width)),
        ]
    scratch += [
        pltpu.SemaphoreType.DMA((256,)),
        pltpu.SemaphoreType.DMA((256,)),
        pltpu.SemaphoreType.DMA((16,)),
    ]
    here = pl.BlockSpec(memory_space=pltpu.VMEM)
    far = pl.BlockSpec(memory_space=pl.ANY)
    output, input_grad, qkv, out, up, down, sums = pl.pallas_call(
        partial(body, sizes, layers),
        out_shape=(
            jax.ShapeDtypeStruct((tokens, width), F32),
            jax.ShapeDtypeStruct((tokens, width), F32),
            jax.ShapeDtypeStruct((layers, 3, width, width), BF),
            jax.ShapeDtypeStruct((layers, width, width), BF),
            jax.ShapeDtypeStruct((layers, width, hidden), BF),
            jax.ShapeDtypeStruct((layers, hidden, width), BF),
            jax.ShapeDtypeStruct((rows, width), F32),
        ),
        in_specs=[here] * 5 + [far] * 4,
        out_specs=(here,) * 7,
        scratch_shapes=scratch,
        compiler_params=pltpu.CompilerParams(
            collective_id=0, has_side_effects=True, vmem_limit_bytes=63 << 20
        ),
        name="encoder",
    )(
        inputs,
        cotangent,
        small_params,
        query_bias,
        up_bias,
        w_qkv.reshape(layers, 2, half, 3 * width),
        w_out.reshape(layers, 2, half, width),
        w_up.reshape(layers, 2, nz, half // nz, hidden),
        w_down.reshape(layers, 2, nz, hidden // (2 * nz), width),
    )
    sums = sums[: layers * (10 + blocks)].reshape(layers, 10 + blocks, width)
    return (
        output,
        input_grad,
        jnp.swapaxes(qkv, 1, 2).astype(F32),
        out.astype(F32),
        up.astype(F32),
        down.astype(F32),
        sums[:, :9],
        sums[:, 9],
        sums[:, 10:].reshape(layers, hidden),
    )


def solution(mesh):
    sizes = {"col": mesh.shape["col"], "row": mesh.shape["row"], "z": mesh.shape["dp"] // 2}
    placed = (
        P(("dp", "row"), "col"),
        P(None, "row", None, "col"),
        P(None, "row", "col"),
        P(None, "row", "col"),
        P(None, "row", "col"),
        P(None, None, "col"),
        P(None, "col"),
        P(None, "col"),
        P(("dp", "row"), "col"),
    )
    return jax.shard_map(
        partial(shards, sizes),
        mesh=mesh,
        in_specs=placed,
        out_specs=(
            P(("dp", "row"), "col"),
            P(("dp", "row"), "col"),
            P(None, "row", None, "col"),
            P(None, "row", "col"),
            P(None, "row", "col"),
            P(None, "row", "col"),
            P(None, None, "col"),
            P(None, "col"),
            P(None, "col"),
        ),
        check_vma=False,
    )
```

```python
from functools import partial

import jax
import jax.numpy as jnp
from jax import lax
from jax.experimental import pallas as pl
from jax.experimental.pallas import tpu as pltpu
from jax.sharding import PartitionSpec as P

HD = 64
EPS = 1e-06
LANES = 128
CHUNKS = 2
BF = jnp.bfloat16
F32 = jnp.float32
MESH = pl.DeviceIdType.MESH


def mm(left, right):
    return jnp.dot(left, right, preferred_element_type=F32)


def mm_nt(left, right):
    return lax.dot_general(left, right, (((1,), (1,)), ((), ())), preferred_element_type=F32)


def mm_tn(left, right):
    return lax.dot_general(left, right, (((0,), (0,)), ((), ())), preferred_element_type=F32)


class Links:
    def __init__(self, sizes, send, recv, local):
        self.sizes = sizes
        self.send, self.recv, self.local = send, recv, local
        self.used = 0
        self.used_local = 0
        self.col = lax.axis_index("col")
        self.row = lax.axis_index("row")
        place = lax.axis_index("dp")
        self.z = place // 2
        self.core = place % 2
        self.sibling = {"dp": self.z * 2 + (1 - self.core)}

    def peer(self, axis, step):
        if axis == "z":
            index = lax.rem(self.z + step, self.sizes["z"])
            return index, {"dp": index * 2 + self.core}
        index = lax.rem(getattr(self, axis) + step, self.sizes[axis])
        return index, {axis: index}

    def start(self, source, target, device, begin=True):
        copy = pltpu.make_async_remote_copy(
            src_ref=source,
            dst_ref=target,
            send_sem=self.send.at[self.used],
            recv_sem=self.recv.at[self.used],
            device_id=device,
            device_id_type=MESH,
        )
        self.used += 1
        if begin:
            copy.start()
        return copy

    def bring(self, source, target):
        copy = pltpu.make_async_copy(source, target, self.local.at[self.used_local])
        self.used_local += 1
        copy.start()
        return copy

    def spread(self, axis, source, target):
        return [
            self.start(source, target, self.peer(axis, step)[1])
            for step in range(1, self.sizes[axis])
        ]

    def deal(self, axis, source_of, target):
        copies = []
        for step in range(1, self.sizes[axis]):
            index, device = self.peer(axis, step)
            copies.append(self.start(source_of(index), target, device))
        return copies


def finish(copies):
    for copy in copies:
        copy.wait()


def as_rows(first, second):
    tokens = first.shape[0]
    lane = lax.broadcasted_iota(jnp.int32, (tokens, LANES), 1)
    both = jnp.where(lane == 0, first, jnp.where(lane == 1, second, 0.0))
    return both.T[:8]


def as_columns(rows):
    count, tokens = rows.shape
    return jnp.concatenate([rows, jnp.zeros((LANES - count, tokens), F32)], 0).T


def body(sizes, layers, *refs):
    (
        x_in, cot, small, qbias, ubias, wq_in, wo_in, wu_in, wd_in,
        x_out, g_out, gq, gout, gup, gdown, small_out, qbias_out, ubias_out,
        wq, wo, wu, wd, smg, xg, st1, h, q, kvg, probs, og, abr, xg2, st2, h2, gp, zz, mbr,
        inv1, inv2, msend, mrecv, dmg, dur, hsend, hrecv2, bst2, osend, orecv, dob, kvsend, kvrecv,
        jg, hrecv1, bst1, sums, sumc, sumy, sumz, *chunk_refs, send, recv, local,
    ) = refs
    bulk, tail = chunk_refs[: len(chunk_refs) // 2], chunk_refs[len(chunk_refs) // 2 :]
    net = Links(sizes, send, recv, local)
    c, r, z, core = net.col, net.row, net.z, net.core
    ncol, nrow, nz = sizes["col"], sizes["row"], sizes["z"]
    tokens, width = x_in.shape
    hidden = ubias.shape[1]
    full = width * ncol
    length = tokens * nrow
    blocks = hidden // width
    pairs = width // LANES
    scale = HD ** (-0.5)
    part = tokens // CHUNKS
    spans = [slice(i * part, (i + 1) * part) for i in range(CHUNKS)]
    whole = slice(0, tokens)

    barrier = pltpu.get_barrier_semaphore()
    greeted = [net.peer(a, s)[1] for a in ("col", "row", "z") for s in range(1, sizes[a])]
    greeted.append(net.sibling)
    for device in greeted:
        pl.semaphore_signal(barrier, inc=1, device_id=device, device_id_type=MESH)
    mirror = {"row": c, "col": r}

    @pl.when(r != c)
    def _():
        pl.semaphore_signal(barrier, inc=1, device_id=mirror, device_id_type=MESH)

    pl.semaphore_wait(barrier, len(greeted) + jnp.where(r != c, 1, 0))

    def flip_start(source, target):
        copy = net.start(source, target, mirror, begin=False)
        here = pltpu.make_async_copy(source, target, local.at[net.used_local])
        net.used_local += 1

        @pl.when(r != c)
        def _():
            copy.start()

        @pl.when(r == c)
        def _():
            here.start()

        return copy, here

    def flip_wait(pair):
        copy, here = pair

        @pl.when(r != c)
        def _():
            copy.wait()

        @pl.when(r == c)
        def _():
            here.wait()

    class Weight:
        def __init__(self, level, source, store):
            self.level, self.source, self.store = level, source, store

        def begin(self):
            place = self.store.at[self.level, r, core]
            if len(self.source.shape) == 5:
                source = self.source.at[self.level, :, core]
            else:
                source = self.source.at[self.level, core]
            self.copies = [net.bring(source, place)] + net.spread("row", source, place)

        def share(self):
            finish(self.copies)
            place = self.store.at[self.level, :, core]
            self.shared = net.start(place, place, net.sibling)

        def ready(self):
            self.shared.wait()

    class Relayed(Weight):
        def begin(self):
            place = self.store.at[self.level, r, core, z]
            self.own = net.bring(self.source.at[self.level, core], self.store.at[self.level, r, core])
            self.copies = net.spread("row", self.source.at[self.level, core, z], place)

        def relay(self):
            finish(self.copies)
            self.copies = [self.own]
            for step in range(1, nrow):
                i, _ = net.peer("row", step)
                place = self.store.at[self.level, i, core, z]
                self.copies += net.spread("z", place, place)

    class Flipped(Weight):
        def flip(self):
            self.turn = flip_start(
                self.source.at[self.level, core, z], self.store.at[self.level, c, core, z]
            )

        def begin(self):
            place = self.store.at[self.level, r, core, z]
            flip_wait(self.turn)
            self.copies = net.spread("row", place, place)

        def relay(self):
            finish(self.copies)
            place = self.store.at[self.level, :, core, z]
            self.copies = net.spread("z", place, place)

    wqs = [Weight(l, wq_in, wq) for l in range(layers)]
    wos = [Weight(l, wo_in, wo) for l in range(layers)]
    wus = [Relayed(l, wu_in, wu) for l in range(layers)]
    wds = [Flipped(l, wd_in, wd) for l in range(layers)]

    def param(level, index):
        return small[index, level : level + 1, :]

    def any_param(level, index, block):
        return smg[block, index, level : level + 1, :]

    def norm_send(ch, value, store, stats):
        mean = jnp.sum(value, 1, keepdims=True) * (1.0 / width)
        centered = value - mean
        place = store.at[c, spans[ch]]
        place[...] = centered.astype(BF)
        stats[ch, c] = as_rows(mean, jnp.sum(centered * centered, 1, keepdims=True))
        copies = net.spread("col", place, place)
        return copies + net.spread("col", stats.at[ch, c], stats.at[ch, c])

    def norm_apply(level, ch, first, store, stats, inverse, result):
        columns = as_columns(stats[ch].reshape(ncol * 8, part))
        means = [columns[:, 8 * i : 8 * i + 1] for i in range(ncol)]
        mean = sum(means) * (1.0 / ncol)
        spread = sum(columns[:, 8 * i + 1 : 8 * i + 2] for i in range(ncol))
        spread = spread + width * sum((m - mean) * (m - mean) for m in means)
        scaled = lax.rsqrt(spread * (1.0 / full) + EPS)
        inverse[spans[ch]] = jnp.broadcast_to(scaled, (part, LANES))
        for i in range(ncol):
            normed = (store[i, spans[ch]].astype(F32) + (means[i] - mean)) * scaled
            store[i, spans[ch]] = normed.astype(BF)
            result[spans[ch], i * width : (i + 1) * width] = (
                normed * any_param(level, first, i) + any_param(level, first + 1, i)
            ).astype(BF)

    def slots(store, rows):
        return sum(store[i, rows].astype(F32) for i in range(store.shape[0]))

    def one_head(value, side):
        spot = lax.broadcasted_iota(jnp.int32, value.shape, 1)
        return jnp.where((spot < HD) == (side == 0), value.astype(F32), 0.0).astype(BF)

    def pick(values):
        side = lax.broadcasted_iota(jnp.int32, values[0].shape, 1)
        return jnp.where(side < HD, values[0], values[1])

    def attend(level, p, rows):
        lanes = slice(p * LANES, (p + 1) * LANES)
        queries = q[level, rows, lanes]
        keys = kvg[level, :, p, 0].reshape(length, LANES)
        values = kvg[level, :, p, 1].reshape(length, LANES)
        found = []
        for side in range(2):
            scores = mm_nt(one_head(queries, side), keys) * scale
            raised = jnp.exp(scores - jnp.max(scores, 1, keepdims=True))
            share = (raised * (1.0 / jnp.sum(raised, 1, keepdims=True))).astype(BF)
            probs[level, 2 * p + side, rows] = share
            found.append(mm(share, values))
        place = og.at[level, c, p, rows]
        place[...] = pick(found).astype(BF)
        return net.spread("col", place, place)

    def attended(level, i, rows):
        return jnp.concatenate([og[level, i, p, rows] for p in range(pairs)], 1)

    def attend_back(level, p):
        lanes = slice(p * LANES, (p + 1) * LANES)
        queries = q[level, :, lanes]
        upstream = dob[:, lanes]
        keys = kvg[level, :, p, 0].reshape(length, LANES)
        values = kvg[level, :, p, 1].reshape(length, LANES)
        dq, dk, dv = [], [], []
        for side in range(2):
            share = probs[level, 2 * p + side]
            wide = share.astype(F32)
            pulled = mm_nt(one_head(upstream, side), values)
            inner = jnp.sum(wide * pulled, 1, keepdims=True)
            slope = (wide * (pulled - inner)).astype(BF)
            dq.append(mm(slope, keys))
            dk.append(mm_tn(slope, queries))
            dv.append(mm_tn(share, upstream))
        jg[:, lanes] = (pick(dq) * scale).astype(BF)
        kvsend[p, :, 0] = (pick(dk) * scale).astype(BF).reshape(nrow, tokens, LANES)
        kvsend[p, :, 1] = pick(dv).astype(BF).reshape(nrow, tokens, LANES)
        for j in range(2):
            kvrecv[level, p, r, j] = kvsend[p, r, j]

    smg[c, :, 0:layers] = small[...]
    wqs[0].begin()
    ahead = net.spread("col", smg.at[c], smg.at[c])
    arriving = []
    for ch in range(CHUNKS):
        value = x_in[spans[ch]]
        x_out[spans[ch]] = value
        arriving.append(norm_send(ch, value, xg.at[0], st1.at[0]))
    for level in range(layers):
        more = level + 1 < layers
        if level == 0:
            wos[0].begin()
            wus[0].begin()
            wds[0].flip()
            finish(ahead)
        travelling = []
        for ch in range(CHUNKS):
            finish(arriving[ch])
            rows = spans[ch]
            norm_apply(level, ch, 0, xg.at[level], st1.at[level], inv1.at[level], h.at[level])
            if ch == 0:
                if level == 0:
                    wqs[0].share()
                    wds[0].begin()
                wqs[level].ready()

            def project(j):
                return mm(h[level, rows], wq[level, :, :, j].reshape(full, width))

            keys = project(1).astype(BF)
            values = (project(2) + param(level, 2)).astype(BF)
            for p in range(pairs):
                lanes = slice(p * LANES, (p + 1) * LANES)
                kvg[level, r, p, 0, rows] = keys[:, lanes]
                kvg[level, r, p, 1, rows] = values[:, lanes]
                place = kvg.at[level, r, p, :, rows]
                travelling.append(net.spread("row", place, place))
            q[level, rows] = (project(0) + qbias[level : level + 1, :]).astype(BF)
        wus[level].relay()
        wds[level].relay()
        if level == 0:
            wos[0].share()
        for ch in range(CHUNKS):
            finish(travelling[ch * pairs])
        early = [attend(level, 0, whole)]
        for p in range(1, pairs):
            for ch in range(CHUNKS):
                finish(travelling[ch * pairs + p])
        late = [[attend(level, p, spans[ch]) for p in range(1, pairs)] for ch in range(CHUNKS)]
        wus[level].share()
        if more:
            wqs[level + 1].begin()
            wos[level + 1].begin()
            wus[level + 1].begin()
            wds[level + 1].flip()
        finish(early[0])
        arriving = []
        for ch in range(CHUNKS):
            rows = spans[ch]
            for copies in late[ch]:
                finish(copies)
            if ch == 0:
                wos[level].ready()
            branch = param(level, 3)
            for i in range(ncol):
                branch = branch + mm(attended(level, i, rows), wo[level, i].reshape(width, width))
            abr[level, rows] = branch
            middle = x_out[rows] + param(level, 4) * branch
            x_out[rows] = middle
            arriving.append(norm_send(ch, middle, xg2.at[level], st2.at[level]))
        wds[level].share()
        if more:
            wds[level + 1].begin()
        travelling = []
        for ch in range(CHUNKS):
            rows = spans[ch]
            finish(arriving[ch])
            norm_apply(level, ch, 5, xg2.at[level], st2.at[level], inv2.at[level], h2.at[level])
            if ch == 0:
                wus[level].ready()

            def widen_step(j, carry):
                lanes = pl.ds(pl.multiple_of(j * width, width), width)
                pre = mm(h2[level, rows], wu[level, :, :, :, :, lanes].reshape(full, width))
                pre = pre + ubias[level : level + 1, lanes]
                below = 0.5 * (1.0 + lax.erf(pre * (0.5**0.5)))
                zz[level, rows, lanes] = (pre * below).astype(BF)
                bell = jnp.exp(-0.5 * pre * pre) * (0.5 / jnp.pi) ** 0.5
                gp[level, rows, lanes] = (below + pre * bell).astype(BF)
                return carry

            lax.fori_loop(0, blocks, widen_step, 0)
            if ch == 0:
                wds[level].ready()
            copies = []
            for step in range(1, ncol + 1):
                i, device = net.peer("col", step)
                piece = mm(zz[level, rows], wd[level, i].reshape(hidden, width)).astype(BF)
                if step < ncol:
                    msend[i, rows] = piece
                    copies.append(net.start(msend.at[i, rows], mrecv.at[level, c, rows], device))
                else:
                    mrecv[level, c, rows] = piece
            travelling.append(copies)
        if more:
            wqs[level + 1].share()
            wos[level + 1].share()
        arriving = []
        for ch in range(CHUNKS):
            rows = spans[ch]
            finish(travelling[ch])
            branch = slots(mrecv.at[level], rows) + param(level, 7)
            mbr[level, rows] = branch
            value = x_out[rows] + param(level, 8) * branch
            x_out[rows] = value
            if more:
                arriving.append(norm_send(ch, value, xg.at[level + 1], st1.at[level + 1]))

    sums[...] = jnp.zeros_like(sums)
    per = 9 + 1 + blocks

    def keep(level, index, value):
        sums[level * per + index : level * per + index + 1, :] += jnp.sum(value, 0, keepdims=True)

    def norm_back_send(level, ch, part_of, gain, normed, store, stats):
        rows = spans[ch]
        copies, first, second = [], 0.0, 0.0
        for step in range(1, ncol + 1):
            i, device = net.peer("col", step)
            value = part_of(i)
            scaled = value * any_param(level, gain, i)
            first = first + jnp.sum(scaled, 1, keepdims=True)
            second = second + jnp.sum(scaled * normed[i, rows].astype(F32), 1, keepdims=True)
            if step < ncol:
                hsend[i, rows] = value.astype(BF)
                copies.append(net.start(hsend.at[i, rows], store.at[c, rows], device))
            else:
                store[c, rows] = value.astype(BF)
        stats[ch, c] = as_rows(first, second)
        return copies + net.spread("col", stats.at[ch, c], stats.at[ch, c])

    def norm_back(level, ch, gain, normed, inverse, store, stats):
        rows = spans[ch]
        upstream = slots(store, rows)
        normed = normed[c, rows].astype(F32)
        keep(level, gain, upstream * normed)
        keep(level, gain + 1, upstream)
        columns = as_columns(sum(stats[ch, i] for i in range(ncol)))
        scaled = upstream * param(level, gain)
        shift = columns[:, 0:1] * (1.0 / full) + normed * (columns[:, 1:2] * (1.0 / full))
        return inverse[rows, 0:1] * (scaled - shift)

    pieces = 2 * nz
    part_out, part_up = width // pieces, hidden // pieces

    def put_rows(store, i, start, value):
        rows = value.shape[0] // pieces
        for piece in range(pieces):
            store[piece % 2, i, piece // 2, start : start + rows, :] = value[piece * rows : (piece + 1) * rows]

    def grads_down_up(level):
        def step(i, carry):
            put_rows(bulk[0], i, part_out + part_up, mm_tn(zz[level], dmg[level, i]).astype(BF))
            lanes = pl.ds(pl.multiple_of(i * width, width), width)
            up = mm_tn(h2[level, :, lanes], dur[...]).astype(BF)
            up = [up[:, j * width : (j + 1) * width] for j in range(blocks)]
            put_rows(bulk[0], i, part_out, jnp.concatenate(up, 0))
            return carry

        lax.fori_loop(0, nrow, step, 0)

    def grads_out(level, low):
        def step(i, carry):
            put_rows(bulk[0], i, 0, mm_tn(attended(level, i, whole), low[...]).astype(BF))
            return carry

        lax.fori_loop(0, nrow, step, 0)

    def grads_qkv(level):
        def step(i, carry):
            lanes = pl.ds(pl.multiple_of(i * width, width), width)
            value = mm_tn(h[level, :, lanes], jg[...]).astype(BF)
            for j in range(3):
                put_rows(tail[0], i, j * part_out, value[:, j * width : (j + 1) * width])
            return carry

        lax.fori_loop(0, nrow, step, 0)

    def reduce_steps(level, store, flipping):
        grad, crecv, ra, rb, ta, tb, ua, ub, fin, flipped, land = store
        rows = grad.shape[3]
        upper = rows // 2
        top, low = pl.ds(0, upper), pl.ds(upper, upper)
        copy = net.start(grad.at[1 - core], crecv, net.sibling)
        yield
        copy.wait()

        def add(i, carry):
            for j in range(nz):
                total = grad[core, i, j].astype(F32) + crecv[i, j].astype(F32)
                grad[core, i, j] = total.astype(BF)
            return carry

        lax.fori_loop(0, nrow, add, 0)
        copies = net.deal("row", lambda i: grad.at[core, i, :, top], ra.at[r])
        copies += net.deal("z", lambda i: grad.at[core, :, i, low], rb.at[z])
        yield
        finish(copies)

        def add_top(j, carry):
            total = grad[core, r, j, 0:upper].astype(F32)
            for step in range(1, nrow):
                total = total + ra[net.peer("row", step)[0], j].astype(F32)
            ta[j] = total.astype(BF)
            return carry

        def add_low(j, carry):
            total = grad[core, j, z, upper:].astype(F32)
            for step in range(1, nz):
                total = total + rb[net.peer("z", step)[0], j].astype(F32)
            tb[j] = total.astype(BF)
            return carry

        lax.fori_loop(0, nz, add_top, 0)
        lax.fori_loop(0, nrow, add_low, 0)
        copies = net.deal("z", lambda i: ta.at[i], ua.at[level, z])
        copies += net.deal("row", lambda i: tb.at[i], ub.at[level, r])
        yield
        finish(copies)
        total = ta[z].astype(F32)
        for step in range(1, nz):
            total = total + ua[level, net.peer("z", step)[0]].astype(F32)
        fin[level, 0:upper] = total.astype(BF)
        total = tb[r].astype(F32)
        for step in range(1, nrow):
            total = total + ub[level, net.peer("row", step)[0]].astype(F32)
        fin[level, upper:] = total.astype(BF)
        straight = rows - (part_up if flipping else 0)
        if flipping:
            turn = flip_start(fin.at[level, pl.ds(straight, part_up)], flipped.at[level])
            yield
            flip_wait(turn)
            land[core, z, straight:] = flipped[level]
        land[core, z, 0:straight] = fin[level, 0:straight]
        copies = net.spread("z", land.at[core, z], land.at[core, z])
        yield
        finish(copies)
        copy = net.start(land.at[core], land.at[core], net.sibling)
        yield
        copy.wait()
        for piece in range(pieces):
            found = land[piece % 2, piece // 2]
            some = slice(piece * part_out, (piece + 1) * part_out)
            if flipping:
                gout[level, some] = found[0:part_out]
                block, inner = divmod(piece * part_up, width)
                gup[level, inner : inner + part_up, block * width : (block + 1) * width] = found[
                    part_out : part_out + part_up
                ]
                gdown[level, piece * part_up : (piece + 1) * part_up] = found[part_out + part_up :]
            else:
                for j in range(3):
                    gq[level, j, some] = found[j * part_out : (j + 1) * part_out]
        yield

    heavy, light = [], []

    def advance(queue):
        for steps in queue:
            next(steps, None)

    def branch_back(level, ch, upstream):
        rows = spans[ch]
        g_out[rows] = upstream
        if level < 0:
            return []
        keep(level, 8, upstream * mbr[level, rows])
        scaled = upstream * param(level, 8)
        keep(level, 7, scaled)
        place = dmg.at[level, c, rows]
        place[...] = scaled.astype(BF)
        return net.spread("col", place, place)

    arriving = [branch_back(layers - 1, ch, cot[spans[ch]]) for ch in range(CHUNKS)]
    for level in reversed(range(layers)):
        advance(heavy)
        advance(light)
        travelling = []
        for ch in range(CHUNKS):
            rows = spans[ch]
            finish(arriving[ch])

            def dz_step(j, carry):
                lanes = pl.ds(pl.multiple_of(j * width, width), width)
                per_half = blocks // 2
                group = width // part_up
                value = 0.0
                for i in range(ncol):
                    weight = wd[level, i, j // per_half, pl.ds((j % per_half) * group, group)]
                    value = value + mm_nt(dmg[level, i, rows], weight.reshape(width, width))
                value = value * gp[level, rows, lanes].astype(F32)
                dur[rows, lanes] = value.astype(BF)
                return carry

            lax.fori_loop(0, blocks, dz_step, 0)
            travelling.append(
                norm_back_send(
                    level, ch, lambda i: mm_nt(dur[rows], wu[level, i].reshape(width, hidden)),
                    5, xg2.at[level], hrecv2.at[level], bst2.at[level],
                )
            )
        for j in range(blocks):
            keep(level, 10 + j, dur[:, j * width : (j + 1) * width].astype(F32))
        advance(heavy)
        advance(light)
        grads_down_up(level)
        arriving = []
        for ch in range(CHUNKS):
            rows = spans[ch]
            finish(travelling[ch])
            middle = g_out[rows] + norm_back(
                level, ch, 5, xg2.at[level], inv2.at[level], hrecv2.at[level], bst2.at[level]
            )
            g_out[rows] = middle
            keep(level, 4, middle * abr[level, rows])
            scaled = middle * param(level, 4)
            keep(level, 3, scaled)
            dob[rows] = scaled.astype(BF)
            copies = []
            for step in range(1, ncol + 1):
                i, device = net.peer("col", step)
                piece = mm_nt(dob[rows], wo[level, i].reshape(width, width)).astype(BF)
                if step < ncol:
                    osend[i, rows] = piece
                    copies.append(net.start(osend.at[i, rows], orecv.at[level, c, rows], device))
                else:
                    orecv[level, c, rows] = piece
            arriving.append(copies)
        advance(heavy)
        advance(light)
        grads_out(level, dob)
        heavy.append(reduce_steps(level, bulk, True))
        advance(heavy[-1:])
        for ch in range(CHUNKS):
            finish(arriving[ch])
            dob[spans[ch]] = slots(orecv.at[level], spans[ch]).astype(BF)
        early, late = [], [[] for _ in range(CHUNKS)]
        for p in range(pairs):
            attend_back(level, p)
            if p + 1 < pairs:
                early += net.deal("row", lambda i: kvsend.at[p, i], kvrecv.at[level, p, r])
            else:
                for ch in range(CHUNKS):
                    late[ch] = net.deal(
                        "row", lambda i: kvsend.at[p, i, :, spans[ch]], kvrecv.at[level, p, r, :, spans[ch]]
                    )
        advance(heavy)
        advance(light)
        finish(early)
        travelling = []
        for ch in range(CHUNKS):
            rows = spans[ch]
            finish(late[ch])
            for p in range(pairs):
                for j in range(2):
                    total = sum(kvrecv[level, p, i, j, rows].astype(F32) for i in range(nrow))
                    start = (j + 1) * width + p * LANES
                    jg[rows, start : start + LANES] = total.astype(BF)

            def dh_part(i):
                return sum(
                    mm_nt(jg[rows, j * width : (j + 1) * width], wq[level, i, :, j].reshape(width, width))
                    for j in range(3)
                )

            travelling.append(
                norm_back_send(
                    level, ch, dh_part, 0, xg.at[level], hrecv1.at[level], bst1.at[level]
                )
            )
        keep(level, 9, jg[:, 0:width].astype(F32))
        keep(level, 2, jg[:, 2 * width :].astype(F32))
        advance(light)
        grads_qkv(level)
        light.append(reduce_steps(level, tail, False))
        advance(light[-1:])
        advance(heavy)
        arriving = []
        for ch in range(CHUNKS):
            finish(travelling[ch])
            upstream = g_out[spans[ch]] + norm_back(
                level, ch, 0, xg.at[level], inv1.at[level], hrecv1.at[level], bst1.at[level]
            )
            arriving.append(branch_back(level - 1, ch, upstream))

    sharing = net.start(sums, sumc, net.sibling)
    advance(light)
    advance(heavy)
    sharing.wait()
    sumy[r] = sums[...] + sumc[...]
    copies = net.spread("row", sumy.at[r], sumy.at[r])
    advance(light)
    advance(heavy)
    finish(copies)
    sumz[z] = sumy[0] + sumy[1] + sumy[2] + sumy[3]
    copies = net.spread("z", sumz.at[z], sumz.at[z])
    advance(light)
    advance(heavy)
    finish(copies)
    total = sumz[0] + sumz[1] + sumz[2] + sumz[3]
    for level in range(layers):
        start = level * per
        for i in range(9):
            small_out[i, level : level + 1, :] = total[start + i : start + i + 1]
        qbias_out[level : level + 1, :] = total[start + 9 : start + 10]
        for j in range(blocks):
            ubias_out[level : level + 1, j * width : (j + 1) * width] = total[start + 10 + j : start + 11 + j]
    for steps in light + heavy:
        for _ in steps:
            pass


def shards(sizes, inputs, w_qkv, w_out, w_up, w_down, small_params, query_bias, up_bias, cotangent):
    tokens, width = inputs.shape
    layers, _, hidden = w_up.shape
    ncol, nrow, nz = sizes["col"], sizes["row"], sizes["z"]
    full, half = width * ncol, width // 2
    blocks = hidden // width
    rows = -(-layers * (10 + blocks) // 8) * 8
    bulk, tail = (width + 2 * hidden) // (2 * nz), 3 * width // (2 * nz)
    vmem = lambda shape, dtype=BF: pltpu.VMEM(shape, dtype)
    scratch = [
        vmem((layers, nrow, 2, 3, half, width)),
        vmem((layers, nrow, 2, half, width)),
        vmem((layers, nrow, 2, nz, half // nz, hidden)),
        vmem((layers, nrow, 2, nz, hidden // (2 * nz), width)),
        vmem((ncol, 9, 8, width), F32),
        vmem((layers, ncol, tokens, width)),
        vmem((layers, CHUNKS, ncol, 8, tokens // CHUNKS), F32),
        vmem((layers, tokens, full)),
        vmem((layers, tokens, width)),
        vmem((layers, nrow, width // LANES, 2, tokens, LANES)),
        vmem((layers, width // HD, tokens, tokens * nrow)),
        vmem((layers, ncol, width // LANES, tokens, LANES)),
        vmem((layers, tokens, width), F32),
        vmem((layers, ncol, tokens, width)),
        vmem((layers, CHUNKS, ncol, 8, tokens // CHUNKS), F32),
        vmem((layers, tokens, full)),
        vmem((layers, tokens, hidden)),
        vmem((layers, tokens, hidden)),
        vmem((layers, tokens, width), F32),
        vmem((layers, tokens, LANES), F32),
        vmem((layers, tokens, LANES), F32),
        vmem((ncol, tokens, width)),
        vmem((layers, ncol, tokens, width)),
        vmem((layers, ncol, tokens, width)),
        vmem((tokens, hidden)),
        vmem((ncol, tokens, width)),
        vmem((layers, ncol, tokens, width)),
        vmem((layers, CHUNKS, ncol, 8, tokens // CHUNKS), F32),
        vmem((ncol, tokens, width)),
        vmem((layers, ncol, tokens, width)),
        vmem((tokens, width)),
        vmem((width // LANES, nrow, 2, tokens, LANES)),
        vmem((layers, width // LANES, nrow, 2, tokens, LANES)),
        vmem((tokens, 3 * width)),
        vmem((layers, ncol, tokens, width)),
        vmem((layers, CHUNKS, ncol, 8, tokens // CHUNKS), F32),
        vmem((rows, width), F32),
        vmem((rows, width), F32),
        vmem((nrow, rows, width), F32),
        vmem((nz, rows, width), F32),
    ]
    for piece in (bulk, tail):
        scratch += [
            vmem((2, nrow, nz, piece, width)),
            vmem((nrow, nz, piece, width)),
            vmem((nrow, nz, piece // 2, width)),
            vmem((nz, nrow, piece // 2, width)),
            vmem((nz, piece // 2, width)),
            vmem((nrow, piece // 2, width)),
            vmem((layers, nz, piece // 2, width)),
            vmem((layers, nrow, piece // 2, width)),
            vmem((layers, piece, width)),
            vmem((layers, hidden // (2 * nz), width)),
            vmem((2, nz, piece, width)),
        ]
    scratch += [
        pltpu.SemaphoreType.DMA((384,)),
        pltpu.SemaphoreType.DMA((384,)),
        pltpu.SemaphoreType.DMA((16,)),
    ]
    here = pl.BlockSpec(memory_space=pltpu.VMEM)
    far = pl.BlockSpec(memory_space=pl.ANY)
    output, input_grad, qkv, out, up, down, small, query, hidden_bias = pl.pallas_call(
        partial(body, sizes, layers),
        out_shape=(
            jax.ShapeDtypeStruct((tokens, width), F32),
            jax.ShapeDtypeStruct((tokens, width), F32),
            jax.ShapeDtypeStruct((layers, 3, width, width), BF),
            jax.ShapeDtypeStruct((layers, width, width), BF),
            jax.ShapeDtypeStruct((layers, width, hidden), BF),
            jax.ShapeDtypeStruct((layers, hidden, width), BF),
            jax.ShapeDtypeStruct((9, layers, width), F32),
            jax.ShapeDtypeStruct((layers, width), F32),
            jax.ShapeDtypeStruct((layers, hidden), F32),
        ),
        in_specs=[here] * 5 + [far] * 4,
        out_specs=(here,) * 9,
        scratch_shapes=scratch,
        compiler_params=pltpu.CompilerParams(
            collective_id=0, has_side_effects=True, vmem_limit_bytes=63 << 20
        ),
        name="encoder",
    )(
        inputs,
        cotangent,
        jnp.swapaxes(small_params, 0, 1),
        query_bias,
        up_bias,
        jnp.swapaxes(w_qkv, 1, 2).reshape(layers, 3, 2, half, width),
        w_out.reshape(layers, 2, half, width),
        w_up.reshape(layers, 2, nz, half // nz, hidden),
        w_down.reshape(layers, 2, nz, hidden // (2 * nz), width),
    )
    return (
        output,
        input_grad,
        jnp.swapaxes(qkv, 1, 2).astype(F32),
        out.astype(F32),
        up.astype(F32),
        down.astype(F32),
        jnp.swapaxes(small, 0, 1),
        query,
        hidden_bias,
    )


def solution(mesh):
    sizes = {"col": mesh.shape["col"], "row": mesh.shape["row"], "z": mesh.shape["dp"] // 2}
    placed = (
        P(("dp", "row"), "col"),
        P(None, "row", None, "col"),
        P(None, "row", "col"),
        P(None, "row", "col"),
        P(None, "row", "col"),
        P(None, None, "col"),
        P(None, "col"),
        P(None, "col"),
        P(("dp", "row"), "col"),
    )
    return jax.shard_map(
        partial(shards, sizes),
        mesh=mesh,
        in_specs=placed,
        out_specs=(
            P(("dp", "row"), "col"),
            P(("dp", "row"), "col"),
            P(None, "row", None, "col"),
            P(None, "row", "col"),
            P(None, "row", "col"),
            P(None, "row", "col"),
            P(None, None, "col"),
            P(None, "col"),
            P(None, "col"),
        ),
        check_vma=False,
    )
```

```python
from functools import partial

import jax
import jax.numpy as jnp
from jax import lax
from jax.experimental import pallas as pl
from jax.experimental.pallas import tpu as pltpu
from jax.sharding import PartitionSpec as P

HD = 64
EPS = 1e-06
LANES = 128
CHUNKS = 2
UNROLL = True
BF = jnp.bfloat16
F32 = jnp.float32
MESH = pl.DeviceIdType.MESH


def mm(left, right):
    return jnp.dot(left, right, preferred_element_type=F32)


def mm_nt(left, right):
    return lax.dot_general(left, right, (((1,), (1,)), ((), ())), preferred_element_type=F32)


def mm_tn(left, right):
    return lax.dot_general(left, right, (((0,), (0,)), ((), ())), preferred_element_type=F32)


class Links:
    def __init__(self, sizes, send, recv, local):
        self.sizes = sizes
        self.send, self.recv, self.local = send, recv, local
        self.used = 0
        self.used_local = 0
        self.col = lax.axis_index("col")
        self.row = lax.axis_index("row")
        place = lax.axis_index("dp")
        self.z = place // 2
        self.core = place % 2
        self.sibling = {"dp": self.z * 2 + (1 - self.core)}

    def peer(self, axis, step):
        if axis == "z":
            index = lax.rem(self.z + step, self.sizes["z"])
            return index, {"dp": index * 2 + self.core}
        index = lax.rem(getattr(self, axis) + step, self.sizes[axis])
        return index, {axis: index}

    def start(self, source, target, device, begin=True):
        copy = pltpu.make_async_remote_copy(
            src_ref=source,
            dst_ref=target,
            send_sem=self.send.at[self.used],
            recv_sem=self.recv.at[self.used],
            device_id=device,
            device_id_type=MESH,
        )
        self.used += 1
        if begin:
            copy.start()
        return copy

    def bring(self, source, target):
        copy = pltpu.make_async_copy(source, target, self.local.at[self.used_local])
        self.used_local += 1
        copy.start()
        return copy

    def spread(self, axis, source, target):
        return [
            self.start(source, target, self.peer(axis, step)[1])
            for step in range(1, self.sizes[axis])
        ]

    def deal(self, axis, source_of, target):
        copies = []
        for step in range(1, self.sizes[axis]):
            index, device = self.peer(axis, step)
            copies.append(self.start(source_of(index), target, device))
        return copies


def finish(copies):
    for copy in copies:
        copy.wait()


def as_rows(first, second):
    tokens = first.shape[0]
    lane = lax.broadcasted_iota(jnp.int32, (tokens, LANES), 1)
    both = jnp.where(lane == 0, first, jnp.where(lane == 1, second, 0.0))
    return both.T[:8]


def as_columns(rows):
    count, tokens = rows.shape
    return jnp.concatenate([rows, jnp.zeros((LANES - count, tokens), F32)], 0).T


def body(sizes, layers, *refs):
    (
        x_in, cot, small, qbias, ubias, wq_in, wo_in, wu_in, wd_in,
        x_out, g_out, gq, gout, gup, gdown, small_out, qbias_out, ubias_out,
        wq, wo, wu, wd, smg, xg, st1, h, q, kvg, probs, og, abr, xg2, st2, h2, gp, zz, mbr,
        inv1, inv2, msend, mrecv, dmg, dur, hsend, hrecv2, bst2, osend, orecv, dob, kvsend, kvrecv,
        jg, hrecv1, bst1, sums, sumc, sumy, sumz, *chunk_refs, send, recv, local,
    ) = refs
    bulk, tail = chunk_refs[: len(chunk_refs) // 2], chunk_refs[len(chunk_refs) // 2 :]
    net = Links(sizes, send, recv, local)
    c, r, z, core = net.col, net.row, net.z, net.core
    ncol, nrow, nz = sizes["col"], sizes["row"], sizes["z"]
    tokens, width = x_in.shape
    hidden = ubias.shape[1]
    full = width * ncol
    length = tokens * nrow
    blocks = hidden // width
    pairs = width // LANES
    scale = HD ** (-0.5)
    part = tokens // CHUNKS
    spans = [slice(i * part, (i + 1) * part) for i in range(CHUNKS)]
    whole = slice(0, tokens)

    barrier = pltpu.get_barrier_semaphore()
    greeted = [net.peer(a, s)[1] for a in ("col", "row", "z") for s in range(1, sizes[a])]
    greeted.append(net.sibling)
    for device in greeted:
        pl.semaphore_signal(barrier, inc=1, device_id=device, device_id_type=MESH)
    mirror = {"row": c, "col": r}

    @pl.when(r != c)
    def _():
        pl.semaphore_signal(barrier, inc=1, device_id=mirror, device_id_type=MESH)

    pl.semaphore_wait(barrier, len(greeted) + jnp.where(r != c, 1, 0))

    def flip_start(source, target):
        copy = net.start(source, target, mirror, begin=False)
        here = pltpu.make_async_copy(source, target, local.at[net.used_local])
        net.used_local += 1

        @pl.when(r != c)
        def _():
            copy.start()

        @pl.when(r == c)
        def _():
            here.start()

        return copy, here

    def flip_wait(pair):
        copy, here = pair

        @pl.when(r != c)
        def _():
            copy.wait()

        @pl.when(r == c)
        def _():
            here.wait()

    class Weight:
        def __init__(self, level, source, store):
            self.level, self.source, self.store = level, source, store

        def split(self, place):
            if len(place.shape) == 3:
                return [place.at[pl.ds(1, 2)], place.at[pl.ds(0, 1)]]
            return [place]

        def begin(self):
            place = self.store.at[self.level, r, core]
            if len(self.source.shape) == 5:
                source = self.source.at[self.level, :, core]
            else:
                source = self.source.at[self.level, core]
            self.queue = [
                [net.bring(a, b)] + net.spread("row", a, b)
                for a, b in zip(self.split(source), self.split(place))
            ]
            self.shared, self.taken = [], 0

        def share(self):
            finish(self.queue.pop(0))
            place = self.store.at[self.level, :, core]
            if len(place.shape) == 4 and place.shape[1] == 3:
                first, count = (0, 1) if self.shared else (1, 2)
                place = place.at[:, pl.ds(first, count)]
            self.shared.append(net.start(place, place, net.sibling))

        def ready(self):
            self.shared[self.taken].wait()
            self.taken += 1

    class Relayed(Weight):
        def begin(self):
            place = self.store.at[self.level, r, core, z]
            self.own = net.bring(self.source.at[self.level, core], self.store.at[self.level, r, core])
            self.copies = net.spread("row", self.source.at[self.level, core, z], place)
            self.shared, self.taken = [], 0

        def relay(self):
            finish(self.copies)
            copies = [self.own]
            for step in range(1, nrow):
                i, _ = net.peer("row", step)
                place = self.store.at[self.level, i, core, z]
                copies += net.spread("z", place, place)
            self.queue = [copies]

    class Flipped(Weight):
        def flip(self):
            self.turn = flip_start(
                self.source.at[self.level, core, z], self.store.at[self.level, c, core, z]
            )

        def begin(self):
            place = self.store.at[self.level, r, core, z]
            flip_wait(self.turn)
            self.copies = net.spread("row", place, place)
            self.shared, self.taken = [], 0

        def relay(self):
            finish(self.copies)
            place = self.store.at[self.level, :, core, z]
            self.queue = [net.spread("z", place, place)]

    wqs = [Weight(l, wq_in, wq) for l in range(layers)]
    wos = [Weight(l, wo_in, wo) for l in range(layers)]
    wus = [Relayed(l, wu_in, wu) for l in range(layers)]
    wds = [Flipped(l, wd_in, wd) for l in range(layers)]

    def param(level, index):
        return small[index, level : level + 1, :]

    def any_param(level, index, block):
        return smg[block, index, level : level + 1, :]

    def norm_send(ch, value, store, stats):
        mean = jnp.sum(value, 1, keepdims=True) * (1.0 / width)
        centered = value - mean
        place = store.at[c, spans[ch]]
        place[...] = centered.astype(BF)
        stats[ch, c] = as_rows(mean, jnp.sum(centered * centered, 1, keepdims=True))
        copies = net.spread("col", place, place)
        return copies + net.spread("col", stats.at[ch, c], stats.at[ch, c])

    def norm_apply(level, ch, first, store, stats, inverse, result):
        columns = as_columns(stats[ch].reshape(ncol * 8, part))
        means = [columns[:, 8 * i : 8 * i + 1] for i in range(ncol)]
        mean = sum(means) * (1.0 / ncol)
        spread = sum(columns[:, 8 * i + 1 : 8 * i + 2] for i in range(ncol))
        spread = spread + width * sum((m - mean) * (m - mean) for m in means)
        scaled = lax.rsqrt(spread * (1.0 / full) + EPS)
        inverse[spans[ch]] = jnp.broadcast_to(scaled, (part, LANES))
        for i in range(ncol):
            normed = (store[i, spans[ch]].astype(F32) + (means[i] - mean)) * scaled
            store[i, spans[ch]] = normed.astype(BF)
            result[spans[ch], i * width : (i + 1) * width] = (
                normed * any_param(level, first, i) + any_param(level, first + 1, i)
            ).astype(BF)

    def slots(store, rows):
        return sum(store[i, rows].astype(F32) for i in range(store.shape[0]))

    def one_head(value, side):
        spot = lax.broadcasted_iota(jnp.int32, value.shape, 1)
        return jnp.where((spot < HD) == (side == 0), value.astype(F32), 0.0).astype(BF)

    def pick(values):
        side = lax.broadcasted_iota(jnp.int32, values[0].shape, 1)
        return jnp.where(side < HD, values[0], values[1])

    def attend(level, p, rows):
        lanes = slice(p * LANES, (p + 1) * LANES)
        queries = q[level, rows, lanes]
        keys = kvg[level, :, p, 0].reshape(length, LANES)
        values = kvg[level, :, p, 1].reshape(length, LANES)
        found = []
        for side in range(2):
            scores = mm_nt(one_head(queries, side), keys) * scale
            raised = jnp.exp(scores - jnp.max(scores, 1, keepdims=True))
            share = (raised * (1.0 / jnp.sum(raised, 1, keepdims=True))).astype(BF)
            probs[level, 2 * p + side, rows] = share
            found.append(mm(share, values))
        place = og.at[level, c, p, rows]
        place[...] = pick(found).astype(BF)
        return net.spread("col", place, place)

    def attended(level, i, rows):
        return jnp.concatenate([og[level, i, p, rows] for p in range(pairs)], 1)

    def attend_back(level, p):
        lanes = slice(p * LANES, (p + 1) * LANES)
        queries = q[level, :, lanes]
        upstream = dob[:, lanes]
        keys = kvg[level, :, p, 0].reshape(length, LANES)
        values = kvg[level, :, p, 1].reshape(length, LANES)
        dq, dk, dv = [], [], []
        for side in range(2):
            share = probs[level, 2 * p + side]
            wide = share.astype(F32)
            pulled = mm_nt(one_head(upstream, side), values)
            inner = jnp.sum(wide * pulled, 1, keepdims=True)
            slope = (wide * (pulled - inner)).astype(BF)
            dq.append(mm(slope, keys))
            dk.append(mm_tn(slope, queries))
            dv.append(mm_tn(share, upstream))
        jg[:, lanes] = (pick(dq) * scale).astype(BF)
        kvsend[p, :, 0] = (pick(dk) * scale).astype(BF).reshape(nrow, tokens, LANES)
        kvsend[p, :, 1] = pick(dv).astype(BF).reshape(nrow, tokens, LANES)
        for j in range(2):
            kvrecv[level, p, r, j] = kvsend[p, r, j]

    def down_send(level, rows):
        copies = []
        for step in range(1, ncol + 1):
            i, device = net.peer("col", step)
            piece = mm(zz[level, rows], wd[level, i].reshape(hidden, width)).astype(BF)
            if step < ncol:
                msend[i, rows] = piece
                copies.append(net.start(msend.at[i, rows], mrecv.at[level, c, rows], device))
            else:
                mrecv[level, c, rows] = piece
        return copies

    def down_take(level, rows):
        branch = slots(mrecv.at[level], rows) + param(level, 7)
        mbr[level, rows] = branch
        value = x_out[rows] + param(level, 8) * branch
        x_out[rows] = value
        return value

    sums[...] = jnp.zeros_like(sums)
    per = 9 + 1 + blocks

    def keep(level, index, value):
        sums[level * per + index : level * per + index + 1, :] += jnp.sum(value, 0, keepdims=True)

    def branch_back(level, ch, upstream):
        rows = spans[ch]
        g_out[rows] = upstream
        if level < 0:
            return []
        if level + 1 < layers:
            keep(level, 8, upstream * mbr[level, rows])
        scaled = upstream * param(level, 8)
        keep(level, 7, scaled)
        place = dmg.at[level, c, rows]
        place[...] = scaled.astype(BF)
        return net.spread("col", place, place)

    smg[c, :, 0:layers] = small[...]
    wqs[0].begin()
    ahead = net.spread("col", smg.at[c], smg.at[c])
    arriving = []
    for ch in range(CHUNKS):
        value = x_in[spans[ch]]
        x_out[spans[ch]] = value
        arriving.append(norm_send(ch, value, xg.at[0], st1.at[0]))
    for level in range(layers):
        more = level + 1 < layers
        if level == 0:
            wos[0].begin()
            wus[0].begin()
            wds[0].flip()
            finish(ahead)
        travelling = []
        for ch in range(CHUNKS):
            finish(arriving[ch])
            rows = spans[ch]
            norm_apply(level, ch, 0, xg.at[level], st1.at[level], inv1.at[level], h.at[level])
            if ch == 0:
                if level == 0:
                    wqs[0].share()
                    wds[0].begin()
                wqs[level].ready()
                if level == 0:
                    wqs[0].share()

            def project(j):
                return mm(h[level, rows], wq[level, :, :, j].reshape(full, width))

            keys = project(1).astype(BF)
            values = (project(2) + param(level, 2)).astype(BF)
            for p in range(pairs):
                lanes = slice(p * LANES, (p + 1) * LANES)
                kvg[level, r, p, 0, rows] = keys[:, lanes]
                kvg[level, r, p, 1, rows] = values[:, lanes]
                place = kvg.at[level, r, p, :, rows]
                if p == 0:
                    travelling.append(net.spread("row", place, place))
        for p in range(1, pairs):
            place = kvg.at[level, r, p]
            travelling.append(net.spread("row", place, place))
        wqs[level].ready()
        q[level] = (
            mm(h[level], wq[level, :, :, 0].reshape(full, width)) + qbias[level : level + 1, :]
        ).astype(BF)
        wus[level].relay()
        wds[level].relay()
        if level == 0:
            wos[0].share()
        if not more:
            above = [branch_back(level, ch, cot[spans[ch]]) for ch in range(CHUNKS)]
        for ch in range(CHUNKS):
            finish(travelling[ch])
        early = [attend(level, 0, whole)]
        for p in range(1, pairs):
            finish(travelling[CHUNKS + p - 1])
        late = [[attend(level, p, spans[ch]) for p in range(1, pairs)] for ch in range(CHUNKS)]
        wus[level].share()
        if more:
            wqs[level + 1].begin()
            wos[level + 1].begin()
            wus[level + 1].begin()
            wds[level + 1].flip()
        finish(early[0])
        arriving = []
        for ch in range(CHUNKS):
            rows = spans[ch]
            for copies in late[ch]:
                finish(copies)
            if ch == 0:
                wos[level].ready()
            branch = param(level, 3)
            for i in range(ncol):
                branch = branch + mm(attended(level, i, rows), wo[level, i].reshape(width, width))
            abr[level, rows] = branch
            middle = x_out[rows] + param(level, 4) * branch
            x_out[rows] = middle
            arriving.append(norm_send(ch, middle, xg2.at[level], st2.at[level]))
        wds[level].share()
        if more:
            wds[level + 1].begin()
        travelling = []
        for ch in range(CHUNKS):
            rows = spans[ch]
            finish(arriving[ch])
            norm_apply(level, ch, 5, xg2.at[level], st2.at[level], inv2.at[level], h2.at[level])
            if ch == 0:
                wus[level].ready()

            def widen_step(j, carry):
                lanes = pl.ds(pl.multiple_of(j * width, width), width)
                pre = mm(h2[level, rows], wu[level, :, :, :, :, lanes].reshape(full, width))
                pre = pre + ubias[level : level + 1, lanes]
                below = 0.5 * (1.0 + lax.erf(pre * (0.5**0.5)))
                zz[level, rows, lanes] = (pre * below).astype(BF)
                bell = jnp.exp(-0.5 * pre * pre) * (0.5 / jnp.pi) ** 0.5
                gp[level, rows, lanes] = (below + pre * bell).astype(BF)
                return carry

            lax.fori_loop(0, blocks, widen_step, 0, unroll=UNROLL)
            if ch == 0:
                wds[level].ready()
            if more:
                travelling.append(down_send(level, rows))
        if more:
            wqs[level + 1].share()
            wqs[level + 1].share()
            wos[level + 1].share()
        arriving = []
        for ch in range(CHUNKS):
            rows = spans[ch]
            if more:
                finish(travelling[ch])
                value = down_take(level, rows)
                arriving.append(norm_send(ch, value, xg.at[level + 1], st1.at[level + 1]))

    def norm_back_send(level, ch, part_of, gain, normed, store, stats):
        rows = spans[ch]
        copies, first, second = [], 0.0, 0.0
        for step in range(1, ncol + 1):
            i, device = net.peer("col", step)
            value = part_of(i)
            scaled = value * any_param(level, gain, i)
            first = first + jnp.sum(scaled, 1, keepdims=True)
            second = second + jnp.sum(scaled * normed[i, rows].astype(F32), 1, keepdims=True)
            if step < ncol:
                hsend[i, rows] = value.astype(BF)
                copies.append(net.start(hsend.at[i, rows], store.at[c, rows], device))
            else:
                store[c, rows] = value.astype(BF)
        stats[ch, c] = as_rows(first, second)
        return copies + net.spread("col", stats.at[ch, c], stats.at[ch, c])

    def norm_back(level, ch, gain, normed, inverse, store, stats):
        rows = spans[ch]
        upstream = slots(store, rows)
        normed = normed[c, rows].astype(F32)
        keep(level, gain, upstream * normed)
        keep(level, gain + 1, upstream)
        columns = as_columns(sum(stats[ch, i] for i in range(ncol)))
        scaled = upstream * param(level, gain)
        shift = columns[:, 0:1] * (1.0 / full) + normed * (columns[:, 1:2] * (1.0 / full))
        return inverse[rows, 0:1] * (scaled - shift)

    pieces = 2 * nz
    part_out, part_up = width // pieces, hidden // pieces

    def put_rows(store, i, start, value):
        rows = value.shape[0] // pieces
        for piece in range(pieces):
            store[piece % 2, i, piece // 2, start : start + rows, :] = value[piece * rows : (piece + 1) * rows]

    def grads_down_up(level):
        def down_step(j, carry):
            lanes = pl.ds(pl.multiple_of(j * width, width), width)
            upstream = jnp.concatenate([dmg[level, i] for i in range(ncol)], 1)
            value = mm_tn(zz[level, :, lanes], upstream).astype(BF)
            start = part_up
            for i in range(ncol):
                for t in range(2):
                    bulk[0][t, i, j, start : start + part_up, :] = value[
                        t * part_up : (t + 1) * part_up, i * width : (i + 1) * width
                    ]
            return carry

        def up_step(i, carry):
            lanes = pl.ds(pl.multiple_of(i * width, width), width)
            up = mm_tn(h2[level, :, lanes], dur[...]).astype(BF)
            up = [up[:, j * width : (j + 1) * width] for j in range(blocks)]
            put_rows(bulk[0], i, 0, jnp.concatenate(up, 0))
            return carry

        lax.fori_loop(0, blocks, down_step, 0, unroll=UNROLL)
        lax.fori_loop(0, nrow, up_step, 0, unroll=UNROLL)

    def grads_out(level, low):
        def step(i, carry):
            put_rows(tail[0], i, 0, mm_tn(attended(level, i, whole), low[...]).astype(BF))
            return carry

        lax.fori_loop(0, nrow, step, 0, unroll=UNROLL)

    def grads_qkv(level):
        def step(i, carry):
            lanes = pl.ds(pl.multiple_of(i * width, width), width)
            value = mm_tn(h[level, :, lanes], jg[...]).astype(BF)
            for j in range(3):
                put_rows(tail[0], i, (j + 1) * part_out, value[:, j * width : (j + 1) * width])
            return carry

        lax.fori_loop(0, nrow, step, 0, unroll=UNROLL)

    def reduce_steps(level, store, flipping):
        grad, crecv, ra, rb, ta, tb, ua, ub, fin, flipped, land = store
        rows = grad.shape[3]
        upper = rows // 2
        top, low = pl.ds(0, upper), pl.ds(upper, upper)
        copy = net.start(grad.at[1 - core], crecv, net.sibling)
        yield
        copy.wait()

        def add(i, carry):
            for j in range(nz):
                total = grad[core, i, j].astype(F32) + crecv[i, j].astype(F32)
                grad[core, i, j] = total.astype(BF)
            return carry

        lax.fori_loop(0, nrow, add, 0)
        copies = net.deal("row", lambda i: grad.at[core, i, :, top], ra.at[r])
        copies += net.deal("z", lambda i: grad.at[core, :, i, low], rb.at[z])
        yield
        finish(copies)

        def add_top(j, carry):
            total = grad[core, r, j, 0:upper].astype(F32)
            for step in range(1, nrow):
                total = total + ra[net.peer("row", step)[0], j].astype(F32)
            ta[j] = total.astype(BF)
            return carry

        def add_low(j, carry):
            total = grad[core, j, z, upper:].astype(F32)
            for step in range(1, nz):
                total = total + rb[net.peer("z", step)[0], j].astype(F32)
            tb[j] = total.astype(BF)
            return carry

        lax.fori_loop(0, nz, add_top, 0)
        lax.fori_loop(0, nrow, add_low, 0)
        copies = net.deal("z", lambda i: ta.at[i], ua.at[level, z])
        copies += net.deal("row", lambda i: tb.at[i], ub.at[level, r])
        yield
        finish(copies)
        total = ta[z].astype(F32)
        for step in range(1, nz):
            total = total + ua[level, net.peer("z", step)[0]].astype(F32)
        fin[level, 0:upper] = total.astype(BF)
        total = tb[r].astype(F32)
        for step in range(1, nrow):
            total = total + ub[level, net.peer("row", step)[0]].astype(F32)
        fin[level, upper:] = total.astype(BF)
        straight = rows - (part_up if flipping else 0)
        if flipping:
            turn = flip_start(fin.at[level, pl.ds(straight, part_up)], flipped.at[level])
            yield
            flip_wait(turn)
            land[core, z, straight:] = flipped[level]
        land[core, z, 0:straight] = fin[level, 0:straight]
        copies = net.spread("z", land.at[core, z], land.at[core, z])
        yield
        finish(copies)
        copy = net.start(land.at[core], land.at[core], net.sibling)
        yield
        copy.wait()
        for piece in range(pieces):
            found = land[piece % 2, piece // 2]
            some = slice(piece * part_out, (piece + 1) * part_out)
            if flipping:
                block, inner = divmod(piece * part_up, width)
                gup[level, inner : inner + part_up, block * width : (block + 1) * width] = found[0:part_up]
                gdown[level, piece * part_up : (piece + 1) * part_up] = found[part_up:]
            else:
                gout[level, some] = found[0:part_out]
                for j in range(3):
                    gq[level, j, some] = found[(j + 1) * part_out : (j + 2) * part_out]
        yield

    heavy, light = [], []

    def advance(queue):
        for steps in queue:
            next(steps, None)

    arriving = above
    for level in reversed(range(layers)):
        last = level == 0
        advance(heavy)
        advance(light)
        travelling = []
        for ch in range(CHUNKS):
            rows = spans[ch]
            finish(arriving[ch])

            def dz_step(j, carry):
                lanes = pl.ds(pl.multiple_of(j * width, width), width)
                per_half = blocks // 2
                group = width // part_up
                value = 0.0
                for i in range(ncol):
                    weight = wd[level, i, j // per_half, pl.ds((j % per_half) * group, group)]
                    value = value + mm_nt(dmg[level, i, rows], weight.reshape(width, width))
                value = value * gp[level, rows, lanes].astype(F32)
                dur[rows, lanes] = value.astype(BF)
                return carry

            lax.fori_loop(0, blocks, dz_step, 0, unroll=UNROLL)
            travelling.append(
                norm_back_send(
                    level, ch, lambda i: mm_nt(dur[rows], wu[level, i].reshape(width, hidden)),
                    5, xg2.at[level], hrecv2.at[level], bst2.at[level],
                )
            )
        for j in range(blocks):
            keep(level, 10 + j, dur[:, j * width : (j + 1) * width].astype(F32))
        advance(heavy)
        advance(light)
        grads_down_up(level)
        heavy.append(reduce_steps(level, bulk, True))
        advance(heavy[-1:])
        arriving = []
        for ch in range(CHUNKS):
            rows = spans[ch]
            finish(travelling[ch])
            middle = g_out[rows] + norm_back(
                level, ch, 5, xg2.at[level], inv2.at[level], hrecv2.at[level], bst2.at[level]
            )
            g_out[rows] = middle
            keep(level, 4, middle * abr[level, rows])
            scaled = middle * param(level, 4)
            keep(level, 3, scaled)
            dob[rows] = scaled.astype(BF)
            copies = []
            for step in range(1, ncol + 1):
                i, device = net.peer("col", step)
                piece = mm_nt(dob[rows], wo[level, i].reshape(width, width)).astype(BF)
                if step < ncol:
                    osend[i, rows] = piece
                    copies.append(net.start(osend.at[i, rows], orecv.at[level, c, rows], device))
                else:
                    orecv[level, c, rows] = piece
            arriving.append(copies)
        advance(heavy)
        advance(light)
        grads_out(level, dob)
        for ch in range(CHUNKS):
            finish(arriving[ch])
            dob[spans[ch]] = slots(orecv.at[level], spans[ch]).astype(BF)
        early, late = [], [[] for _ in range(CHUNKS)]
        for p in range(pairs):
            attend_back(level, p)
            if p + 1 < pairs:
                early += net.deal("row", lambda i: kvsend.at[p, i], kvrecv.at[level, p, r])
            else:
                for ch in range(CHUNKS):
                    late[ch] = net.deal(
                        "row", lambda i: kvsend.at[p, i, :, spans[ch]], kvrecv.at[level, p, r, :, spans[ch]]
                    )
        if level + 1 == layers:
            descending = [down_send(level, spans[ch]) for ch in range(CHUNKS)]
        advance(heavy)
        advance(light)
        finish(early)
        travelling = []
        def take_kv(ch):
            rows = spans[ch]
            finish(late[ch])
            for p in range(pairs):
                for j in range(2):
                    total = sum(kvrecv[level, p, i, j, rows].astype(F32) for i in range(nrow))
                    start = (j + 1) * width + p * LANES
                    jg[rows, start : start + LANES] = total.astype(BF)

        def send_dh(ch):
            rows = spans[ch]

            def dh_part(i):
                return sum(
                    mm_nt(jg[rows, j * width : (j + 1) * width], wq[level, i, :, j].reshape(width, width))
                    for j in range(3)
                )

            return norm_back_send(level, ch, dh_part, 0, xg.at[level], hrecv1.at[level], bst1.at[level])

        def reduce_qkv():
            advance(light)
            grads_qkv(level)
            light.append(reduce_steps(level, tail, False))
            advance(light[-1:])

        for ch in range(CHUNKS):
            take_kv(ch)
            if not last:
                travelling.append(send_dh(ch))
        reduce_qkv()
        if last:
            travelling = [send_dh(ch) for ch in range(CHUNKS)]
            advance(light)
        keep(level, 9, jg[:, 0:width].astype(F32))
        keep(level, 2, jg[:, 2 * width :].astype(F32))
        if last:
            advance(heavy)
        if level + 1 == layers:
            for ch in range(CHUNKS):
                finish(descending[ch])
                down_take(level, spans[ch])
                keep(level, 8, cot[spans[ch]] * mbr[level, spans[ch]])
        arriving = []
        for ch in range(CHUNKS):
            finish(travelling[ch])
            upstream = g_out[spans[ch]] + norm_back(
                level, ch, 0, xg.at[level], inv1.at[level], hrecv1.at[level], bst1.at[level]
            )
            arriving.append(branch_back(level - 1, ch, upstream))

    sharing = net.start(sums, sumc, net.sibling)
    advance(light)
    advance(heavy)
    sharing.wait()
    sumy[r] = sums[...] + sumc[...]
    copies = net.spread("row", sumy.at[r], sumy.at[r])
    advance(light)
    advance(heavy)
    finish(copies)
    sumz[z] = sumy[0] + sumy[1] + sumy[2] + sumy[3]
    copies = net.spread("z", sumz.at[z], sumz.at[z])
    advance(light)
    advance(heavy)
    finish(copies)
    total = sumz[0] + sumz[1] + sumz[2] + sumz[3]
    for level in range(layers):
        start = level * per
        for i in range(9):
            small_out[i, level : level + 1, :] = total[start + i : start + i + 1]
        qbias_out[level : level + 1, :] = total[start + 9 : start + 10]
        for j in range(blocks):
            ubias_out[level : level + 1, j * width : (j + 1) * width] = total[start + 10 + j : start + 11 + j]
    for steps in light + heavy:
        for _ in steps:
            pass


def shards(sizes, inputs, w_qkv, w_out, w_up, w_down, small_params, query_bias, up_bias, cotangent):
    tokens, width = inputs.shape
    layers, _, hidden = w_up.shape
    ncol, nrow, nz = sizes["col"], sizes["row"], sizes["z"]
    full, half = width * ncol, width // 2
    blocks = hidden // width
    rows = -(-layers * (10 + blocks) // 8) * 8
    bulk, tail = 2 * hidden // (2 * nz), 4 * width // (2 * nz)
    vmem = lambda shape, dtype=BF: pltpu.VMEM(shape, dtype)
    scratch = [
        vmem((layers, nrow, 2, 3, half, width)),
        vmem((layers, nrow, 2, half, width)),
        vmem((layers, nrow, 2, nz, half // nz, hidden)),
        vmem((layers, nrow, 2, nz, hidden // (2 * nz), width)),
        vmem((ncol, 9, 8, width), F32),
        vmem((layers, ncol, tokens, width)),
        vmem((layers, CHUNKS, ncol, 8, tokens // CHUNKS), F32),
        vmem((layers, tokens, full)),
        vmem((layers, tokens, width)),
        vmem((layers, nrow, width // LANES, 2, tokens, LANES)),
        vmem((layers, width // HD, tokens, tokens * nrow)),
        vmem((layers, ncol, width // LANES, tokens, LANES)),
        vmem((layers, tokens, width), F32),
        vmem((layers, ncol, tokens, width)),
        vmem((layers, CHUNKS, ncol, 8, tokens // CHUNKS), F32),
        vmem((layers, tokens, full)),
        vmem((layers, tokens, hidden)),
        vmem((layers, tokens, hidden)),
        vmem((layers, tokens, width), F32),
        vmem((layers, tokens, LANES), F32),
        vmem((layers, tokens, LANES), F32),
        vmem((ncol, tokens, width)),
        vmem((layers, ncol, tokens, width)),
        vmem((layers, ncol, tokens, width)),
        vmem((tokens, hidden)),
        vmem((ncol, tokens, width)),
        vmem((layers, ncol, tokens, width)),
        vmem((layers, CHUNKS, ncol, 8, tokens // CHUNKS), F32),
        vmem((ncol, tokens, width)),
        vmem((layers, ncol, tokens, width)),
        vmem((tokens, width)),
        vmem((width // LANES, nrow, 2, tokens, LANES)),
        vmem((layers, width // LANES, nrow, 2, tokens, LANES)),
        vmem((tokens, 3 * width)),
        vmem((layers, ncol, tokens, width)),
        vmem((layers, CHUNKS, ncol, 8, tokens // CHUNKS), F32),
        vmem((rows, width), F32),
        vmem((rows, width), F32),
        vmem((nrow, rows, width), F32),
        vmem((nz, rows, width), F32),
    ]
    for piece in (bulk, tail):
        scratch += [
            vmem((2, nrow, nz, piece, width)),
            vmem((nrow, nz, piece, width)),
            vmem((nrow, nz, piece // 2, width)),
            vmem((nz, nrow, piece // 2, width)),
            vmem((nz, piece // 2, width)),
            vmem((nrow, piece // 2, width)),
            vmem((layers, nz, piece // 2, width)),
            vmem((layers, nrow, piece // 2, width)),
            vmem((layers, piece, width)),
            vmem((layers, hidden // (2 * nz), width)),
            vmem((2, nz, piece, width)),
        ]
    scratch += [
        pltpu.SemaphoreType.DMA((384,)),
        pltpu.SemaphoreType.DMA((384,)),
        pltpu.SemaphoreType.DMA((16,)),
    ]
    here = pl.BlockSpec(memory_space=pltpu.VMEM)
    far = pl.BlockSpec(memory_space=pl.ANY)
    output, input_grad, qkv, out, up, down, small, query, hidden_bias = pl.pallas_call(
        partial(body, sizes, layers),
        out_shape=(
            jax.ShapeDtypeStruct((tokens, width), F32),
            jax.ShapeDtypeStruct((tokens, width), F32),
            jax.ShapeDtypeStruct((layers, 3, width, width), BF),
            jax.ShapeDtypeStruct((layers, width, width), BF),
            jax.ShapeDtypeStruct((layers, width, hidden), BF),
            jax.ShapeDtypeStruct((layers, hidden, width), BF),
            jax.ShapeDtypeStruct((9, layers, width), F32),
            jax.ShapeDtypeStruct((layers, width), F32),
            jax.ShapeDtypeStruct((layers, hidden), F32),
        ),
        in_specs=[here] * 5 + [far] * 4,
        out_specs=(here,) * 9,
        scratch_shapes=scratch,
        compiler_params=pltpu.CompilerParams(
            collective_id=0, has_side_effects=True, vmem_limit_bytes=63 << 20
        ),
        name="encoder",
    )(
        inputs,
        cotangent,
        jnp.swapaxes(small_params, 0, 1),
        query_bias,
        up_bias,
        jnp.swapaxes(w_qkv, 1, 2).reshape(layers, 3, 2, half, width),
        w_out.reshape(layers, 2, half, width),
        w_up.reshape(layers, 2, nz, half // nz, hidden),
        w_down.reshape(layers, 2, nz, hidden // (2 * nz), width),
    )
    return (
        output,
        input_grad,
        jnp.swapaxes(qkv, 1, 2).astype(F32),
        out.astype(F32),
        up.astype(F32),
        down.astype(F32),
        jnp.swapaxes(small, 0, 1),
        query,
        hidden_bias,
    )


def solution(mesh):
    sizes = {"col": mesh.shape["col"], "row": mesh.shape["row"], "z": mesh.shape["dp"] // 2}
    placed = (
        P(("dp", "row"), "col"),
        P(None, "row", None, "col"),
        P(None, "row", "col"),
        P(None, "row", "col"),
        P(None, "row", "col"),
        P(None, None, "col"),
        P(None, "col"),
        P(None, "col"),
        P(("dp", "row"), "col"),
    )
    return jax.shard_map(
        partial(shards, sizes),
        mesh=mesh,
        in_specs=placed,
        out_specs=(
            P(("dp", "row"), "col"),
            P(("dp", "row"), "col"),
            P(None, "row", None, "col"),
            P(None, "row", "col"),
            P(None, "row", "col"),
            P(None, "row", "col"),
            P(None, None, "col"),
            P(None, "col"),
            P(None, "col"),
        ),
        check_vma=False,
    )
```

```python
from functools import partial

import jax
import jax.numpy as jnp
from jax import lax
from jax.experimental import pallas as pl
from jax.experimental.pallas import tpu as pltpu
from jax.sharding import PartitionSpec as P

HD = 64
EPS = 1e-06
LANES = 128
CHUNKS = 2
UNROLL = 1
BF = jnp.bfloat16
F32 = jnp.float32
MESH = pl.DeviceIdType.MESH


def mm(left, right):
    return jnp.dot(left, right, preferred_element_type=F32)


def mm_nt(left, right):
    return lax.dot_general(left, right, (((1,), (1,)), ((), ())), preferred_element_type=F32)


def mm_tn(left, right):
    return lax.dot_general(left, right, (((0,), (0,)), ((), ())), preferred_element_type=F32)


class Links:
    def __init__(self, sizes, send, recv, local):
        self.sizes = sizes
        self.send, self.recv, self.local = send, recv, local
        self.used = 0
        self.used_local = 0
        self.col = lax.axis_index("col")
        self.row = lax.axis_index("row")
        place = lax.axis_index("dp")
        self.z = place // 2
        self.core = place % 2
        self.sibling = {"dp": self.z * 2 + (1 - self.core)}

    def peer(self, axis, step):
        if axis == "z":
            index = lax.rem(self.z + step, self.sizes["z"])
            return index, {"dp": index * 2 + self.core}
        index = lax.rem(getattr(self, axis) + step, self.sizes[axis])
        return index, {axis: index}

    def start(self, source, target, device, begin=True):
        copy = pltpu.make_async_remote_copy(
            src_ref=source,
            dst_ref=target,
            send_sem=self.send.at[self.used],
            recv_sem=self.recv.at[self.used],
            device_id=device,
            device_id_type=MESH,
        )
        self.used += 1
        if begin:
            copy.start()
        return copy

    def bring(self, source, target):
        copy = pltpu.make_async_copy(source, target, self.local.at[self.used_local])
        self.used_local += 1
        copy.start()
        return copy

    def spread(self, axis, source, target):
        return [
            self.start(source, target, self.peer(axis, step)[1])
            for step in far_first(self.sizes[axis])
        ]

    def deal(self, axis, source_of, target):
        copies = []
        for step in far_first(self.sizes[axis]):
            index, device = self.peer(axis, step)
            copies.append(self.start(source_of(index), target, device))
        return copies


def far_first(count):
    return sorted(range(1, count), key=lambda step: -min(step, count - step))


def finish(copies):
    for copy in copies:
        copy.wait()


def as_rows(first, second):
    tokens = first.shape[0]
    lane = lax.broadcasted_iota(jnp.int32, (tokens, LANES), 1)
    both = jnp.where(lane == 0, first, jnp.where(lane == 1, second, 0.0))
    return both.T[:8]


def as_columns(rows):
    count, tokens = rows.shape
    return jnp.concatenate([rows, jnp.zeros((LANES - count, tokens), F32)], 0).T


def body(sizes, layers, *refs):
    (
        x_in, cot, small, qbias, ubias, wq_in, wo_in, wu_in, wd_in,
        x_out, g_out, gq, gout, gup, gdown, small_out, qbias_out, ubias_out,
        wq, wo, wu, wd, smg, xg, st1, h, q, kvg, probs, og, abr, xg2, st2, h2, gp, zz, mbr,
        inv1, inv2, msend, mrecv, dmg, dur, hsend, hrecv2, bst2, osend, orecv, dob, kvsend, kvrecv,
        jg, hrecv1, bst1, sums, sumc, sumy, sumz, *chunk_refs, send, recv, local,
    ) = refs
    bulk, tail = chunk_refs[: len(chunk_refs) // 2], chunk_refs[len(chunk_refs) // 2 :]
    net = Links(sizes, send, recv, local)
    c, r, z, core = net.col, net.row, net.z, net.core
    ncol, nrow, nz = sizes["col"], sizes["row"], sizes["z"]
    tokens, width = x_in.shape
    hidden = ubias.shape[1]
    full = width * ncol
    length = tokens * nrow
    blocks = hidden // width
    pairs = width // LANES
    scale = HD ** (-0.5)
    part = tokens // CHUNKS
    spans = [slice(i * part, (i + 1) * part) for i in range(CHUNKS)]
    whole = slice(0, tokens)

    barrier = pltpu.get_barrier_semaphore()
    greeted = [net.peer(a, s)[1] for a in ("col", "row", "z") for s in range(1, sizes[a])]
    greeted.append(net.sibling)
    for device in greeted:
        pl.semaphore_signal(barrier, inc=1, device_id=device, device_id_type=MESH)
    mirror = {"row": c, "col": r}

    @pl.when(r != c)
    def _():
        pl.semaphore_signal(barrier, inc=1, device_id=mirror, device_id_type=MESH)

    pl.semaphore_wait(barrier, len(greeted) + jnp.where(r != c, 1, 0))

    def flip_start(source, target):
        copy = net.start(source, target, mirror, begin=False)
        here = pltpu.make_async_copy(source, target, local.at[net.used_local])
        net.used_local += 1

        @pl.when(r != c)
        def _():
            copy.start()

        @pl.when(r == c)
        def _():
            here.start()

        return copy, here

    def flip_wait(pair):
        copy, here = pair

        @pl.when(r != c)
        def _():
            copy.wait()

        @pl.when(r == c)
        def _():
            here.wait()

    class Weight:
        def __init__(self, level, source, store):
            self.level, self.source, self.store = level, source, store

        def split(self, place):
            if len(place.shape) == 3:
                return [place.at[pl.ds(1, 2)], place.at[pl.ds(0, 1)]]
            return [place]

        def begin(self):
            place = self.store.at[self.level, r, core]
            if len(self.source.shape) == 5:
                source = self.source.at[self.level, :, core]
            else:
                source = self.source.at[self.level, core]
            self.queue = [
                [net.bring(a, b)] + net.spread("row", a, b)
                for a, b in zip(self.split(source), self.split(place))
            ]
            self.shared, self.taken = [], 0

        def share(self):
            finish(self.queue.pop(0))
            place = self.store.at[self.level, :, core]
            if len(place.shape) == 4 and place.shape[1] == 3:
                first, count = (0, 1) if self.shared else (1, 2)
                place = place.at[:, pl.ds(first, count)]
            self.shared.append(net.start(place, place, net.sibling))

        def ready(self):
            self.shared[self.taken].wait()
            self.taken += 1

    class Relayed(Weight):
        def begin(self):
            place = self.store.at[self.level, r, core, z]
            self.own = net.bring(self.source.at[self.level, core], self.store.at[self.level, r, core])
            self.copies = net.spread("row", self.source.at[self.level, core, z], place)
            self.shared, self.taken = [], 0

        def relay(self):
            finish(self.copies)
            copies = [self.own]
            for step in range(1, nrow):
                i, _ = net.peer("row", step)
                place = self.store.at[self.level, i, core, z]
                copies += net.spread("z", place, place)
            self.queue = [copies]

    class Flipped(Weight):
        def flip(self):
            self.turn = flip_start(
                self.source.at[self.level, core, z], self.store.at[self.level, c, core, z]
            )

        def begin(self):
            place = self.store.at[self.level, r, core, z]
            flip_wait(self.turn)
            self.copies = net.spread("row", place, place)
            self.shared, self.taken = [], 0

        def relay(self):
            finish(self.copies)
            place = self.store.at[self.level, :, core, z]
            self.queue = [net.spread("z", place, place)]

    wqs = [Weight(l, wq_in, wq) for l in range(layers)]
    wos = [Weight(l, wo_in, wo) for l in range(layers)]
    wus = [Relayed(l, wu_in, wu) for l in range(layers)]
    wds = [Flipped(l, wd_in, wd) for l in range(layers)]

    def param(level, index):
        return small[index, level : level + 1, :]

    def any_param(level, index, block):
        return smg[block, index, level : level + 1, :]

    def norm_send(ch, value, store, stats):
        mean = jnp.sum(value, 1, keepdims=True) * (1.0 / width)
        centered = value - mean
        place = store.at[c, spans[ch]]
        place[...] = centered.astype(BF)
        stats[ch, c] = as_rows(mean, jnp.sum(centered * centered, 1, keepdims=True))
        copies = net.spread("col", place, place)
        return copies + net.spread("col", stats.at[ch, c], stats.at[ch, c])

    def norm_apply(level, ch, first, store, stats, inverse, result):
        columns = as_columns(stats[ch].reshape(ncol * 8, part))
        means = [columns[:, 8 * i : 8 * i + 1] for i in range(ncol)]
        mean = sum(means) * (1.0 / ncol)
        spread = sum(columns[:, 8 * i + 1 : 8 * i + 2] for i in range(ncol))
        spread = spread + width * sum((m - mean) * (m - mean) for m in means)
        scaled = lax.rsqrt(spread * (1.0 / full) + EPS)
        inverse[spans[ch]] = jnp.broadcast_to(scaled, (part, LANES))
        for i in range(ncol):
            normed = (store[i, spans[ch]].astype(F32) + (means[i] - mean)) * scaled
            store[i, spans[ch]] = normed.astype(BF)
            result[spans[ch], i * width : (i + 1) * width] = (
                normed * any_param(level, first, i) + any_param(level, first + 1, i)
            ).astype(BF)

    def slots(store, rows):
        return sum(store[i, rows].astype(F32) for i in range(store.shape[0]))

    def one_head(value, side):
        spot = lax.broadcasted_iota(jnp.int32, value.shape, 1)
        return jnp.where((spot < HD) == (side == 0), value.astype(F32), 0.0).astype(BF)

    def pick(values):
        side = lax.broadcasted_iota(jnp.int32, values[0].shape, 1)
        return jnp.where(side < HD, values[0], values[1])

    def attend(level, p, rows):
        lanes = slice(p * LANES, (p + 1) * LANES)
        queries = q[level, rows, lanes]
        keys = kvg[level, :, p, 0].reshape(length, LANES)
        values = kvg[level, :, p, 1].reshape(length, LANES)
        found = []
        for side in range(2):
            scores = mm_nt(one_head(queries, side), keys) * scale
            raised = jnp.exp(scores - jnp.max(scores, 1, keepdims=True))
            share = (raised * (1.0 / jnp.sum(raised, 1, keepdims=True))).astype(BF)
            probs[level, 2 * p + side, rows] = share
            found.append(mm(share, values))
        place = og.at[level, c, p, rows]
        place[...] = pick(found).astype(BF)
        return net.spread("col", place, place)

    def attended(level, i, rows):
        return jnp.concatenate([og[level, i, p, rows] for p in range(pairs)], 1)

    def attend_back(level, p):
        lanes = slice(p * LANES, (p + 1) * LANES)
        queries = q[level, :, lanes]
        upstream = dob[:, lanes]
        keys = kvg[level, :, p, 0].reshape(length, LANES)
        values = kvg[level, :, p, 1].reshape(length, LANES)
        dq, dk, dv = [], [], []
        for side in range(2):
            share = probs[level, 2 * p + side]
            wide = share.astype(F32)
            pulled = mm_nt(one_head(upstream, side), values)
            inner = jnp.sum(wide * pulled, 1, keepdims=True)
            slope = (wide * (pulled - inner)).astype(BF)
            dq.append(mm(slope, keys))
            dk.append(mm_tn(slope, queries))
            dv.append(mm_tn(share, upstream))
        jg[:, lanes] = (pick(dq) * scale).astype(BF)
        kvsend[p, :, 0] = (pick(dk) * scale).astype(BF).reshape(nrow, tokens, LANES)
        kvsend[p, :, 1] = pick(dv).astype(BF).reshape(nrow, tokens, LANES)
        for j in range(2):
            kvrecv[level, p, r, j] = kvsend[p, r, j]

    def down_send(level, rows):
        copies = []
        for step in far_first(ncol) + [ncol]:
            i, device = net.peer("col", step)
            piece = mm(zz[level, rows], wd[level, i].reshape(hidden, width)).astype(BF)
            if step < ncol:
                msend[i, rows] = piece
                copies.append(net.start(msend.at[i, rows], mrecv.at[level, c, rows], device))
            else:
                mrecv[level, c, rows] = piece
        return copies

    def down_take(level, rows):
        branch = slots(mrecv.at[level], rows) + param(level, 7)
        mbr[level, rows] = branch
        value = x_out[rows] + param(level, 8) * branch
        x_out[rows] = value
        return value

    sums[...] = jnp.zeros_like(sums)
    per = 9 + 1 + blocks

    def keep(level, index, value):
        sums[level * per + index : level * per + index + 1, :] += jnp.sum(value, 0, keepdims=True)

    def branch_back(level, ch, upstream):
        rows = spans[ch]
        g_out[rows] = upstream
        if level < 0:
            return []
        if level + 1 < layers:
            keep(level, 8, upstream * mbr[level, rows])
        scaled = upstream * param(level, 8)
        keep(level, 7, scaled)
        place = dmg.at[level, c, rows]
        place[...] = scaled.astype(BF)
        return net.spread("col", place, place)

    smg[c, :, 0:layers] = small[...]
    wqs[0].begin()
    ahead = net.spread("col", smg.at[c], smg.at[c])
    arriving = []
    for ch in range(CHUNKS):
        value = x_in[spans[ch]]
        x_out[spans[ch]] = value
        arriving.append(norm_send(ch, value, xg.at[0], st1.at[0]))
    for level in range(layers):
        more = level + 1 < layers
        if level == 0:
            wos[0].begin()
            wus[0].begin()
            wds[0].flip()
            finish(ahead)
        travelling = []
        for ch in range(CHUNKS):
            finish(arriving[ch])
            rows = spans[ch]
            norm_apply(level, ch, 0, xg.at[level], st1.at[level], inv1.at[level], h.at[level])
            if ch == 0:
                if level == 0:
                    wqs[0].share()
                    wds[0].begin()
                wqs[level].ready()
                if level == 0:
                    wqs[0].share()

            def project(j):
                return mm(h[level, rows], wq[level, :, :, j].reshape(full, width))

            keys = project(1).astype(BF)
            values = (project(2) + param(level, 2)).astype(BF)
            for p in range(pairs):
                lanes = slice(p * LANES, (p + 1) * LANES)
                kvg[level, r, p, 0, rows] = keys[:, lanes]
                kvg[level, r, p, 1, rows] = values[:, lanes]
                place = kvg.at[level, r, p, :, rows]
                if p == 0:
                    travelling.append(net.spread("row", place, place))
        for p in range(1, pairs):
            place = kvg.at[level, r, p]
            travelling.append(net.spread("row", place, place))
        wqs[level].ready()
        q[level] = (
            mm(h[level], wq[level, :, :, 0].reshape(full, width)) + qbias[level : level + 1, :]
        ).astype(BF)
        wus[level].relay()
        wds[level].relay()
        if level == 0:
            wos[0].share()
        if not more:
            above = [branch_back(level, ch, cot[spans[ch]]) for ch in range(CHUNKS)]
        for ch in range(CHUNKS):
            finish(travelling[ch])
        early = [attend(level, 0, whole)]
        for p in range(1, pairs):
            finish(travelling[CHUNKS + p - 1])
        late = [[attend(level, p, spans[ch]) for p in range(1, pairs)] for ch in range(CHUNKS)]
        wus[level].share()
        if more:
            wqs[level + 1].begin()
            wos[level + 1].begin()
            wus[level + 1].begin()
            wds[level + 1].flip()
        finish(early[0])
        arriving = []
        for ch in range(CHUNKS):
            rows = spans[ch]
            for copies in late[ch]:
                finish(copies)
            if ch == 0:
                wos[level].ready()
            branch = param(level, 3)
            for i in range(ncol):
                branch = branch + mm(attended(level, i, rows), wo[level, i].reshape(width, width))
            abr[level, rows] = branch
            middle = x_out[rows] + param(level, 4) * branch
            x_out[rows] = middle
            arriving.append(norm_send(ch, middle, xg2.at[level], st2.at[level]))
        wds[level].share()
        if more:
            wds[level + 1].begin()
        travelling = []
        for ch in range(CHUNKS):
            rows = spans[ch]
            finish(arriving[ch])
            norm_apply(level, ch, 5, xg2.at[level], st2.at[level], inv2.at[level], h2.at[level])
            if ch == 0:
                wus[level].ready()

            def widen_step(j, carry):
                lanes = pl.ds(pl.multiple_of(j * width, width), width)
                pre = mm(h2[level, rows], wu[level, :, :, :, :, lanes].reshape(full, width))
                pre = pre + ubias[level : level + 1, lanes]
                below = 0.5 * (1.0 + lax.erf(pre * (0.5**0.5)))
                zz[level, rows, lanes] = (pre * below).astype(BF)
                bell = jnp.exp(-0.5 * pre * pre) * (0.5 / jnp.pi) ** 0.5
                gp[level, rows, lanes] = (below + pre * bell).astype(BF)
                return carry

            lax.fori_loop(0, blocks, widen_step, 0, unroll=UNROLL)
            if ch == 0:
                wds[level].ready()
            if more:
                travelling.append(down_send(level, rows))
        if more:
            wqs[level + 1].share()
            wqs[level + 1].share()
            wos[level + 1].share()
        arriving = []
        for ch in range(CHUNKS):
            rows = spans[ch]
            if more:
                finish(travelling[ch])
                value = down_take(level, rows)
                arriving.append(norm_send(ch, value, xg.at[level + 1], st1.at[level + 1]))

    def norm_back_send(level, ch, part_of, gain, normed, store, stats):
        rows = spans[ch]
        copies, first, second = [], 0.0, 0.0
        for step in far_first(ncol) + [ncol]:
            i, device = net.peer("col", step)
            value = part_of(i)
            scaled = value * any_param(level, gain, i)
            first = first + jnp.sum(scaled, 1, keepdims=True)
            second = second + jnp.sum(scaled * normed[i, rows].astype(F32), 1, keepdims=True)
            if step < ncol:
                hsend[i, rows] = value.astype(BF)
                copies.append(net.start(hsend.at[i, rows], store.at[c, rows], device))
            else:
                store[c, rows] = value.astype(BF)
        stats[ch, c] = as_rows(first, second)
        return copies + net.spread("col", stats.at[ch, c], stats.at[ch, c])

    def norm_back(level, ch, gain, normed, inverse, store, stats):
        rows = spans[ch]
        upstream = slots(store, rows)
        normed = normed[c, rows].astype(F32)
        keep(level, gain, upstream * normed)
        keep(level, gain + 1, upstream)
        columns = as_columns(sum(stats[ch, i] for i in range(ncol)))
        scaled = upstream * param(level, gain)
        shift = columns[:, 0:1] * (1.0 / full) + normed * (columns[:, 1:2] * (1.0 / full))
        return inverse[rows, 0:1] * (scaled - shift)

    pieces = 2 * nz
    part_out, part_up = width // pieces, hidden // pieces

    def put_rows(store, i, start, value):
        rows = value.shape[0] // pieces
        for piece in range(pieces):
            store[piece % 2, i, piece // 2, start : start + rows, :] = value[piece * rows : (piece + 1) * rows]

    def grads_down_up(level):
        def down_step(j, carry):
            lanes = pl.ds(pl.multiple_of(j * width, width), width)
            upstream = jnp.concatenate([dmg[level, i] for i in range(ncol)], 1)
            value = mm_tn(zz[level, :, lanes], upstream).astype(BF)
            start = part_up
            for i in range(ncol):
                for t in range(2):
                    bulk[0][t, i, j, start : start + part_up, :] = value[
                        t * part_up : (t + 1) * part_up, i * width : (i + 1) * width
                    ]
            return carry

        def up_step(i, carry):
            lanes = pl.ds(pl.multiple_of(i * width, width), width)
            up = mm_tn(h2[level, :, lanes], dur[...]).astype(BF)
            up = [up[:, j * width : (j + 1) * width] for j in range(blocks)]
            put_rows(bulk[0], i, 0, jnp.concatenate(up, 0))
            return carry

        lax.fori_loop(0, blocks, down_step, 0)
        lax.fori_loop(0, nrow, up_step, 0)

    def grads_out(level, low):
        def step(i, carry):
            put_rows(tail[0], i, 0, mm_tn(attended(level, i, whole), low[...]).astype(BF))
            return carry

        lax.fori_loop(0, nrow, step, 0)

    def grads_qkv(level):
        def step(i, carry):
            lanes = pl.ds(pl.multiple_of(i * width, width), width)
            value = mm_tn(h[level, :, lanes], jg[...]).astype(BF)
            for j in range(3):
                put_rows(tail[0], i, (j + 1) * part_out, value[:, j * width : (j + 1) * width])
            return carry

        lax.fori_loop(0, nrow, step, 0)

    def reduce_steps(level, store, flipping):
        grad, crecv, ra, rb, ta, tb, ua, ub, fin, flipped, land = store
        rows = grad.shape[3]
        upper = ta.shape[1]
        top, low = pl.ds(0, upper), pl.ds(upper, rows - upper)
        copy = net.start(grad.at[1 - core], crecv, net.sibling)
        yield
        copy.wait()

        def add(i, carry):
            for j in range(nz):
                total = grad[core, i, j].astype(F32) + crecv[i, j].astype(F32)
                grad[core, i, j] = total.astype(BF)
            return carry

        lax.fori_loop(0, nrow, add, 0)
        copies = net.deal("row", lambda i: grad.at[core, i, :, top], ra.at[r])
        copies += net.deal("z", lambda i: grad.at[core, :, i, low], rb.at[z])
        yield
        finish(copies)

        def add_top(j, carry):
            total = grad[core, r, j, 0:upper].astype(F32)
            for step in range(1, nrow):
                total = total + ra[net.peer("row", step)[0], j].astype(F32)
            ta[j] = total.astype(BF)
            return carry

        def add_low(j, carry):
            total = grad[core, j, z, upper:].astype(F32)
            for step in range(1, nz):
                total = total + rb[net.peer("z", step)[0], j].astype(F32)
            tb[j] = total.astype(BF)
            return carry

        lax.fori_loop(0, nz, add_top, 0)
        lax.fori_loop(0, nrow, add_low, 0)
        copies = net.deal("z", lambda i: ta.at[i], ua.at[level, z])
        copies += net.deal("row", lambda i: tb.at[i], ub.at[level, r])
        yield
        finish(copies)
        total = ta[z].astype(F32)
        for step in range(1, nz):
            total = total + ua[level, net.peer("z", step)[0]].astype(F32)
        fin[level, 0:upper] = total.astype(BF)
        total = tb[r].astype(F32)
        for step in range(1, nrow):
            total = total + ub[level, net.peer("row", step)[0]].astype(F32)
        fin[level, upper:] = total.astype(BF)
        straight = rows - (part_up if flipping else 0)
        if flipping:
            turn = flip_start(fin.at[level, pl.ds(straight, part_up)], flipped.at[level])
            yield
            flip_wait(turn)
            land[core, z, straight:] = flipped[level]
        land[core, z, 0:straight] = fin[level, 0:straight]
        copies = net.spread("z", land.at[core, z], land.at[core, z])
        yield
        finish(copies)
        copy = net.start(land.at[core], land.at[core], net.sibling)
        yield
        copy.wait()
        for piece in range(pieces):
            found = land[piece % 2, piece // 2]
            some = slice(piece * part_out, (piece + 1) * part_out)
            if flipping:
                block, inner = divmod(piece * part_up, width)
                gup[level, inner : inner + part_up, block * width : (block + 1) * width] = found[0:part_up]
                gdown[level, piece * part_up : (piece + 1) * part_up] = found[part_up:]
            else:
                gout[level, some] = found[0:part_out]
                for j in range(3):
                    gq[level, j, some] = found[(j + 1) * part_out : (j + 2) * part_out]
        yield

    heavy, light = [], []

    def advance(queue):
        for steps in queue:
            next(steps, None)

    arriving = above
    for level in reversed(range(layers)):
        last = level == 0
        advance(heavy)
        advance(light)
        travelling = []
        for ch in range(CHUNKS):
            rows = spans[ch]
            finish(arriving[ch])

            def dz_step(j, carry):
                lanes = pl.ds(pl.multiple_of(j * width, width), width)
                per_half = blocks // 2
                group = width // part_up
                value = 0.0
                for i in range(ncol):
                    weight = wd[level, i, j // per_half, pl.ds((j % per_half) * group, group)]
                    value = value + mm_nt(dmg[level, i, rows], weight.reshape(width, width))
                value = value * gp[level, rows, lanes].astype(F32)
                dur[rows, lanes] = value.astype(BF)
                return carry

            lax.fori_loop(0, blocks, dz_step, 0, unroll=UNROLL)
            travelling.append(
                norm_back_send(
                    level, ch, lambda i: mm_nt(dur[rows], wu[level, i].reshape(width, hidden)),
                    5, xg2.at[level], hrecv2.at[level], bst2.at[level],
                )
            )
        for j in range(blocks):
            keep(level, 10 + j, dur[:, j * width : (j + 1) * width].astype(F32))
        advance(heavy)
        advance(light)
        grads_down_up(level)
        heavy.append(reduce_steps(level, bulk, True))
        advance(heavy[-1:])
        arriving = []
        for ch in range(CHUNKS):
            rows = spans[ch]
            finish(travelling[ch])
            middle = g_out[rows] + norm_back(
                level, ch, 5, xg2.at[level], inv2.at[level], hrecv2.at[level], bst2.at[level]
            )
            g_out[rows] = middle
            keep(level, 4, middle * abr[level, rows])
            scaled = middle * param(level, 4)
            keep(level, 3, scaled)
            dob[rows] = scaled.astype(BF)
            copies = []
            for step in far_first(ncol) + [ncol]:
                i, device = net.peer("col", step)
                piece = mm_nt(dob[rows], wo[level, i].reshape(width, width)).astype(BF)
                if step < ncol:
                    osend[i, rows] = piece
                    copies.append(net.start(osend.at[i, rows], orecv.at[level, c, rows], device))
                else:
                    orecv[level, c, rows] = piece
            arriving.append(copies)
        advance(heavy)
        advance(light)
        grads_out(level, dob)
        for ch in range(CHUNKS):
            finish(arriving[ch])
            dob[spans[ch]] = slots(orecv.at[level], spans[ch]).astype(BF)
        early, late = [], [[] for _ in range(CHUNKS)]
        for p in range(pairs):
            attend_back(level, p)
            if p + 1 < pairs:
                early += net.deal("row", lambda i: kvsend.at[p, i], kvrecv.at[level, p, r])
            else:
                for ch in range(CHUNKS):
                    late[ch] = net.deal(
                        "row", lambda i: kvsend.at[p, i, :, spans[ch]], kvrecv.at[level, p, r, :, spans[ch]]
                    )
        if level + 1 == layers:
            descending = [down_send(level, spans[ch]) for ch in range(CHUNKS)]
        advance(heavy)
        advance(light)
        finish(early)
        travelling = []
        def take_kv(ch):
            rows = spans[ch]
            finish(late[ch])
            for p in range(pairs):
                for j in range(2):
                    total = sum(kvrecv[level, p, i, j, rows].astype(F32) for i in range(nrow))
                    start = (j + 1) * width + p * LANES
                    jg[rows, start : start + LANES] = total.astype(BF)

        def send_dh(ch):
            rows = spans[ch]

            def dh_part(i):
                return sum(
                    mm_nt(jg[rows, j * width : (j + 1) * width], wq[level, i, :, j].reshape(width, width))
                    for j in range(3)
                )

            return norm_back_send(level, ch, dh_part, 0, xg.at[level], hrecv1.at[level], bst1.at[level])

        def reduce_qkv():
            advance(light)
            grads_qkv(level)
            light.append(reduce_steps(level, tail, False))
            advance(light[-1:])

        for ch in range(CHUNKS):
            take_kv(ch)
            if not last:
                travelling.append(send_dh(ch))
        reduce_qkv()
        if last:
            travelling = [send_dh(ch) for ch in range(CHUNKS)]
            advance(light)
        keep(level, 9, jg[:, 0:width].astype(F32))
        keep(level, 2, jg[:, 2 * width :].astype(F32))
        if last:
            advance(heavy)
        if level + 1 == layers:
            for ch in range(CHUNKS):
                finish(descending[ch])
                down_take(level, spans[ch])
                keep(level, 8, cot[spans[ch]] * mbr[level, spans[ch]])
        arriving = []
        for ch in range(CHUNKS):
            finish(travelling[ch])
            upstream = g_out[spans[ch]] + norm_back(
                level, ch, 0, xg.at[level], inv1.at[level], hrecv1.at[level], bst1.at[level]
            )
            arriving.append(branch_back(level - 1, ch, upstream))

    sharing = net.start(sums, sumc, net.sibling)
    advance(light)
    advance(heavy)
    sharing.wait()
    sumy[r] = sums[...] + sumc[...]
    copies = net.spread("row", sumy.at[r], sumy.at[r])
    advance(light)
    advance(heavy)
    finish(copies)
    sumz[z] = sumy[0] + sumy[1] + sumy[2] + sumy[3]
    copies = net.spread("z", sumz.at[z], sumz.at[z])
    advance(light)
    advance(heavy)
    finish(copies)
    total = sumz[0] + sumz[1] + sumz[2] + sumz[3]
    for level in range(layers):
        start = level * per
        for i in range(9):
            small_out[i, level : level + 1, :] = total[start + i : start + i + 1]
        qbias_out[level : level + 1, :] = total[start + 9 : start + 10]
        for j in range(blocks):
            ubias_out[level : level + 1, j * width : (j + 1) * width] = total[start + 10 + j : start + 11 + j]
    for steps in light + heavy:
        for _ in steps:
            pass


def shards(sizes, inputs, w_qkv, w_out, w_up, w_down, small_params, query_bias, up_bias, cotangent):
    tokens, width = inputs.shape
    layers, _, hidden = w_up.shape
    ncol, nrow, nz = sizes["col"], sizes["row"], sizes["z"]
    full, half = width * ncol, width // 2
    blocks = hidden // width
    rows = -(-layers * (10 + blocks) // 8) * 8
    bulk, tail = 2 * hidden // (2 * nz), 4 * width // (2 * nz)
    vmem = lambda shape, dtype=BF: pltpu.VMEM(shape, dtype)
    scratch = [
        vmem((layers, nrow, 2, 3, half, width)),
        vmem((layers, nrow, 2, half, width)),
        vmem((layers, nrow, 2, nz, half // nz, hidden)),
        vmem((layers, nrow, 2, nz, hidden // (2 * nz), width)),
        vmem((ncol, 9, 8, width), F32),
        vmem((layers, ncol, tokens, width)),
        vmem((layers, CHUNKS, ncol, 8, tokens // CHUNKS), F32),
        vmem((layers, tokens, full)),
        vmem((layers, tokens, width)),
        vmem((layers, nrow, width // LANES, 2, tokens, LANES)),
        vmem((layers, width // HD, tokens, tokens * nrow)),
        vmem((layers, ncol, width // LANES, tokens, LANES)),
        vmem((layers, tokens, width), F32),
        vmem((layers, ncol, tokens, width)),
        vmem((layers, CHUNKS, ncol, 8, tokens // CHUNKS), F32),
        vmem((layers, tokens, full)),
        vmem((layers, tokens, hidden)),
        vmem((layers, tokens, hidden)),
        vmem((layers, tokens, width), F32),
        vmem((layers, tokens, LANES), F32),
        vmem((layers, tokens, LANES), F32),
        vmem((ncol, tokens, width)),
        vmem((layers, ncol, tokens, width)),
        vmem((layers, ncol, tokens, width)),
        vmem((tokens, hidden)),
        vmem((ncol, tokens, width)),
        vmem((layers, ncol, tokens, width)),
        vmem((layers, CHUNKS, ncol, 8, tokens // CHUNKS), F32),
        vmem((ncol, tokens, width)),
        vmem((layers, ncol, tokens, width)),
        vmem((tokens, width)),
        vmem((width // LANES, nrow, 2, tokens, LANES)),
        vmem((layers, width // LANES, nrow, 2, tokens, LANES)),
        vmem((tokens, 3 * width)),
        vmem((layers, ncol, tokens, width)),
        vmem((layers, CHUNKS, ncol, 8, tokens // CHUNKS), F32),
        vmem((rows, width), F32),
        vmem((rows, width), F32),
        vmem((nrow, rows, width), F32),
        vmem((nz, rows, width), F32),
    ]
    for piece, upper in ((bulk, bulk // 4), (tail, tail // 2)):
        lower = piece - upper
        scratch += [
            vmem((2, nrow, nz, piece, width)),
            vmem((nrow, nz, piece, width)),
            vmem((nrow, nz, upper, width)),
            vmem((nz, nrow, lower, width)),
            vmem((nz, upper, width)),
            vmem((nrow, lower, width)),
            vmem((layers, nz, upper, width)),
            vmem((layers, nrow, lower, width)),
            vmem((layers, piece, width)),
            vmem((layers, hidden // (2 * nz), width)),
            vmem((2, nz, piece, width)),
        ]
    scratch += [
        pltpu.SemaphoreType.DMA((384,)),
        pltpu.SemaphoreType.DMA((384,)),
        pltpu.SemaphoreType.DMA((16,)),
    ]
    here = pl.BlockSpec(memory_space=pltpu.VMEM)
    far = pl.BlockSpec(memory_space=pl.ANY)
    output, input_grad, qkv, out, up, down, small, query, hidden_bias = pl.pallas_call(
        partial(body, sizes, layers),
        out_shape=(
            jax.ShapeDtypeStruct((tokens, width), F32),
            jax.ShapeDtypeStruct((tokens, width), F32),
            jax.ShapeDtypeStruct((layers, 3, width, width), BF),
            jax.ShapeDtypeStruct((layers, width, width), BF),
            jax.ShapeDtypeStruct((layers, width, hidden), BF),
            jax.ShapeDtypeStruct((layers, hidden, width), BF),
            jax.ShapeDtypeStruct((9, layers, width), F32),
            jax.ShapeDtypeStruct((layers, width), F32),
            jax.ShapeDtypeStruct((layers, hidden), F32),
        ),
        in_specs=[here] * 5 + [far] * 4,
        out_specs=(here,) * 9,
        scratch_shapes=scratch,
        compiler_params=pltpu.CompilerParams(
            collective_id=0, has_side_effects=True, vmem_limit_bytes=63 << 20
        ),
        name="encoder",
    )(
        inputs,
        cotangent,
        jnp.swapaxes(small_params, 0, 1),
        query_bias,
        up_bias,
        jnp.swapaxes(w_qkv, 1, 2).reshape(layers, 3, 2, half, width),
        w_out.reshape(layers, 2, half, width),
        w_up.reshape(layers, 2, nz, half // nz, hidden),
        w_down.reshape(layers, 2, nz, hidden // (2 * nz), width),
    )
    return (
        output,
        input_grad,
        jnp.swapaxes(qkv, 1, 2).astype(F32),
        out.astype(F32),
        up.astype(F32),
        down.astype(F32),
        jnp.swapaxes(small, 0, 1),
        query,
        hidden_bias,
    )


def solution(mesh):
    sizes = {"col": mesh.shape["col"], "row": mesh.shape["row"], "z": mesh.shape["dp"] // 2}
    placed = (
        P(("dp", "row"), "col"),
        P(None, "row", None, "col"),
        P(None, "row", "col"),
        P(None, "row", "col"),
        P(None, "row", "col"),
        P(None, None, "col"),
        P(None, "col"),
        P(None, "col"),
        P(("dp", "row"), "col"),
    )
    return jax.shard_map(
        partial(shards, sizes),
        mesh=mesh,
        in_specs=placed,
        out_specs=(
            P(("dp", "row"), "col"),
            P(("dp", "row"), "col"),
            P(None, "row", None, "col"),
            P(None, "row", "col"),
            P(None, "row", "col"),
            P(None, "row", "col"),
            P(None, None, "col"),
            P(None, "col"),
            P(None, "col"),
        ),
        check_vma=False,
    )
```

```python
from functools import partial

import jax
import jax.numpy as jnp
from jax import lax
from jax.experimental import pallas as pl
from jax.experimental.pallas import tpu as pltpu
from jax.sharding import PartitionSpec as P

HD = 64
EPS = 1e-06
LANES = 128
CHUNKS = 2
UNROLL = 2
BF = jnp.bfloat16
F32 = jnp.float32
MESH = pl.DeviceIdType.MESH


def mm(left, right):
    return jnp.dot(left, right, preferred_element_type=F32)


def mm_nt(left, right):
    return lax.dot_general(left, right, (((1,), (1,)), ((), ())), preferred_element_type=F32)


def mm_tn(left, right):
    return lax.dot_general(left, right, (((0,), (0,)), ((), ())), preferred_element_type=F32)


class Links:
    def __init__(self, sizes, send, recv, local):
        self.sizes = sizes
        self.send, self.recv, self.local = send, recv, local
        self.used = 0
        self.used_local = 0
        self.col = lax.axis_index("col")
        self.row = lax.axis_index("row")
        place = lax.axis_index("dp")
        self.z = place // 2
        self.core = place % 2
        self.sibling = {"dp": self.z * 2 + (1 - self.core)}

    def peer(self, axis, step):
        if axis == "z":
            index = lax.rem(self.z + step, self.sizes["z"])
            return index, {"dp": index * 2 + self.core}
        index = lax.rem(getattr(self, axis) + step, self.sizes[axis])
        return index, {axis: index}

    def start(self, source, target, device, begin=True):
        copy = pltpu.make_async_remote_copy(
            src_ref=source,
            dst_ref=target,
            send_sem=self.send.at[self.used],
            recv_sem=self.recv.at[self.used],
            device_id=device,
            device_id_type=MESH,
        )
        self.used += 1
        if begin:
            copy.start()
        return copy

    def bring(self, source, target):
        copy = pltpu.make_async_copy(source, target, self.local.at[self.used_local])
        self.used_local += 1
        copy.start()
        return copy

    def spread(self, axis, source, target):
        return [
            self.start(source, target, self.peer(axis, step)[1])
            for step in far_first(self.sizes[axis])
        ]

    def deal(self, axis, source_of, target):
        copies = []
        for step in far_first(self.sizes[axis]):
            index, device = self.peer(axis, step)
            copies.append(self.start(source_of(index), target, device))
        return copies


def far_first(count):
    return sorted(range(1, count), key=lambda step: -min(step, count - step))


def finish(copies):
    for copy in copies:
        copy.wait()


def as_rows(first, second):
    tokens = first.shape[0]
    lane = lax.broadcasted_iota(jnp.int32, (tokens, LANES), 1)
    both = jnp.where(lane == 0, first, jnp.where(lane == 1, second, 0.0))
    return both.T[:8]


def as_columns(rows):
    count, tokens = rows.shape
    return jnp.concatenate([rows, jnp.zeros((LANES - count, tokens), F32)], 0).T


def body(sizes, layers, *refs):
    (
        x_in, cot, small, qbias, ubias, wq_in, wo_in, wu_in, wd_in,
        x_out, g_out, gq, gout, gup, gdown, small_out, qbias_out, ubias_out,
        wq, wo, wu, wd, smg, xg, st1, h, q, kvg, probs, og, abr, xg2, st2, h2, gp, zz, mbr,
        inv1, inv2, msend, mrecv, dmg, dur, hsend, hrecv2, bst2, osend, orecv, dob, kvsend, kvrecv,
        jg, hrecv1, bst1, sums, sumc, sumy, sumz, *chunk_refs, send, recv, local,
    ) = refs
    bulk, tail = chunk_refs[: len(chunk_refs) // 2], chunk_refs[len(chunk_refs) // 2 :]
    net = Links(sizes, send, recv, local)
    c, r, z, core = net.col, net.row, net.z, net.core
    ncol, nrow, nz = sizes["col"], sizes["row"], sizes["z"]
    tokens, width = x_in.shape
    hidden = ubias.shape[1]
    full = width * ncol
    length = tokens * nrow
    blocks = hidden // width
    pairs = width // LANES
    scale = HD ** (-0.5)
    part = tokens // CHUNKS
    spans = [slice(i * part, (i + 1) * part) for i in range(CHUNKS)]
    whole = slice(0, tokens)

    barrier = pltpu.get_barrier_semaphore()
    greeted = [net.peer(a, s)[1] for a in ("col", "row", "z") for s in range(1, sizes[a])]
    greeted.append(net.sibling)
    for device in greeted:
        pl.semaphore_signal(barrier, inc=1, device_id=device, device_id_type=MESH)
    mirror = {"row": c, "col": r}

    @pl.when(r != c)
    def _():
        pl.semaphore_signal(barrier, inc=1, device_id=mirror, device_id_type=MESH)

    pl.semaphore_wait(barrier, len(greeted) + jnp.where(r != c, 1, 0))

    def flip_start(source, target):
        copy = net.start(source, target, mirror, begin=False)
        here = pltpu.make_async_copy(source, target, local.at[net.used_local])
        net.used_local += 1

        @pl.when(r != c)
        def _():
            copy.start()

        @pl.when(r == c)
        def _():
            here.start()

        return copy, here

    def flip_wait(pair):
        copy, here = pair

        @pl.when(r != c)
        def _():
            copy.wait()

        @pl.when(r == c)
        def _():
            here.wait()

    class Weight:
        def __init__(self, level, source, store):
            self.level, self.source, self.store = level, source, store

        def split(self, place):
            if len(place.shape) == 3:
                return [place.at[pl.ds(1, 2)], place.at[pl.ds(0, 1)]]
            return [place]

        def begin(self):
            place = self.store.at[self.level, r, core]
            if len(self.source.shape) == 5:
                source = self.source.at[self.level, :, core]
            else:
                source = self.source.at[self.level, core]
            self.queue = [
                [net.bring(a, b)] + net.spread("row", a, b)
                for a, b in zip(self.split(source), self.split(place))
            ]
            self.shared, self.taken = [], 0

        def share(self):
            finish(self.queue.pop(0))
            place = self.store.at[self.level, :, core]
            if len(place.shape) == 4 and place.shape[1] == 3:
                first, count = (0, 1) if self.shared else (1, 2)
                place = place.at[:, pl.ds(first, count)]
            self.shared.append(net.start(place, place, net.sibling))

        def ready(self):
            self.shared[self.taken].wait()
            self.taken += 1

    class Relayed(Weight):
        def begin(self):
            place = self.store.at[self.level, r, core, z]
            self.own = net.bring(self.source.at[self.level, core], self.store.at[self.level, r, core])
            self.copies = net.spread("row", self.source.at[self.level, core, z], place)
            self.shared, self.taken = [], 0

        def relay(self):
            finish(self.copies)
            copies = [self.own]
            for step in range(1, nrow):
                i, _ = net.peer("row", step)
                place = self.store.at[self.level, i, core, z]
                copies += net.spread("z", place, place)
            self.queue = [copies]

    class Flipped(Weight):
        def flip(self):
            self.turn = flip_start(
                self.source.at[self.level, core, z], self.store.at[self.level, c, core, z]
            )

        def begin(self):
            place = self.store.at[self.level, r, core, z]
            flip_wait(self.turn)
            self.copies = net.spread("row", place, place)
            self.shared, self.taken = [], 0

        def relay(self):
            finish(self.copies)
            place = self.store.at[self.level, :, core, z]
            self.queue = [net.spread("z", place, place)]

    wqs = [Weight(l, wq_in, wq) for l in range(layers)]
    wos = [Weight(l, wo_in, wo) for l in range(layers)]
    wus = [Relayed(l, wu_in, wu) for l in range(layers)]
    wds = [Flipped(l, wd_in, wd) for l in range(layers)]

    def param(level, index):
        return small[index, level : level + 1, :]

    def any_param(level, index, block):
        return smg[block, index, level : level + 1, :]

    def norm_send(ch, value, store, stats):
        mean = jnp.sum(value, 1, keepdims=True) * (1.0 / width)
        centered = value - mean
        place = store.at[c, spans[ch]]
        place[...] = centered.astype(BF)
        stats[ch, c] = as_rows(mean, jnp.sum(centered * centered, 1, keepdims=True))
        copies = net.spread("col", place, place)
        return copies + net.spread("col", stats.at[ch, c], stats.at[ch, c])

    def norm_apply(level, ch, first, store, stats, inverse, result):
        columns = as_columns(stats[ch].reshape(ncol * 8, part))
        means = [columns[:, 8 * i : 8 * i + 1] for i in range(ncol)]
        mean = sum(means) * (1.0 / ncol)
        spread = sum(columns[:, 8 * i + 1 : 8 * i + 2] for i in range(ncol))
        spread = spread + width * sum((m - mean) * (m - mean) for m in means)
        scaled = lax.rsqrt(spread * (1.0 / full) + EPS)
        inverse[spans[ch]] = jnp.broadcast_to(scaled, (part, LANES))
        for i in range(ncol):
            normed = (store[i, spans[ch]].astype(F32) + (means[i] - mean)) * scaled
            store[i, spans[ch]] = normed.astype(BF)
            result[spans[ch], i * width : (i + 1) * width] = (
                normed * any_param(level, first, i) + any_param(level, first + 1, i)
            ).astype(BF)

    def slots(store, rows):
        return sum(store[i, rows].astype(F32) for i in range(store.shape[0]))

    def one_head(value, side):
        spot = lax.broadcasted_iota(jnp.int32, value.shape, 1)
        return jnp.where((spot < HD) == (side == 0), value.astype(F32), 0.0).astype(BF)

    def pick(values):
        side = lax.broadcasted_iota(jnp.int32, values[0].shape, 1)
        return jnp.where(side < HD, values[0], values[1])

    def attend(level, p, rows):
        lanes = slice(p * LANES, (p + 1) * LANES)
        queries = q[level, rows, lanes]
        keys = kvg[level, :, p, 0].reshape(length, LANES)
        values = kvg[level, :, p, 1].reshape(length, LANES)
        found = []
        for side in range(2):
            scores = mm_nt(one_head(queries, side), keys) * scale
            raised = jnp.exp(scores - jnp.max(scores, 1, keepdims=True))
            share = (raised * (1.0 / jnp.sum(raised, 1, keepdims=True))).astype(BF)
            probs[level, 2 * p + side, rows] = share
            found.append(mm(share, values))
        place = og.at[level, c, p, rows]
        place[...] = pick(found).astype(BF)
        return net.spread("col", place, place)

    def attended(level, i, rows):
        return jnp.concatenate([og[level, i, p, rows] for p in range(pairs)], 1)

    def attend_back(level, p):
        lanes = slice(p * LANES, (p + 1) * LANES)
        queries = q[level, :, lanes]
        upstream = dob[:, lanes]
        keys = kvg[level, :, p, 0].reshape(length, LANES)
        values = kvg[level, :, p, 1].reshape(length, LANES)
        dq, dk, dv = [], [], []
        for side in range(2):
            share = probs[level, 2 * p + side]
            wide = share.astype(F32)
            pulled = mm_nt(one_head(upstream, side), values)
            inner = jnp.sum(wide * pulled, 1, keepdims=True)
            slope = (wide * (pulled - inner)).astype(BF)
            dq.append(mm(slope, keys))
            dk.append(mm_tn(slope, queries))
            dv.append(mm_tn(share, upstream))
        jg[:, lanes] = (pick(dq) * scale).astype(BF)
        kvsend[p, :, 0] = (pick(dk) * scale).astype(BF).reshape(nrow, tokens, LANES)
        kvsend[p, :, 1] = pick(dv).astype(BF).reshape(nrow, tokens, LANES)
        for j in range(2):
            kvrecv[level, p, r, j] = kvsend[p, r, j]

    def down_send(level, rows):
        copies = []
        for step in far_first(ncol) + [ncol]:
            i, device = net.peer("col", step)
            piece = mm(zz[level, rows], wd[level, i].reshape(hidden, width)).astype(BF)
            if step < ncol:
                msend[i, rows] = piece
                copies.append(net.start(msend.at[i, rows], mrecv.at[level, c, rows], device))
            else:
                mrecv[level, c, rows] = piece
        return copies

    def down_take(level, rows):
        branch = slots(mrecv.at[level], rows) + param(level, 7)
        mbr[level, rows] = branch
        value = x_out[rows] + param(level, 8) * branch
        x_out[rows] = value
        return value

    sums[...] = jnp.zeros_like(sums)
    per = 9 + 1 + blocks

    def keep(level, index, value):
        sums[level * per + index : level * per + index + 1, :] += jnp.sum(value, 0, keepdims=True)

    def branch_back(level, ch, upstream):
        rows = spans[ch]
        g_out[rows] = upstream
        if level < 0:
            return []
        if level + 1 < layers:
            keep(level, 8, upstream * mbr[level, rows])
        scaled = upstream * param(level, 8)
        keep(level, 7, scaled)
        place = dmg.at[level, c, rows]
        place[...] = scaled.astype(BF)
        return net.spread("col", place, place)

    smg[c, :, 0:layers] = small[...]
    wqs[0].begin()
    ahead = net.spread("col", smg.at[c], smg.at[c])
    arriving = []
    for ch in range(CHUNKS):
        value = x_in[spans[ch]]
        x_out[spans[ch]] = value
        arriving.append(norm_send(ch, value, xg.at[0], st1.at[0]))
    for level in range(layers):
        more = level + 1 < layers
        if level == 0:
            wos[0].begin()
            wus[0].begin()
            wds[0].flip()
            finish(ahead)
        travelling = []
        for ch in range(CHUNKS):
            finish(arriving[ch])
            rows = spans[ch]
            norm_apply(level, ch, 0, xg.at[level], st1.at[level], inv1.at[level], h.at[level])
            if ch == 0:
                if level == 0:
                    wqs[0].share()
                    wds[0].begin()
                wqs[level].ready()
                if level == 0:
                    wqs[0].share()

            def project(j):
                return mm(h[level, rows], wq[level, :, :, j].reshape(full, width))

            keys = project(1).astype(BF)
            values = (project(2) + param(level, 2)).astype(BF)
            for p in range(pairs):
                lanes = slice(p * LANES, (p + 1) * LANES)
                kvg[level, r, p, 0, rows] = keys[:, lanes]
                kvg[level, r, p, 1, rows] = values[:, lanes]
                place = kvg.at[level, r, p, :, rows]
                if p == 0:
                    travelling.append(net.spread("row", place, place))
        for p in range(1, pairs):
            place = kvg.at[level, r, p]
            travelling.append(net.spread("row", place, place))
        wqs[level].ready()
        q[level] = (
            mm(h[level], wq[level, :, :, 0].reshape(full, width)) + qbias[level : level + 1, :]
        ).astype(BF)
        wus[level].relay()
        wds[level].relay()
        if level == 0:
            wos[0].share()
        if not more:
            above = [branch_back(level, ch, cot[spans[ch]]) for ch in range(CHUNKS)]
        for ch in range(CHUNKS):
            finish(travelling[ch])
        early = [attend(level, 0, whole)]
        for p in range(1, pairs):
            finish(travelling[CHUNKS + p - 1])
        late = [[attend(level, p, spans[ch]) for p in range(1, pairs)] for ch in range(CHUNKS)]
        wus[level].share()
        if more:
            wqs[level + 1].begin()
            wos[level + 1].begin()
            wus[level + 1].begin()
            wds[level + 1].flip()
        finish(early[0])
        arriving = []
        for ch in range(CHUNKS):
            rows = spans[ch]
            for copies in late[ch]:
                finish(copies)
            if ch == 0:
                wos[level].ready()
            branch = param(level, 3)
            for i in range(ncol):
                branch = branch + mm(attended(level, i, rows), wo[level, i].reshape(width, width))
            abr[level, rows] = branch
            middle = x_out[rows] + param(level, 4) * branch
            x_out[rows] = middle
            arriving.append(norm_send(ch, middle, xg2.at[level], st2.at[level]))
        wds[level].share()
        if more:
            wds[level + 1].begin()
        travelling = []
        for ch in range(CHUNKS):
            rows = spans[ch]
            finish(arriving[ch])
            norm_apply(level, ch, 5, xg2.at[level], st2.at[level], inv2.at[level], h2.at[level])
            if ch == 0:
                wus[level].ready()

            def widen_step(j, carry):
                lanes = pl.ds(pl.multiple_of(j * width, width), width)
                pre = mm(h2[level, rows], wu[level, :, :, :, :, lanes].reshape(full, width))
                pre = pre + ubias[level : level + 1, lanes]
                below = 0.5 * (1.0 + lax.erf(pre * (0.5**0.5)))
                zz[level, rows, lanes] = (pre * below).astype(BF)
                bell = jnp.exp(-0.5 * pre * pre) * (0.5 / jnp.pi) ** 0.5
                gp[level, rows, lanes] = (below + pre * bell).astype(BF)
                return carry

            lax.fori_loop(0, blocks, widen_step, 0, unroll=UNROLL)
            if ch == 0:
                wds[level].ready()
            if more:
                travelling.append(down_send(level, rows))
        if more:
            wqs[level + 1].share()
            wqs[level + 1].share()
            wos[level + 1].share()
        arriving = []
        for ch in range(CHUNKS):
            rows = spans[ch]
            if more:
                finish(travelling[ch])
                value = down_take(level, rows)
                arriving.append(norm_send(ch, value, xg.at[level + 1], st1.at[level + 1]))

    def norm_back_send(level, ch, part_of, gain, normed, store, stats):
        rows = spans[ch]
        copies, first, second = [], 0.0, 0.0
        for step in far_first(ncol) + [ncol]:
            i, device = net.peer("col", step)
            value = part_of(i)
            scaled = value * any_param(level, gain, i)
            first = first + jnp.sum(scaled, 1, keepdims=True)
            second = second + jnp.sum(scaled * normed[i, rows].astype(F32), 1, keepdims=True)
            if step < ncol:
                hsend[i, rows] = value.astype(BF)
                copies.append(net.start(hsend.at[i, rows], store.at[c, rows], device))
            else:
                store[c, rows] = value.astype(BF)
        stats[ch, c] = as_rows(first, second)
        return copies + net.spread("col", stats.at[ch, c], stats.at[ch, c])

    def norm_back(level, ch, gain, normed, inverse, store, stats):
        rows = spans[ch]
        upstream = slots(store, rows)
        normed = normed[c, rows].astype(F32)
        keep(level, gain, upstream * normed)
        keep(level, gain + 1, upstream)
        columns = as_columns(sum(stats[ch, i] for i in range(ncol)))
        scaled = upstream * param(level, gain)
        shift = columns[:, 0:1] * (1.0 / full) + normed * (columns[:, 1:2] * (1.0 / full))
        return inverse[rows, 0:1] * (scaled - shift)

    pieces = 2 * nz
    part_out, part_up = width // pieces, hidden // pieces

    def put_rows(store, i, start, value):
        rows = value.shape[0] // pieces
        for piece in range(pieces):
            store[piece % 2, i, piece // 2, start : start + rows, :] = value[piece * rows : (piece + 1) * rows]

    def grads_down_up(level):
        def down_step(j, carry):
            lanes = pl.ds(pl.multiple_of(j * width, width), width)
            upstream = jnp.concatenate([dmg[level, i] for i in range(ncol)], 1)
            value = mm_tn(zz[level, :, lanes], upstream).astype(BF)
            start = part_up
            for i in range(ncol):
                for t in range(2):
                    bulk[0][t, i, j, start : start + part_up, :] = value[
                        t * part_up : (t + 1) * part_up, i * width : (i + 1) * width
                    ]
            return carry

        def up_step(i, carry):
            lanes = pl.ds(pl.multiple_of(i * width, width), width)
            up = mm_tn(h2[level, :, lanes], dur[...]).astype(BF)
            up = [up[:, j * width : (j + 1) * width] for j in range(blocks)]
            put_rows(bulk[0], i, 0, jnp.concatenate(up, 0))
            return carry

        lax.fori_loop(0, blocks, down_step, 0)
        lax.fori_loop(0, nrow, up_step, 0)

    def grads_out(level, low):
        def step(i, carry):
            put_rows(tail[0], i, 0, mm_tn(attended(level, i, whole), low[...]).astype(BF))
            return carry

        lax.fori_loop(0, nrow, step, 0)

    def grads_qkv(level):
        def step(i, carry):
            lanes = pl.ds(pl.multiple_of(i * width, width), width)
            value = mm_tn(h[level, :, lanes], jg[...]).astype(BF)
            for j in range(3):
                put_rows(tail[0], i, (j + 1) * part_out, value[:, j * width : (j + 1) * width])
            return carry

        lax.fori_loop(0, nrow, step, 0)

    def reduce_steps(level, store, flipping):
        grad, crecv, ra, rb, ta, tb, ua, ub, fin, flipped, land = store
        rows = grad.shape[3]
        upper = ta.shape[1]
        top, low = pl.ds(0, upper), pl.ds(upper, rows - upper)
        copy = net.start(grad.at[1 - core], crecv, net.sibling)
        yield
        copy.wait()

        def add(i, carry):
            for j in range(nz):
                total = grad[core, i, j].astype(F32) + crecv[i, j].astype(F32)
                grad[core, i, j] = total.astype(BF)
            return carry

        lax.fori_loop(0, nrow, add, 0)
        copies = net.deal("row", lambda i: grad.at[core, i, :, top], ra.at[r])
        copies += net.deal("z", lambda i: grad.at[core, :, i, low], rb.at[z])
        yield
        finish(copies)

        def add_top(j, carry):
            total = grad[core, r, j, 0:upper].astype(F32)
            for step in range(1, nrow):
                total = total + ra[net.peer("row", step)[0], j].astype(F32)
            ta[j] = total.astype(BF)
            return carry

        def add_low(j, carry):
            total = grad[core, j, z, upper:].astype(F32)
            for step in range(1, nz):
                total = total + rb[net.peer("z", step)[0], j].astype(F32)
            tb[j] = total.astype(BF)
            return carry

        lax.fori_loop(0, nz, add_top, 0)
        lax.fori_loop(0, nrow, add_low, 0)
        copies = net.deal("z", lambda i: ta.at[i], ua.at[level, z])
        copies += net.deal("row", lambda i: tb.at[i], ub.at[level, r])
        yield
        finish(copies)
        total = ta[z].astype(F32)
        for step in range(1, nz):
            total = total + ua[level, net.peer("z", step)[0]].astype(F32)
        fin[level, 0:upper] = total.astype(BF)
        total = tb[r].astype(F32)
        for step in range(1, nrow):
            total = total + ub[level, net.peer("row", step)[0]].astype(F32)
        fin[level, upper:] = total.astype(BF)
        straight = rows - (part_up if flipping else 0)
        if flipping:
            turn = flip_start(fin.at[level, pl.ds(straight, part_up)], flipped.at[level])
            yield
            flip_wait(turn)
            land[core, z, straight:] = flipped[level]
        land[core, z, 0:straight] = fin[level, 0:straight]
        copies = net.spread("z", land.at[core, z], land.at[core, z])
        yield
        finish(copies)
        copy = net.start(land.at[core], land.at[core], net.sibling)
        yield
        copy.wait()
        for piece in range(pieces):
            found = land[piece % 2, piece // 2]
            some = slice(piece * part_out, (piece + 1) * part_out)
            if flipping:
                block, inner = divmod(piece * part_up, width)
                gup[level, inner : inner + part_up, block * width : (block + 1) * width] = found[0:part_up]
                gdown[level, piece * part_up : (piece + 1) * part_up] = found[part_up:]
            else:
                gout[level, some] = found[0:part_out]
                for j in range(3):
                    gq[level, j, some] = found[(j + 1) * part_out : (j + 2) * part_out]
        yield

    heavy, light = [], []

    def advance(queue):
        for steps in queue:
            next(steps, None)

    arriving = above
    for level in reversed(range(layers)):
        last = level == 0
        advance(heavy)
        advance(light)
        travelling = []
        for ch in range(CHUNKS):
            rows = spans[ch]
            finish(arriving[ch])

            def dz_step(j, carry):
                lanes = pl.ds(pl.multiple_of(j * width, width), width)
                per_half = blocks // 2
                group = width // part_up
                value = 0.0
                for i in range(ncol):
                    weight = wd[level, i, j // per_half, pl.ds((j % per_half) * group, group)]
                    value = value + mm_nt(dmg[level, i, rows], weight.reshape(width, width))
                value = value * gp[level, rows, lanes].astype(F32)
                dur[rows, lanes] = value.astype(BF)
                return carry

            lax.fori_loop(0, blocks, dz_step, 0, unroll=UNROLL)
            travelling.append(
                norm_back_send(
                    level, ch, lambda i: mm_nt(dur[rows], wu[level, i].reshape(width, hidden)),
                    5, xg2.at[level], hrecv2.at[level], bst2.at[level],
                )
            )
        for j in range(blocks):
            keep(level, 10 + j, dur[:, j * width : (j + 1) * width].astype(F32))
        advance(heavy)
        advance(light)
        grads_down_up(level)
        heavy.append(reduce_steps(level, bulk, True))
        advance(heavy[-1:])
        arriving = []
        for ch in range(CHUNKS):
            rows = spans[ch]
            finish(travelling[ch])
            middle = g_out[rows] + norm_back(
                level, ch, 5, xg2.at[level], inv2.at[level], hrecv2.at[level], bst2.at[level]
            )
            g_out[rows] = middle
            keep(level, 4, middle * abr[level, rows])
            scaled = middle * param(level, 4)
            keep(level, 3, scaled)
            dob[rows] = scaled.astype(BF)
            copies = []
            for step in far_first(ncol) + [ncol]:
                i, device = net.peer("col", step)
                piece = mm_nt(dob[rows], wo[level, i].reshape(width, width)).astype(BF)
                if step < ncol:
                    osend[i, rows] = piece
                    copies.append(net.start(osend.at[i, rows], orecv.at[level, c, rows], device))
                else:
                    orecv[level, c, rows] = piece
            arriving.append(copies)
        advance(heavy)
        advance(light)
        grads_out(level, dob)
        for ch in range(CHUNKS):
            finish(arriving[ch])
            dob[spans[ch]] = slots(orecv.at[level], spans[ch]).astype(BF)
        early, late = [], [[] for _ in range(CHUNKS)]
        for p in range(pairs):
            attend_back(level, p)
            if p + 1 < pairs:
                early += net.deal("row", lambda i: kvsend.at[p, i], kvrecv.at[level, p, r])
            else:
                for ch in range(CHUNKS):
                    late[ch] = net.deal(
                        "row", lambda i: kvsend.at[p, i, :, spans[ch]], kvrecv.at[level, p, r, :, spans[ch]]
                    )
        if level + 1 == layers:
            descending = [down_send(level, spans[ch]) for ch in range(CHUNKS)]
        advance(heavy)
        advance(light)
        finish(early)
        travelling = []
        def take_kv(ch):
            rows = spans[ch]
            finish(late[ch])
            for p in range(pairs):
                for j in range(2):
                    total = sum(kvrecv[level, p, i, j, rows].astype(F32) for i in range(nrow))
                    start = (j + 1) * width + p * LANES
                    jg[rows, start : start + LANES] = total.astype(BF)

        def send_dh(ch):
            rows = spans[ch]

            def dh_part(i):
                return sum(
                    mm_nt(jg[rows, j * width : (j + 1) * width], wq[level, i, :, j].reshape(width, width))
                    for j in range(3)
                )

            return norm_back_send(level, ch, dh_part, 0, xg.at[level], hrecv1.at[level], bst1.at[level])

        def reduce_qkv():
            advance(light)
            grads_qkv(level)
            light.append(reduce_steps(level, tail, False))
            advance(light[-1:])

        for ch in range(CHUNKS):
            take_kv(ch)
            if not last:
                travelling.append(send_dh(ch))
        reduce_qkv()
        if last:
            travelling = [send_dh(ch) for ch in range(CHUNKS)]
            advance(light)
        keep(level, 9, jg[:, 0:width].astype(F32))
        keep(level, 2, jg[:, 2 * width :].astype(F32))
        if last:
            advance(heavy)
        if level + 1 == layers:
            for ch in range(CHUNKS):
                finish(descending[ch])
                down_take(level, spans[ch])
                keep(level, 8, cot[spans[ch]] * mbr[level, spans[ch]])
        arriving = []
        for ch in range(CHUNKS):
            finish(travelling[ch])
            upstream = g_out[spans[ch]] + norm_back(
                level, ch, 0, xg.at[level], inv1.at[level], hrecv1.at[level], bst1.at[level]
            )
            arriving.append(branch_back(level - 1, ch, upstream))

    sharing = net.start(sums, sumc, net.sibling)
    advance(light)
    advance(heavy)
    sharing.wait()
    sumy[r] = sums[...] + sumc[...]
    copies = net.spread("row", sumy.at[r], sumy.at[r])
    advance(light)
    advance(heavy)
    finish(copies)
    sumz[z] = sumy[0] + sumy[1] + sumy[2] + sumy[3]
    copies = net.spread("z", sumz.at[z], sumz.at[z])
    advance(light)
    advance(heavy)
    finish(copies)
    total = sumz[0] + sumz[1] + sumz[2] + sumz[3]
    for level in range(layers):
        start = level * per
        for i in range(9):
            small_out[i, level : level + 1, :] = total[start + i : start + i + 1]
        qbias_out[level : level + 1, :] = total[start + 9 : start + 10]
        for j in range(blocks):
            ubias_out[level : level + 1, j * width : (j + 1) * width] = total[start + 10 + j : start + 11 + j]
    for steps in light + heavy:
        for _ in steps:
            pass


def shards(sizes, inputs, w_qkv, w_out, w_up, w_down, small_params, query_bias, up_bias, cotangent):
    tokens, width = inputs.shape
    layers, _, hidden = w_up.shape
    ncol, nrow, nz = sizes["col"], sizes["row"], sizes["z"]
    full, half = width * ncol, width // 2
    blocks = hidden // width
    rows = -(-layers * (10 + blocks) // 8) * 8
    bulk, tail = 2 * hidden // (2 * nz), 4 * width // (2 * nz)
    vmem = lambda shape, dtype=BF: pltpu.VMEM(shape, dtype)
    scratch = [
        vmem((layers, nrow, 2, 3, half, width)),
        vmem((layers, nrow, 2, half, width)),
        vmem((layers, nrow, 2, nz, half // nz, hidden)),
        vmem((layers, nrow, 2, nz, hidden // (2 * nz), width)),
        vmem((ncol, 9, 8, width), F32),
        vmem((layers, ncol, tokens, width)),
        vmem((layers, CHUNKS, ncol, 8, tokens // CHUNKS), F32),
        vmem((layers, tokens, full)),
        vmem((layers, tokens, width)),
        vmem((layers, nrow, width // LANES, 2, tokens, LANES)),
        vmem((layers, width // HD, tokens, tokens * nrow)),
        vmem((layers, ncol, width // LANES, tokens, LANES)),
        vmem((layers, tokens, width), F32),
        vmem((layers, ncol, tokens, width)),
        vmem((layers, CHUNKS, ncol, 8, tokens // CHUNKS), F32),
        vmem((layers, tokens, full)),
        vmem((layers, tokens, hidden)),
        vmem((layers, tokens, hidden)),
        vmem((layers, tokens, width), F32),
        vmem((layers, tokens, LANES), F32),
        vmem((layers, tokens, LANES), F32),
        vmem((ncol, tokens, width)),
        vmem((layers, ncol, tokens, width)),
        vmem((layers, ncol, tokens, width)),
        vmem((tokens, hidden)),
        vmem((ncol, tokens, width)),
        vmem((layers, ncol, tokens, width)),
        vmem((layers, CHUNKS, ncol, 8, tokens // CHUNKS), F32),
        vmem((ncol, tokens, width)),
        vmem((layers, ncol, tokens, width)),
        vmem((tokens, width)),
        vmem((width // LANES, nrow, 2, tokens, LANES)),
        vmem((layers, width // LANES, nrow, 2, tokens, LANES)),
        vmem((tokens, 3 * width)),
        vmem((layers, ncol, tokens, width)),
        vmem((layers, CHUNKS, ncol, 8, tokens // CHUNKS), F32),
        vmem((rows, width), F32),
        vmem((rows, width), F32),
        vmem((nrow, rows, width), F32),
        vmem((nz, rows, width), F32),
    ]
    for piece, upper in ((bulk, bulk // 8), (tail, tail // 2)):
        lower = piece - upper
        scratch += [
            vmem((2, nrow, nz, piece, width)),
            vmem((nrow, nz, piece, width)),
            vmem((nrow, nz, upper, width)),
            vmem((nz, nrow, lower, width)),
            vmem((nz, upper, width)),
            vmem((nrow, lower, width)),
            vmem((layers, nz, upper, width)),
            vmem((layers, nrow, lower, width)),
            vmem((layers, piece, width)),
            vmem((layers, hidden // (2 * nz), width)),
            vmem((2, nz, piece, width)),
        ]
    scratch += [
        pltpu.SemaphoreType.DMA((384,)),
        pltpu.SemaphoreType.DMA((384,)),
        pltpu.SemaphoreType.DMA((16,)),
    ]
    here = pl.BlockSpec(memory_space=pltpu.VMEM)
    far = pl.BlockSpec(memory_space=pl.ANY)
    output, input_grad, qkv, out, up, down, small, query, hidden_bias = pl.pallas_call(
        partial(body, sizes, layers),
        out_shape=(
            jax.ShapeDtypeStruct((tokens, width), F32),
            jax.ShapeDtypeStruct((tokens, width), F32),
            jax.ShapeDtypeStruct((layers, 3, width, width), BF),
            jax.ShapeDtypeStruct((layers, width, width), BF),
            jax.ShapeDtypeStruct((layers, width, hidden), BF),
            jax.ShapeDtypeStruct((layers, hidden, width), BF),
            jax.ShapeDtypeStruct((9, layers, width), F32),
            jax.ShapeDtypeStruct((layers, width), F32),
            jax.ShapeDtypeStruct((layers, hidden), F32),
        ),
        in_specs=[here] * 5 + [far] * 4,
        out_specs=(here,) * 9,
        scratch_shapes=scratch,
        compiler_params=pltpu.CompilerParams(
            collective_id=0, has_side_effects=True, vmem_limit_bytes=63 << 20
        ),
        name="encoder",
    )(
        inputs,
        cotangent,
        jnp.swapaxes(small_params, 0, 1),
        query_bias,
        up_bias,
        jnp.swapaxes(w_qkv, 1, 2).reshape(layers, 3, 2, half, width),
        w_out.reshape(layers, 2, half, width),
        w_up.reshape(layers, 2, nz, half // nz, hidden),
        w_down.reshape(layers, 2, nz, hidden // (2 * nz), width),
    )
    return (
        output,
        input_grad,
        jnp.swapaxes(qkv, 1, 2).astype(F32),
        out.astype(F32),
        up.astype(F32),
        down.astype(F32),
        jnp.swapaxes(small, 0, 1),
        query,
        hidden_bias,
    )


def solution(mesh):
    sizes = {"col": mesh.shape["col"], "row": mesh.shape["row"], "z": mesh.shape["dp"] // 2}
    placed = (
        P(("dp", "row"), "col"),
        P(None, "row", None, "col"),
        P(None, "row", "col"),
        P(None, "row", "col"),
        P(None, "row", "col"),
        P(None, None, "col"),
        P(None, "col"),
        P(None, "col"),
        P(("dp", "row"), "col"),
    )
    return jax.shard_map(
        partial(shards, sizes),
        mesh=mesh,
        in_specs=placed,
        out_specs=(
            P(("dp", "row"), "col"),
            P(("dp", "row"), "col"),
            P(None, "row", None, "col"),
            P(None, "row", "col"),
            P(None, "row", "col"),
            P(None, "row", "col"),
            P(None, None, "col"),
            P(None, "col"),
            P(None, "col"),
        ),
        check_vma=False,
    )
```
